1024 devices in a mesh: dp: 16 (over y, x), seq: 64 (over z, core).
Axes of the slice: x: 4, y: 4, z: 32, core: 2. Of those that a mesh axis runs over, the one named last changes fastest.
Arguments:
- queries: bfloat16 [16, 8192, 1024], P('dp', 'seq'), may hold values from -68 to 68
- keys: bfloat16 [16, 8192, 1024], P('dp', 'seq'), may hold values from -4 to 4
- values: bfloat16 [16, 8192, 1024], P('dp', 'seq'), may hold values from -6 to 6
- cotangent: bfloat16 [16, 8192, 1024], P('dp', 'seq'), may hold values from -6 to 6
- w_out: bfloat16 [1024, 1024], replicated, may hold values from -3 to 3
- blocks: int32 [16, 64, 4], P('dp'), may hold values from 0 to 63, as said below
- counts: int32 [16, 64], P('dp'), may hold values from 1 to 4, as said below
Outputs:
- layer_out: bfloat16 [16, 8192, 1024], P('dp', 'seq')
- value_grad: bfloat16 [16, 8192, 1024], P('dp', 'seq')
- weight_grad: float32 [1024, 1024], P('seq')
The draws below stay inside these ranges and needn't reach their ends.
Inputs may be any that keep to these rules, and one draw needn't show every extreme that they name: blocks[g, c, 0] is c; the entries of one row are distinct clusters; only the first counts[g, c] entries are used. `counts`: every batch has at least one cluster with 4 blocks.
All inputs are finite; a program needn't handle non-finite values.
Results may differ from the reference program's by a relative error of at most 0.019.
Values may be sent and summed in bfloat16 or wider, within the bound.
No kernel may reach another device: no remote copies, remote signals or barrier semaphores. Data moves between devices by JAX's collectives and lax.ppermute only.
A program may use at most 64 MiB of HBM per device.

```python
import jax
import jax.numpy as jnp
from jax import lax

H = 16
HD = 64
D = 1024
CSIZE = 128
MAXB = 4
CLUSTERS = 64
NODES = 8192
N_DP = 16
N_SEQ = 64


def draw_queries(key, part):
    shape = (N_DP, NODES, H * HD)
    key = jax.random.fold_in(key, 1)
    return jnp.clip(jax.random.normal(key, shape, jnp.float32), -4.0, 4.0).astype(jnp.bfloat16)


def draw_keys(key, part):
    shape = (N_DP, NODES, H * HD)
    key = jax.random.fold_in(key, 2)
    return jnp.clip(jax.random.normal(key, shape, jnp.float32), -4.0, 4.0).astype(jnp.bfloat16)


def draw_counts(key, part):
    key = jax.random.fold_in(key, 5)
    drawn = jax.random.randint(key, (N_DP, CLUSTERS), 1, MAXB + 1)
    chosen = jax.random.randint(jax.random.fold_in(key, 6), (N_DP, 1), 0, CLUSTERS)
    return jnp.where(jnp.arange(CLUSTERS)[None, :] == chosen, MAXB, drawn).astype(jnp.int32)


def draw_blocks(key, part):
    key = jax.random.fold_in(key, 7)

    def one_row(index):
        order = jax.random.permutation(jax.random.fold_in(key, index), CLUSTERS - 1)[:MAXB - 1]
        own = index % CLUSTERS
        return jnp.concatenate([own[None], (own + 1 + order) % CLUSTERS]).astype(jnp.int32)
    table = jax.vmap(one_row)(jnp.arange(N_DP * CLUSTERS, dtype=jnp.int32))
    return table.reshape(N_DP, CLUSTERS, MAXB)


def block_levels(key, shape, cuts, least, top_value):
    def one(axis_at, blocks):
        steps = jax.random.uniform(jax.random.fold_in(jax.random.fold_in(key, 6), axis_at), (blocks,), jnp.float32, least / len(cuts), top_value / len(cuts))
        return jnp.repeat(jnp.exp(steps), shape[axis_at] // blocks).reshape((-1,) + (1,) * (len(shape) - axis_at - 1))

    loudness = one(*cuts[0])
    for cut in cuts[1:]:
        loudness = loudness * one(*cut)
    return loudness


def gaussian(own_key, extent, spread, reach, cuts=(), held_as=jnp.bfloat16):
    level = block_levels(own_key, extent, cuts, -0.22, 0.18) if cuts else 1.0
    array = jax.random.normal(own_key, extent, jnp.float32) * spread * level
    return jnp.minimum(jnp.maximum(array, -reach), reach).astype(held_as)


def setup_inputs(seed: int = 0) -> dict:
    key_list = jax.random.split(jax.random.key(seed), 8)
    queries = draw_queries(jax.random.fold_in(key_list[7], 71), 0)
    keys = draw_keys(jax.random.fold_in(key_list[7], 71), 0)
    values = gaussian(key_list[2], (N_DP, NODES, D), 1.0, 6.0, ((0, 16), (1, 64)))
    cotangent = gaussian(key_list[3], (N_DP, NODES, D), 1.0, 6.0, ((0, 16), (1, 64)))
    w_out = gaussian(key_list[4], (D, D), 0.5, 3.0)
    blocks = draw_blocks(jax.random.fold_in(key_list[7], 71), 0)
    counts = draw_counts(jax.random.fold_in(key_list[7], 71), 0)
    return dict(queries=queries, keys=keys, values=values, cotangent=cotangent, w_out=w_out, blocks=blocks, counts=counts)


def reference(queries, keys, values, cotangent, w_out, blocks, counts):
    qsplit = max(N_SEQ // H, 1)
    part_rows = CSIZE // qsplit
    scale = HD ** -0.5

    def one_batch(items):
        q_all, k_all, v_all, grad_in, blk, cnt = items
        out_grad = lax.dot_general(grad_in, w_out, (((1,), (1,)), ((), ())), preferred_element_type=jnp.float32).astype(jnp.bfloat16)
        q_four = q_all.reshape(CLUSTERS, CSIZE, H, HD)
        k_four = k_all.reshape(CLUSTERS, CSIZE, H, HD)
        v_four = v_all.reshape(CLUSTERS, CSIZE, H, HD)
        g_four = out_grad.reshape(CLUSTERS, CSIZE, H, HD)

        def step(carry, index):
            ids = blk[index]
            key_rows = k_four[ids].astype(jnp.float32)
            val_rows = v_four[ids].astype(jnp.float32)
            scores = jnp.einsum('qhd,jkhd->hqjk', q_four[index].astype(jnp.float32), key_rows) * scale
            valid = (jnp.arange(MAXB) < cnt[index])[None, None, :, None]
            scores = jnp.where(valid, scores, -1e30)
            top = jnp.max(scores, axis=(2, 3), keepdims=True)
            expd = jnp.where(valid, jnp.exp(scores - top), 0.0)
            probs = lax.optimization_barrier((expd / jnp.sum(expd, axis=(2, 3), keepdims=True)).astype(jnp.bfloat16)).astype(jnp.float32)
            attended = jnp.einsum('hqjk,jkhd->qhd', probs, val_rows).astype(jnp.bfloat16)
            split_probs = probs.reshape(H, qsplit, part_rows, MAXB, CSIZE)
            split_grad = g_four[index].astype(jnp.float32).reshape(qsplit, part_rows, H, HD)
            contrib = jnp.einsum('hasjk,ashd->ajkhd', split_probs, split_grad)
            return carry.at[:, ids].add(contrib), attended

        start = jnp.zeros((qsplit, CLUSTERS, CSIZE, H, HD), jnp.float32)
        partial_value, attended = lax.scan(step, start, jnp.arange(CLUSTERS))
        node_rows = attended.reshape(NODES, H * HD)
        layer_out = jnp.dot(node_rows, w_out, preferred_element_type=jnp.float32).astype(jnp.bfloat16)
        rounded = lax.optimization_barrier(partial_value.astype(jnp.bfloat16))
        value_grad = jnp.sum(rounded.astype(jnp.float32), axis=0).astype(jnp.bfloat16).reshape(NODES, H * HD)
        weight_part = lax.dot_general(node_rows, grad_in, (((0,), (0,)), ((), ())), preferred_element_type=jnp.float32)
        return layer_out, value_grad, weight_part

    layer_out, value_grad, weight_part = lax.map(one_batch, (queries, keys, values, cotangent, blocks, counts))
    return layer_out, value_grad, jnp.sum(weight_part, axis=0)
```

```python
import jax
import jax.numpy as jnp
from jax import lax
from jax.experimental import pallas as pl
from jax.experimental.pallas import tpu as pltpu
from jax.sharding import PartitionSpec as P

H = 16
HD = 64
CSIZE = 128
HALF = CSIZE // 2
MAXB = 4
SITE = 4
BATCHES = 4
BF = jnp.bfloat16
F32 = jnp.float32


def params(mib=40):
    return pltpu.CompilerParams(vmem_limit_bytes=mib * 1024 * 1024)


def pack_kernel(q_ref, k_ref, v_ref, c_ref, w_ref, out_ref):
    keys = k_ref[...]
    vals = v_ref[...].T
    qrys = q_ref[...].T
    grad = lax.dot_general(
        w_ref[...], c_ref[...], (((1,), (1,)), ((), ())), preferred_element_type=F32
    ).astype(BF)
    for i in range(2):
        part = keys[:, i * HD : (i + 1) * HD]
        out_ref[i, 0:HALF, :] = jnp.concatenate([part[:HALF], part[HALF:]], axis=1)
        out_ref[i, 64:128, :] = vals[i * HD : (i + 1) * HD]
        out_ref[i, 128:192, :] = qrys[i * HD : (i + 1) * HD]
        out_ref[i, 192:256, :] = grad[i * HD : (i + 1) * HD]


def pack(q, k, v, cot, w_out):
    rows, width = q.shape
    pair = pl.BlockSpec((rows, 2 * HD), lambda i: (0, i))
    return pl.pallas_call(
        pack_kernel,
        grid=(H // 2,),
        in_specs=[
            pair,
            pair,
            pair,
            pl.BlockSpec((rows, width), lambda i: (0, 0)),
            pl.BlockSpec((2 * HD, width), lambda i: (i, 0)),
        ],
        out_specs=pl.BlockSpec((2, 256, CSIZE), lambda i: (i, 0, 0)),
        out_shape=jax.ShapeDtypeStruct((H, 256, CSIZE), BF),
        compiler_params=params(60),
        cost_estimate=pl.CostEstimate(
            flops=2 * rows * width * width, bytes_accessed=2 * width * width + 10 * rows * width, transcendentals=0
        ),
        name="pack",
    )(q, k, v, cot, w_out)


def forward_kernel(site_ref, blk_ref, cnt_ref, q_ref, kv_ref, att_ref, prob_ref):
    cluster = SITE * pl.program_id(0) + site_ref[0]
    number = cnt_ref[cluster]
    ids = [blk_ref[MAXB * cluster + j] for j in range(MAXB)]
    q = q_ref[0]
    zero = jnp.zeros_like(q)
    both = jnp.concatenate(
        [jnp.concatenate([q, zero], axis=1), jnp.concatenate([zero, q], axis=1)], axis=0
    )
    scores = []
    for j in range(MAXB):
        keys = kv_ref[ids[j] % SITE, ids[j] // SITE, 0:64, :]
        s = jnp.dot(keys, both, preferred_element_type=F32)
        scores.append(s if j == 0 else jnp.where(j < number, s, -1e30))
    s = jnp.concatenate(scores, axis=0)
    top = jnp.max(s, axis=0, keepdims=True)
    top = jnp.maximum(top[:, :CSIZE], top[:, CSIZE:])
    e = jnp.exp((s - jnp.concatenate([top, top], axis=1)) * (HD**-0.5))
    total = jnp.sum(e, axis=0, keepdims=True)
    total = total[:, :CSIZE] + total[:, CSIZE:]
    inv = 1.0 / total
    p = (e * jnp.concatenate([inv, inv], axis=1)).astype(BF)
    att = jnp.zeros((HD, CSIZE), F32)
    for j in range(MAXB):
        part = p[j * HALF : (j + 1) * HALF]
        pj = jnp.concatenate([part[:, :CSIZE], part[:, CSIZE:]], axis=0)
        prob_ref[0, j] = pj
        vals = kv_ref[ids[j] % SITE, ids[j] // SITE, 64:128, :]
        att += jnp.dot(vals, pj, preferred_element_type=F32)
    att_ref[0] = att.astype(BF)


def forward(site, blk, cnt, recv, kv):
    n = recv.shape[0]
    return pl.pallas_call(
        forward_kernel,
        grid_spec=pltpu.PrefetchScalarGridSpec(
            num_scalar_prefetch=3,
            grid=(n,),
            in_specs=[
                pl.BlockSpec((1, 64, CSIZE), lambda i, *_: (i, 2, 0)),
                pl.BlockSpec(kv.shape, lambda i, *_: (0, 0, 0, 0)),
            ],
            out_specs=[
                pl.BlockSpec((1, HD, CSIZE), lambda i, *_: (i, 0, 0)),
                pl.BlockSpec((1, MAXB, CSIZE, CSIZE), lambda i, *_: (i, 0, 0, 0)),
            ],
        ),
        out_shape=[
            jax.ShapeDtypeStruct((n, HD, CSIZE), BF),
            jax.ShapeDtypeStruct((n, MAXB, CSIZE, CSIZE), BF),
        ],
        compiler_params=params(),
        cost_estimate=pl.CostEstimate(
            flops=n * 4 * MAXB * CSIZE * CSIZE * HD, bytes_accessed=5 << 20, transcendentals=n * MAXB * CSIZE * CSIZE
        ),
        name="attend",
    )(site, blk, cnt, recv, kv)


def backward_kernel(site_ref, blk_ref, cnt_ref, g_ref, prob_ref, out_ref, acc_ref):
    step = pl.program_id(0)

    @pl.when(step == 0)
    def _():
        acc_ref[...] = jnp.zeros_like(acc_ref)

    cluster = SITE * step + site_ref[0]
    number = cnt_ref[cluster]
    g = g_ref[0]
    for j in range(MAXB):

        @pl.when(j < number)
        def _():
            at = blk_ref[MAXB * cluster + j]
            acc_ref[at] += lax.dot_general(
                g, prob_ref[0, j], (((1,), (1,)), ((), ())), preferred_element_type=F32
            )

    @pl.when(step == pl.num_programs(0) - 1)
    def _():
        for s in range(SITE):
            out_ref[s] = acc_ref[:, 16 * s : 16 * (s + 1), :].astype(BF)


def backward(site, blk, cnt, recv, probs):
    n = recv.shape[0]
    clusters = SITE * n
    return pl.pallas_call(
        backward_kernel,
        grid_spec=pltpu.PrefetchScalarGridSpec(
            num_scalar_prefetch=3,
            grid=(n,),
            in_specs=[
                pl.BlockSpec((1, 64, CSIZE), lambda i, *_: (i, 3, 0)),
                pl.BlockSpec((1, MAXB, CSIZE, CSIZE), lambda i, *_: (i, 0, 0, 0)),
            ],
            out_specs=pl.BlockSpec((SITE, clusters, 16, CSIZE), lambda i, *_: (0, 0, 0, 0)),
            scratch_shapes=[pltpu.VMEM((clusters, HD, CSIZE), F32)],
        ),
        out_shape=jax.ShapeDtypeStruct((SITE, clusters, 16, CSIZE), BF),
        compiler_params=params(),
        cost_estimate=pl.CostEstimate(
            flops=n * 2 * MAXB * CSIZE * CSIZE * HD, bytes_accessed=3 << 20, transcendentals=0
        ),
        name="value_contrib",
    )(site, blk, cnt, recv, probs)


def split_kernel(att_ref, out_ref, wide_ref):
    wide_ref[...] = att_ref[...].astype(F32)
    n = out_ref.shape[0]
    for p in range(n):
        out_ref[p] = wide_ref[pl.ds(p, out_ref.shape[1], stride=n), :].astype(BF)


def split_rows(att_t, n):
    rows = att_t.shape[0]
    return pl.pallas_call(
        split_kernel,
        out_shape=jax.ShapeDtypeStruct((n, rows // n, CSIZE), BF),
        scratch_shapes=[pltpu.VMEM((rows, CSIZE), F32)],
        compiler_params=params(),
        cost_estimate=pl.CostEstimate(flops=0, bytes_accessed=4 * rows * CSIZE, transcendentals=0),
        name="split_rows",
    )(att_t)


def weight_kernel(att_ref, cot_ref, out_ref):
    @pl.when(pl.program_id(0) == 0)
    def _():
        out_ref[...] = jnp.zeros_like(out_ref)

    att = jnp.concatenate([att_ref[i] for i in range(BATCHES)], axis=1)
    out_ref[...] += jnp.dot(att, cot_ref[...], preferred_element_type=F32)


def weight_part(att, cots):
    n, rows, nodes = att.shape
    width = cots.shape[1]
    return pl.pallas_call(
        weight_kernel,
        grid=(n // BATCHES,),
        in_specs=[
            pl.BlockSpec((BATCHES, rows, nodes), lambda i: (i, 0, 0)),
            pl.BlockSpec((BATCHES * nodes, width), lambda i: (i, 0)),
        ],
        out_specs=pl.BlockSpec((rows, width), lambda i: (0, 0)),
        out_shape=jax.ShapeDtypeStruct((rows, width), F32),
        compiler_params=params(),
        cost_estimate=pl.CostEstimate(
            flops=2 * n * rows * nodes * width, bytes_accessed=2 * n * nodes * width, transcendentals=0
        ),
        name="weight_part",
    )(att, cots)


def flip_kernel(x_ref, out_ref):
    out_ref[...] = x_ref[...].T


def flip(x):
    rows, cols = x.shape
    return pl.pallas_call(
        flip_kernel,
        out_shape=jax.ShapeDtypeStruct((cols, rows), x.dtype),
        compiler_params=params(),
        cost_estimate=pl.CostEstimate(flops=0, bytes_accessed=4 * rows * cols, transcendentals=0),
        name="flip",
    )(x)


def body(queries, keys, values, cotangent, w_out, blocks, counts):
    nseq = lax.axis_size("seq")
    ndp = lax.axis_size("dp")
    width = w_out.shape[0]
    site = (lax.axis_index("seq") % SITE).astype(jnp.int32)[None]
    same_site = [[SITE * h + s for h in range(H)] for s in range(SITE)]
    same_head = [[SITE * h + s for s in range(SITE)] for h in range(H)]
    blk = blocks[0].reshape(-1)
    cnt = counts[0]
    cot = cotangent[0]

    sent = pack(queries[0], keys[0], values[0], cot, w_out)
    recv = lax.all_to_all(sent, "seq", split_axis=0, concat_axis=0, tiled=True, axis_index_groups=same_site)

    cots = lax.all_gather(cot, "dp", axis=0, tiled=True)

    kv, cots = lax.optimization_barrier((recv[:, :128], cots))
    kv = lax.all_gather(kv, "seq", axis_index_groups=same_head, axis=0, tiled=False)
    att, probs = forward(site, blk, cnt, recv, kv)
    att_home = lax.all_to_all(att, "seq", split_axis=0, concat_axis=0, tiled=True, axis_index_groups=same_site)
    contrib = backward(site, blk, cnt, recv, probs)
    contrib = lax.psum_scatter(contrib, "seq", axis_index_groups=same_head, scatter_dimension=0, tiled=False)

    att_t = att_home.reshape(width, CSIZE)
    pieces = lax.all_to_all(split_rows(att_t, ndp), "dp", split_axis=0, concat_axis=0, tiled=True)
    part = weight_part(pieces, cots)
    layer_out = lax.dot_general(
        att_t, w_out, (((0,), (0,)), ((), ())), preferred_element_type=F32
    ).astype(BF)

    last = jnp.concatenate([contrib, part.astype(BF).reshape(nseq, -1, CSIZE)], axis=1)
    back = lax.all_to_all(last, "seq", split_axis=0, concat_axis=0, tiled=True)
    rows = jnp.sum(back[:, 16:].astype(F32), axis=0)
    every = lax.all_to_all(
        jnp.broadcast_to(rows[None], (ndp,) + rows.shape), "dp", split_axis=0, concat_axis=0, tiled=True
    )
    value_grad = flip(back[:, :16].reshape(width, CSIZE))
    weight_grad = every.reshape(width // nseq, width)
    return (layer_out[None], value_grad[None], weight_grad)


def solution(mesh):
    return jax.shard_map(
        body,
        mesh=mesh,
        in_specs=(
            P("dp", "seq", None),
            P("dp", "seq", None),
            P("dp", "seq", None),
            P("dp", "seq", None),
            P(),
            P("dp", None, None),
            P("dp", None),
        ),
        out_specs=(P("dp", "seq", None), P("dp", "seq", None), P("seq", None)),
        check_vma=False,
    )
```

```python
import jax
import jax.numpy as jnp
from jax import lax
from jax.experimental import pallas as pl
from jax.experimental.pallas import tpu as pltpu
from jax.sharding import PartitionSpec as P

H = 16
HD = 64
CSIZE = 128
HALF = CSIZE // 2
MAXB = 4
SITE = 4
BATCHES = 8
ROWS = 8
PAIR = 8
BF = jnp.bfloat16
F32 = jnp.float32


def params(mib=40):
    return pltpu.CompilerParams(vmem_limit_bytes=mib * 1024 * 1024)


def pack_kernel(q_ref, k_ref, v_ref, c_ref, w_ref, out_ref, ct_ref):
    @pl.when(pl.program_id(0) == 0)
    def _():
        ct_ref[...] = c_ref[...].T

    keys = k_ref[...]
    vals = v_ref[...].T
    qrys = q_ref[...].T
    grad = jnp.dot(w_ref[...], ct_ref[...], preferred_element_type=F32).astype(BF)
    for i in range(PAIR):
        part = keys[:, i * HD : (i + 1) * HD]
        out_ref[i, 0:HALF, :] = jnp.concatenate([part[:HALF], part[HALF:]], axis=1)
        out_ref[i, 64:128, :] = vals[i * HD : (i + 1) * HD]
        out_ref[i, 128:192, :] = qrys[i * HD : (i + 1) * HD]
        out_ref[i, 192:256, :] = grad[i * HD : (i + 1) * HD]


def pack(q, k, v, cot, w_out):
    rows, width = q.shape
    pair = pl.BlockSpec((rows, PAIR * HD), lambda i: (0, i))
    return pl.pallas_call(
        pack_kernel,
        grid=(H // PAIR,),
        in_specs=[
            pair,
            pair,
            pair,
            pl.BlockSpec((rows, width), lambda i: (0, 0)),
            pl.BlockSpec((PAIR * HD, width), lambda i: (i, 0)),
        ],
        out_specs=pl.BlockSpec((PAIR, 256, CSIZE), lambda i: (i, 0, 0)),
        scratch_shapes=[pltpu.VMEM((width, rows), BF)],
        out_shape=jax.ShapeDtypeStruct((H, 256, CSIZE), BF),
        compiler_params=params(60),
        cost_estimate=pl.CostEstimate(
            flops=2 * rows * width * width, bytes_accessed=2 * width * width + 10 * rows * width, transcendentals=0
        ),
        name="pack",
    )(q, k, v, cot, w_out)


def forward_kernel(site_ref, blk_ref, cnt_ref, q_ref, kv0, kv1, kv2, kv3, att_ref, prob_ref, kv_ref, sems):
    @pl.when(pl.program_id(0) == 0)
    def _():
        copies = [
            pltpu.make_async_copy(part, kv_ref.at[t], sems.at[t])
            for t, part in enumerate((kv0, kv1, kv2, kv3))
        ]
        for copy in copies:
            copy.start()
        for copy in copies:
            copy.wait()

    count = q_ref.shape[0]
    ids, slots, scores = [], [], []
    for u in range(count):
        cluster = SITE * (count * pl.program_id(0) + u) + site_ref[0]
        number = cnt_ref[cluster]
        q = q_ref[u]
        zero = jnp.zeros_like(q)
        both = jnp.concatenate(
            [jnp.concatenate([q, zero], axis=1), jnp.concatenate([zero, q], axis=1)], axis=0
        )
        at = [blk_ref[MAXB * cluster + j] for j in range(MAXB)]
        ids.append([i // SITE for i in at])
        slots.append([(i % SITE) ^ site_ref[0] for i in at])
        mine = []
        for j in range(MAXB):
            keys = kv_ref[slots[u][j], ids[u][j], 0:64, :]
            s = jnp.dot(keys, both, preferred_element_type=F32)
            mine.append(s if j == 0 else jnp.where(j < number, s, -1e30))
        scores.append(jnp.concatenate(mine, axis=0))
    for u in range(count):
        s = scores[u]
        top = jnp.max(s, axis=0, keepdims=True)
        top = jnp.maximum(top[:, :CSIZE], top[:, CSIZE:])
        e = jnp.exp((s - jnp.concatenate([top, top], axis=1)) * (HD**-0.5))
        total = jnp.sum(e, axis=0, keepdims=True)
        inv = 1.0 / (total[:, :CSIZE] + total[:, CSIZE:])
        p = (e * jnp.concatenate([inv, inv], axis=1)).astype(BF)
        halves = [p[i * HALF : (i + 1) * HALF, h : h + CSIZE] for i in range(MAXB) for h in (0, CSIZE)]
        for j in range(MAXB):
            prob_ref[u, j] = jnp.concatenate(halves[2 * j : 2 * j + 2], axis=0)
        vals = jnp.concatenate([kv_ref[slots[u][j], ids[u][j], 64:128, :] for j in range(MAXB)], axis=1)
        att = jnp.dot(vals, jnp.concatenate(halves, axis=0), preferred_element_type=F32)
        att_ref[u] = att.astype(BF)


def forward(site, blk, cnt, recv, kvs):
    n = recv.shape[0]
    return pl.pallas_call(
        forward_kernel,
        grid_spec=pltpu.PrefetchScalarGridSpec(
            num_scalar_prefetch=3,
            grid=(n // ROWS,),
            in_specs=[
                pl.BlockSpec((ROWS, 64, CSIZE), lambda i, *_: (i, 2, 0)),
            ]
            + [pl.BlockSpec(memory_space=pl.ANY)] * SITE,
            out_specs=[
                pl.BlockSpec((ROWS, HD, CSIZE), lambda i, *_: (i, 0, 0)),
                pl.BlockSpec((ROWS, MAXB, CSIZE, CSIZE), lambda i, *_: (i, 0, 0, 0)),
            ],
            scratch_shapes=[pltpu.VMEM((SITE,) + kvs[0].shape, BF), pltpu.SemaphoreType.DMA((SITE,))],
        ),
        out_shape=[
            jax.ShapeDtypeStruct((n, HD, CSIZE), BF),
            jax.ShapeDtypeStruct((n, MAXB, CSIZE, CSIZE), BF),
        ],
        compiler_params=params(60),
        cost_estimate=pl.CostEstimate(
            flops=n * 4 * MAXB * CSIZE * CSIZE * HD, bytes_accessed=5 << 20, transcendentals=n * MAXB * CSIZE * CSIZE
        ),
        name="attend",
    )(site, blk, cnt, recv, *kvs)


def backward_kernel(site_ref, blk_ref, cnt_ref, g_ref, prob_ref, keep_ref, swap_ref, acc_ref):
    step = pl.program_id(0)

    @pl.when(step == 0)
    def _():
        acc_ref[...] = jnp.zeros_like(acc_ref)

    cluster = SITE * step + site_ref[0]
    number = cnt_ref[cluster]
    g = g_ref[0]
    for j in range(MAXB):

        @pl.when(j < number)
        def _():
            at = blk_ref[MAXB * cluster + j]
            acc_ref[at] += lax.dot_general(
                g, prob_ref[0, j], (((1,), (1,)), ((), ())), preferred_element_type=F32
            )

    @pl.when(step == pl.num_programs(0) - 1)
    def _():
        for t in range(SITE):
            first = pl.multiple_of(16 * (site_ref[0] ^ t), 16)
            (swap_ref if t % 2 else keep_ref)[t // 2] = acc_ref[:, pl.ds(first, 16), :].astype(BF)


def backward(site, blk, cnt, recv, probs):
    n = recv.shape[0]
    clusters = SITE * n
    return pl.pallas_call(
        backward_kernel,
        grid_spec=pltpu.PrefetchScalarGridSpec(
            num_scalar_prefetch=3,
            grid=(n,),
            in_specs=[
                pl.BlockSpec((1, 64, CSIZE), lambda i, *_: (i, 3, 0)),
                pl.BlockSpec((1, MAXB, CSIZE, CSIZE), lambda i, *_: (i, 0, 0, 0)),
            ],
            out_specs=[pl.BlockSpec((2, clusters, 16, CSIZE), lambda i, *_: (0, 0, 0, 0))] * 2,
            scratch_shapes=[pltpu.VMEM((clusters, HD, CSIZE), F32)],
        ),
        out_shape=[jax.ShapeDtypeStruct((2, clusters, 16, CSIZE), BF)] * 2,
        compiler_params=params(),
        cost_estimate=pl.CostEstimate(
            flops=n * 2 * MAXB * CSIZE * CSIZE * HD, bytes_accessed=3 << 20, transcendentals=0
        ),
        name="value_contrib",
    )(site, blk, cnt, recv, probs)


def split_kernel(att_ref, out_ref, wide_ref):
    wide_ref[...] = att_ref[...].astype(F32)
    n = out_ref.shape[0]
    for p in range(n):
        out_ref[p] = wide_ref[pl.ds(p, out_ref.shape[1], stride=n), :].astype(BF)


def split_rows(att_t, n):
    rows = att_t.shape[0]
    return pl.pallas_call(
        split_kernel,
        out_shape=jax.ShapeDtypeStruct((n, rows // n, CSIZE), BF),
        scratch_shapes=[pltpu.VMEM((rows, CSIZE), F32)],
        compiler_params=params(),
        cost_estimate=pl.CostEstimate(flops=0, bytes_accessed=4 * rows * CSIZE, transcendentals=0),
        name="split_rows",
    )(att_t)


def weight_kernel(att_ref, cot_ref, out_ref):
    @pl.when(pl.program_id(0) == 0)
    def _():
        out_ref[...] = jnp.zeros_like(out_ref)

    att = jnp.concatenate([att_ref[i] for i in range(att_ref.shape[0])], axis=1)
    out_ref[...] += jnp.dot(att, cot_ref[...], preferred_element_type=F32)


def weight_part(att, cots):
    n, rows, nodes = att.shape
    width = cots.shape[1]
    batches = min(BATCHES, n)
    return pl.pallas_call(
        weight_kernel,
        grid=(n // batches,),
        in_specs=[
            pl.BlockSpec((batches, rows, nodes), lambda i: (i, 0, 0)),
            pl.BlockSpec((batches * nodes, width), lambda i: (i, 0)),
        ],
        out_specs=pl.BlockSpec((rows, width), lambda i: (0, 0)),
        out_shape=jax.ShapeDtypeStruct((rows, width), F32),
        compiler_params=params(60),
        cost_estimate=pl.CostEstimate(
            flops=2 * n * rows * nodes * width, bytes_accessed=2 * n * nodes * width, transcendentals=0
        ),
        name="weight_part",
    )(att, cots)


def flip_kernel(x_ref, out_ref):
    out_ref[...] = x_ref[...].T


def flip(x):
    rows, cols = x.shape
    return pl.pallas_call(
        flip_kernel,
        out_shape=jax.ShapeDtypeStruct((cols, rows), x.dtype),
        compiler_params=params(),
        cost_estimate=pl.CostEstimate(flops=0, bytes_accessed=4 * rows * cols, transcendentals=0),
        name="flip",
    )(x)


def body(queries, keys, values, cotangent, w_out, blocks, counts):
    nseq = lax.axis_size("seq")
    ndp = lax.axis_size("dp")
    width = w_out.shape[0]
    site = (lax.axis_index("seq") % SITE).astype(jnp.int32)[None]
    same_site = [[SITE * h + s for h in range(H)] for s in range(SITE)]

    def swap(x, bit):
        return lax.ppermute(x, "seq", [(i, i ^ bit) for i in range(nseq)])

    blk = blocks[0].reshape(-1)
    cnt = counts[0]
    cot = cotangent[0]

    sent = pack(queries[0], keys[0], values[0], cot, w_out)
    recv = lax.all_to_all(sent, "seq", split_axis=0, concat_axis=0, tiled=True, axis_index_groups=same_site)

    cots = lax.all_gather(cot, "dp", axis=0, tiled=True)

    kv, cots = lax.optimization_barrier((recv[:, :128], cots))
    kv_z = swap(kv, 2)
    kvs = [kv, swap(kv, 1), kv_z, swap(kv_z, 1)]
    att, probs = forward(site, blk, cnt, recv, kvs)
    att_home = lax.all_to_all(att, "seq", split_axis=0, concat_axis=0, tiled=True, axis_index_groups=same_site)
    keep, give = backward(site, blk, cnt, recv, probs)
    chip = (keep.astype(F32) + swap(give, 1).astype(F32)).astype(BF)
    contrib = (chip[0].astype(F32) + swap(chip[1], 2).astype(F32)).astype(BF)

    att_t = att_home.reshape(width, CSIZE)
    pieces = lax.all_to_all(split_rows(att_t, ndp), "dp", split_axis=0, concat_axis=0, tiled=True)
    part = weight_part(pieces, cots)
    layer_out = lax.dot_general(
        att_t, w_out, (((0,), (0,)), ((), ())), preferred_element_type=F32
    ).astype(BF)

    last = jnp.concatenate([contrib, part.astype(BF).reshape(nseq, -1, CSIZE)], axis=1)
    back = lax.all_to_all(last, "seq", split_axis=0, concat_axis=0, tiled=True)
    rows = jnp.sum(back[:, 16:].astype(F32), axis=0)
    every = lax.all_to_all(
        jnp.broadcast_to(rows[None], (ndp,) + rows.shape), "dp", split_axis=0, concat_axis=0, tiled=True
    )
    value_grad = flip(back[:, :16].reshape(width, CSIZE))
    weight_grad = every.reshape(width // nseq, width)
    return (layer_out[None], value_grad[None], weight_grad)


def solution(mesh):
    return jax.shard_map(
        body,
        mesh=mesh,
        in_specs=(
            P("dp", "seq", None),
            P("dp", "seq", None),
            P("dp", "seq", None),
            P("dp", "seq", None),
            P(),
            P("dp", None, None),
            P("dp", None),
        ),
        out_specs=(P("dp", "seq", None), P("dp", "seq", None), P("seq", None)),
        check_vma=False,
    )
```

```python
import jax
import jax.numpy as jnp
from jax import lax
from jax.experimental import pallas as pl
from jax.experimental.pallas import tpu as pltpu
from jax.sharding import PartitionSpec as P

H = 16
HD = 64
CSIZE = 128
HALF = CSIZE // 2
MAXB = 4
SITE = 4
BATCHES = 8
ROWS = 8
PAIR = 8
BF = jnp.bfloat16
F32 = jnp.float32


def params(mib=40):
    return pltpu.CompilerParams(vmem_limit_bytes=mib * 1024 * 1024)


def pack_kernel(q_ref, k_ref, v_ref, c_ref, w_ref, out_ref, ct_ref):
    @pl.when(pl.program_id(0) == 0)
    def _():
        ct_ref[...] = c_ref[...].T

    keys = k_ref[...]
    vals = v_ref[...].T
    qrys = q_ref[...].T
    grad = jnp.dot(w_ref[...], ct_ref[...], preferred_element_type=F32).astype(BF)
    for i in range(PAIR):
        part = keys[:, i * HD : (i + 1) * HD]
        out_ref[i, 0:HALF, :] = jnp.concatenate([part[:HALF], part[HALF:]], axis=1)
        out_ref[i, 64:128, :] = vals[i * HD : (i + 1) * HD]
        out_ref[i, 128:192, :] = qrys[i * HD : (i + 1) * HD]
        out_ref[i, 192:256, :] = grad[i * HD : (i + 1) * HD]


def pack(q, k, v, cot, w_out):
    rows, width = q.shape
    pair = pl.BlockSpec((rows, PAIR * HD), lambda i: (0, i))
    return pl.pallas_call(
        pack_kernel,
        grid=(H // PAIR,),
        in_specs=[
            pair,
            pair,
            pair,
            pl.BlockSpec((rows, width), lambda i: (0, 0)),
            pl.BlockSpec((PAIR * HD, width), lambda i: (i, 0)),
        ],
        out_specs=pl.BlockSpec((PAIR, 256, CSIZE), lambda i: (i, 0, 0)),
        scratch_shapes=[pltpu.VMEM((width, rows), BF)],
        out_shape=jax.ShapeDtypeStruct((H, 256, CSIZE), BF),
        compiler_params=params(60),
        cost_estimate=pl.CostEstimate(
            flops=2 * rows * width * width, bytes_accessed=2 * width * width + 10 * rows * width, transcendentals=0
        ),
        name="pack",
    )(q, k, v, cot, w_out)


def forward_kernel(site_ref, blk_ref, cnt_ref, q_ref, kv0, kv1, kv2, kv3, att_ref, prob_ref, kv_ref, wide_ref, sems):
    @pl.when(pl.program_id(0) == 0)
    def _():
        copies = [
            pltpu.make_async_copy(part, kv_ref.at[t], sems.at[t])
            for t, part in enumerate((kv0, kv1, kv2, kv3))
        ]
        for copy in copies:
            copy.start()
        for copy in copies:
            copy.wait()

    count = q_ref.shape[0]
    ids, slots, scores = [], [], []
    for u in range(count):
        cluster = SITE * (count * pl.program_id(0) + u) + site_ref[0]
        number = cnt_ref[cluster]
        q = q_ref[u]
        zero = jnp.zeros_like(q)
        both = jnp.concatenate(
            [jnp.concatenate([q, zero], axis=1), jnp.concatenate([zero, q], axis=1)], axis=0
        )
        at = [blk_ref[MAXB * cluster + j] for j in range(MAXB)]
        ids.append([i // SITE for i in at])
        slots.append([(i % SITE) ^ site_ref[0] for i in at])
        mine = []
        for j in range(MAXB):
            keys = kv_ref[slots[u][j], ids[u][j], 0:64, :]
            s = jnp.dot(keys, both, preferred_element_type=F32)
            mine.append(s if j == 0 else jnp.where(j < number, s, -1e30))
        scores.append(jnp.concatenate(mine, axis=0))
    for u in range(count):
        s = scores[u]
        top = jnp.max(s, axis=0, keepdims=True)
        top = jnp.maximum(top[:, :CSIZE], top[:, CSIZE:])
        e = jnp.exp((s - jnp.concatenate([top, top], axis=1)) * (HD**-0.5))
        total = jnp.sum(e, axis=0, keepdims=True)
        inv = 1.0 / (total[:, :CSIZE] + total[:, CSIZE:])
        p = (e * jnp.concatenate([inv, inv], axis=1)).astype(BF)
        halves = [p[i * HALF : (i + 1) * HALF, h : h + CSIZE] for i in range(MAXB) for h in (0, CSIZE)]
        for j in range(MAXB):
            prob_ref[u, j] = jnp.concatenate(halves[2 * j : 2 * j + 2], axis=0)
        vals = jnp.concatenate([kv_ref[slots[u][j], ids[u][j], 64:128, :] for j in range(MAXB)], axis=1)
        att = jnp.dot(vals, jnp.concatenate(halves, axis=0), preferred_element_type=F32)
        wide_ref[u * HD : (u + 1) * HD, :] = att
    split = att_ref.shape[0]
    for p in range(split):
        att_ref[p] = wide_ref[pl.ds(p, att_ref.shape[1], stride=split), :].astype(BF)


def forward(site, blk, cnt, recv, kvs, split):
    n = recv.shape[0]
    return pl.pallas_call(
        forward_kernel,
        grid_spec=pltpu.PrefetchScalarGridSpec(
            num_scalar_prefetch=3,
            grid=(n // ROWS,),
            in_specs=[
                pl.BlockSpec((ROWS, 64, CSIZE), lambda i, *_: (i, 2, 0)),
            ]
            + [pl.BlockSpec(memory_space=pl.ANY)] * SITE,
            out_specs=[
                pl.BlockSpec((split, ROWS * HD // split, CSIZE), lambda i, *_: (0, i, 0)),
                pl.BlockSpec((ROWS, MAXB, CSIZE, CSIZE), lambda i, *_: (i, 0, 0, 0)),
            ],
            scratch_shapes=[
                pltpu.VMEM((SITE,) + kvs[0].shape, BF),
                pltpu.VMEM((ROWS * HD, CSIZE), F32),
                pltpu.SemaphoreType.DMA((SITE,)),
            ],
        ),
        out_shape=[
            jax.ShapeDtypeStruct((split, n * HD // split, CSIZE), BF),
            jax.ShapeDtypeStruct((n, MAXB, CSIZE, CSIZE), BF),
        ],
        compiler_params=params(60),
        cost_estimate=pl.CostEstimate(
            flops=n * 4 * MAXB * CSIZE * CSIZE * HD, bytes_accessed=5 << 20, transcendentals=n * MAXB * CSIZE * CSIZE
        ),
        name="attend",
    )(site, blk, cnt, recv, *kvs)


def backward_kernel(site_ref, blk_ref, cnt_ref, g_ref, prob_ref, keep_ref, swap_ref, acc_ref):
    step = pl.program_id(0)

    @pl.when(step == 0)
    def _():
        acc_ref[...] = jnp.zeros_like(acc_ref)

    cluster = SITE * step + site_ref[0]
    number = cnt_ref[cluster]
    g = g_ref[0]
    for j in range(MAXB):

        @pl.when(j < number)
        def _():
            at = blk_ref[MAXB * cluster + j]
            acc_ref[at] += lax.dot_general(
                g, prob_ref[0, j], (((1,), (1,)), ((), ())), preferred_element_type=F32
            )

    @pl.when(step == pl.num_programs(0) - 1)
    def _():
        for t in range(SITE):
            first = pl.multiple_of(16 * (site_ref[0] ^ t), 16)
            (swap_ref if t % 2 else keep_ref)[t // 2] = acc_ref[:, pl.ds(first, 16), :].astype(BF)


def backward(site, blk, cnt, recv, probs):
    n = recv.shape[0]
    clusters = SITE * n
    return pl.pallas_call(
        backward_kernel,
        grid_spec=pltpu.PrefetchScalarGridSpec(
            num_scalar_prefetch=3,
            grid=(n,),
            in_specs=[
                pl.BlockSpec((1, 64, CSIZE), lambda i, *_: (i, 3, 0)),
                pl.BlockSpec((1, MAXB, CSIZE, CSIZE), lambda i, *_: (i, 0, 0, 0)),
            ],
            out_specs=[pl.BlockSpec((2, clusters, 16, CSIZE), lambda i, *_: (0, 0, 0, 0))] * 2,
            scratch_shapes=[pltpu.VMEM((clusters, HD, CSIZE), F32)],
        ),
        out_shape=[jax.ShapeDtypeStruct((2, clusters, 16, CSIZE), BF)] * 2,
        compiler_params=params(),
        cost_estimate=pl.CostEstimate(
            flops=n * 2 * MAXB * CSIZE * CSIZE * HD, bytes_accessed=3 << 20, transcendentals=0
        ),
        name="value_contrib",
    )(site, blk, cnt, recv, probs)


def weight_kernel(att_ref, cot_ref, out_ref, acc_ref):
    step = pl.program_id(0)

    @pl.when(step == 0)
    def _():
        acc_ref[...] = jnp.zeros_like(acc_ref)

    att = jnp.concatenate([att_ref[i] for i in range(att_ref.shape[0])], axis=1)
    acc_ref[...] += jnp.dot(att, cot_ref[...], preferred_element_type=F32)

    @pl.when(step == pl.num_programs(0) - 1)
    def _():
        for i in range(out_ref.shape[1]):
            out_ref[:, i, :] = acc_ref[:, CSIZE * i : CSIZE * (i + 1)]


def weight_part(att, cots):
    n, rows, nodes = att.shape
    width = cots.shape[1]
    batches = min(BATCHES, n)
    return pl.pallas_call(
        weight_kernel,
        grid=(n // batches,),
        in_specs=[
            pl.BlockSpec((batches, rows, nodes), lambda i: (i, 0, 0)),
            pl.BlockSpec((batches * nodes, width), lambda i: (i, 0)),
        ],
        out_specs=pl.BlockSpec((rows, width // CSIZE, CSIZE), lambda i: (0, 0, 0)),
        out_shape=jax.ShapeDtypeStruct((rows, width // CSIZE, CSIZE), F32),
        scratch_shapes=[pltpu.VMEM((rows, width), F32)],
        compiler_params=params(60),
        cost_estimate=pl.CostEstimate(
            flops=2 * n * rows * nodes * width, bytes_accessed=2 * n * nodes * width, transcendentals=0
        ),
        name="weight_part",
    )(att, cots)


def gather_kernel(back_ref, att_ref, out_ref):
    n, rows, _ = att_ref.shape
    total = jnp.sum(back_ref[...].astype(F32), axis=0)[16:]
    high = total.astype(BF).astype(F32)
    both = jnp.concatenate([high, total - high], axis=0).astype(BF)
    for p in range(n):
        out_ref[p, :rows, :] = att_ref[p]
        out_ref[p, rows:, :] = both


def gather_send(back, att):
    n, rows, nodes = att.shape
    more = 2 * (back.shape[1] - 16)
    return pl.pallas_call(
        gather_kernel,
        out_shape=jax.ShapeDtypeStruct((n, rows + more, nodes), BF),
        compiler_params=params(),
        cost_estimate=pl.CostEstimate(flops=back.size, bytes_accessed=2 * back.size + 4 * att.size, transcendentals=0),
        name="gather_send",
    )(back, att)


def finish_kernel(got_ref, w_ref, layer_ref, weight_ref, wide_ref, rows_ref):
    n, total, nodes = got_ref.shape
    rows = w_ref.shape[0] // n
    more = (total - rows) // 2
    for p in range(n):
        wide_ref[pl.ds(p, rows, stride=n), :] = got_ref[p, :rows, :].astype(F32)
        both = got_ref[p, rows:, :].astype(F32)
        rows_ref[p * more : (p + 1) * more, :] = both[:more] + both[more:]
    layer_ref[...] = jnp.dot(
        wide_ref[...].T.astype(BF), w_ref[...], preferred_element_type=F32
    ).astype(BF)
    pieces = weight_ref.shape[1] // nodes
    for i in range(pieces):
        weight_ref[:, i * nodes : (i + 1) * nodes] = rows_ref[pl.ds(i, weight_ref.shape[0], stride=pieces), :]


def finish(got, w_out, own):
    nodes = got.shape[2]
    width = w_out.shape[0]
    more = (got.shape[1] - width // got.shape[0]) // 2
    return pl.pallas_call(
        finish_kernel,
        out_shape=[
            jax.ShapeDtypeStruct((nodes, width), BF),
            jax.ShapeDtypeStruct((own, width), F32),
        ],
        scratch_shapes=[pltpu.VMEM((width, nodes), F32), pltpu.VMEM((got.shape[0] * more, nodes), F32)],
        compiler_params=params(),
        cost_estimate=pl.CostEstimate(flops=2 * nodes * width * width, bytes_accessed=2 * width * width, transcendentals=0),
        name="finish",
    )(got, w_out)


def flip_kernel(x_ref, out_ref):
    out_ref[...] = x_ref[...].T


def flip(x):
    rows, cols = x.shape
    return pl.pallas_call(
        flip_kernel,
        out_shape=jax.ShapeDtypeStruct((cols, rows), x.dtype),
        compiler_params=params(),
        cost_estimate=pl.CostEstimate(flops=0, bytes_accessed=4 * rows * cols, transcendentals=0),
        name="flip",
    )(x)


def body(queries, keys, values, cotangent, w_out, blocks, counts):
    nseq = lax.axis_size("seq")
    ndp = lax.axis_size("dp")
    width = w_out.shape[0]
    site = (lax.axis_index("seq") % SITE).astype(jnp.int32)[None]
    same_site = [[SITE * h + s for h in range(H)] for s in range(SITE)]
    same_site_dp = [[p * nseq + i for p in range(ndp) for i in group] for group in same_site]

    def swap(x, bit):
        return lax.ppermute(x, "seq", [(i, i ^ bit) for i in range(nseq)])

    blk = blocks[0].reshape(-1)
    cnt = counts[0]
    cot = cotangent[0]

    sent = pack(queries[0], keys[0], values[0], cot, w_out)
    recv = lax.all_to_all(sent, "seq", split_axis=0, concat_axis=0, tiled=True, axis_index_groups=same_site)

    cots = lax.all_gather(cot, "dp", axis=0, tiled=True)

    kv, cots = lax.optimization_barrier((recv[:, :128], cots))
    kv_z = swap(kv, 2)
    kvs = [kv, swap(kv, 1), kv_z, swap(kv_z, 1)]
    att, probs = forward(site, blk, cnt, recv, kvs, ndp)
    sent_att = att.reshape(ndp * H, HD // ndp, CSIZE)
    pieces = lax.all_to_all(
        sent_att, ("dp", "seq"), split_axis=0, concat_axis=0, tiled=True, axis_index_groups=same_site_dp
    ).reshape(ndp, width // ndp, CSIZE)
    keep, give = backward(site, blk, cnt, recv, probs)
    chip = (keep.astype(F32) + swap(give, 1).astype(F32)).astype(BF)
    contrib = (chip[0].astype(F32) + swap(chip[1], 2).astype(F32)).astype(BF)

    part = weight_part(pieces, cots).astype(BF).reshape(nseq, -1, CSIZE)
    back = lax.all_to_all(
        jnp.concatenate([contrib, part], axis=1), "seq", split_axis=0, concat_axis=0, tiled=True
    )
    got = lax.all_to_all(gather_send(back, pieces), "dp", split_axis=0, concat_axis=0, tiled=True)
    value_grad = flip(back[:, :16].reshape(width, CSIZE))
    layer_out, weight_grad = finish(got, w_out, width // nseq)
    return (layer_out[None], value_grad[None], weight_grad)


def solution(mesh):
    return jax.shard_map(
        body,
        mesh=mesh,
        in_specs=(
            P("dp", "seq", None),
            P("dp", "seq", None),
            P("dp", "seq", None),
            P("dp", "seq", None),
            P(),
            P("dp", None, None),
            P("dp", None),
        ),
        out_specs=(P("dp", "seq", None), P("dp", "seq", None), P("seq", None)),
        check_vma=False,
    )
```

```python
import jax
import jax.numpy as jnp
from jax import lax
from jax.experimental import pallas as pl
from jax.experimental.pallas import tpu as pltpu
from jax.sharding import PartitionSpec as P

H = 16
HD = 64
CSIZE = 128
HALF = CSIZE // 2
MAXB = 4
SITE = 4
BATCHES = 8
ROWS = 8
PAIR = 8
BROWS = 8
BF = jnp.bfloat16
F32 = jnp.float32


def params(mib=40):
    return pltpu.CompilerParams(vmem_limit_bytes=mib * 1024 * 1024)


def pack_kernel(q_ref, k_ref, v_ref, c_ref, w_ref, out_ref, ct_ref):
    @pl.when(pl.program_id(0) == 0)
    def _():
        ct_ref[...] = c_ref[...].T

    keys = k_ref[...]
    vals = v_ref[...].T
    qrys = q_ref[...].T
    grad = jnp.dot(w_ref[...], ct_ref[...], preferred_element_type=F32).astype(BF)
    for i in range(PAIR):
        part = keys[:, i * HD : (i + 1) * HD]
        out_ref[i, 0:HALF, :] = jnp.concatenate([part[:HALF], part[HALF:]], axis=1)
        out_ref[i, 64:128, :] = vals[i * HD : (i + 1) * HD]
        out_ref[i, 128:192, :] = qrys[i * HD : (i + 1) * HD]
        out_ref[i, 192:256, :] = grad[i * HD : (i + 1) * HD]


def pack(q, k, v, cot, w_out):
    rows, width = q.shape
    pair = pl.BlockSpec((rows, PAIR * HD), lambda i: (0, i))
    return pl.pallas_call(
        pack_kernel,
        grid=(H // PAIR,),
        in_specs=[
            pair,
            pair,
            pair,
            pl.BlockSpec((rows, width), lambda i: (0, 0)),
            pl.BlockSpec((PAIR * HD, width), lambda i: (i, 0)),
        ],
        out_specs=pl.BlockSpec((PAIR, 256, CSIZE), lambda i: (i, 0, 0)),
        scratch_shapes=[pltpu.VMEM((width, rows), BF)],
        out_shape=jax.ShapeDtypeStruct((H, 256, CSIZE), BF),
        compiler_params=params(60),
        cost_estimate=pl.CostEstimate(
            flops=2 * rows * width * width, bytes_accessed=2 * width * width + 10 * rows * width, transcendentals=0
        ),
        name="pack",
    )(q, k, v, cot, w_out)


def forward_kernel(site_ref, blk_ref, cnt_ref, q_ref, kv0, kv1, kv2, kv3, att_ref, prob_ref, kv_ref, wide_ref, sems):
    @pl.when(pl.program_id(0) == 0)
    def _():
        copies = [
            pltpu.make_async_copy(part, kv_ref.at[t], sems.at[t])
            for t, part in enumerate((kv0, kv1, kv2, kv3))
        ]
        for copy in copies:
            copy.start()
        for copy in copies:
            copy.wait()

    count = q_ref.shape[0]
    ids, slots, scores = [], [], []
    for u in range(count):
        cluster = SITE * (count * pl.program_id(0) + u) + site_ref[0]
        number = cnt_ref[cluster]
        q = q_ref[u]
        zero = jnp.zeros_like(q)
        both = jnp.concatenate(
            [jnp.concatenate([q, zero], axis=1), jnp.concatenate([zero, q], axis=1)], axis=0
        )
        at = [blk_ref[MAXB * cluster + j] for j in range(MAXB)]
        ids.append([i // SITE for i in at])
        slots.append([(i % SITE) ^ site_ref[0] for i in at])
        mine = []
        for j in range(MAXB):
            keys = kv_ref[slots[u][j], ids[u][j], 0:64, :]
            s = jnp.dot(keys, both, preferred_element_type=F32)
            mine.append(s if j == 0 else jnp.where(j < number, s, -1e30))
        scores.append(jnp.concatenate(mine, axis=0))
    for u in range(count):
        s = scores[u]
        top = jnp.max(s, axis=0, keepdims=True)
        top = jnp.maximum(top[:, :CSIZE], top[:, CSIZE:])
        e = jnp.exp((s - jnp.concatenate([top, top], axis=1)) * (HD**-0.5))
        total = jnp.sum(e, axis=0, keepdims=True)
        inv = 1.0 / (total[:, :CSIZE] + total[:, CSIZE:])
        p = (e * jnp.concatenate([inv, inv], axis=1)).astype(BF)
        halves = [p[i * HALF : (i + 1) * HALF, h : h + CSIZE] for i in range(MAXB) for h in (0, CSIZE)]
        for j in range(MAXB):
            prob_ref[u, j] = jnp.concatenate(halves[2 * j : 2 * j + 2], axis=0)
        vals = jnp.concatenate([kv_ref[slots[u][j], ids[u][j], 64:128, :] for j in range(MAXB)], axis=1)
        att = jnp.dot(vals, jnp.concatenate(halves, axis=0), preferred_element_type=F32)
        wide_ref[u * HD : (u + 1) * HD, :] = att
    split = att_ref.shape[0]
    for p in range(split):
        att_ref[p] = wide_ref[pl.ds(p, att_ref.shape[1], stride=split), :].astype(BF)


def forward(site, blk, cnt, recv, kvs, split):
    n = recv.shape[0]
    return pl.pallas_call(
        forward_kernel,
        grid_spec=pltpu.PrefetchScalarGridSpec(
            num_scalar_prefetch=3,
            grid=(n // ROWS,),
            in_specs=[
                pl.BlockSpec((ROWS, 64, CSIZE), lambda i, *_: (i, 2, 0)),
            ]
            + [pl.BlockSpec(memory_space=pl.ANY)] * SITE,
            out_specs=[
                pl.BlockSpec((split, ROWS * HD // split, CSIZE), lambda i, *_: (0, i, 0)),
                pl.BlockSpec((ROWS, MAXB, CSIZE, CSIZE), lambda i, *_: (i, 0, 0, 0)),
            ],
            scratch_shapes=[
                pltpu.VMEM((SITE,) + kvs[0].shape, BF),
                pltpu.VMEM((ROWS * HD, CSIZE), F32),
                pltpu.SemaphoreType.DMA((SITE,)),
            ],
        ),
        out_shape=[
            jax.ShapeDtypeStruct((split, n * HD // split, CSIZE), BF),
            jax.ShapeDtypeStruct((n, MAXB, CSIZE, CSIZE), BF),
        ],
        compiler_params=params(60),
        cost_estimate=pl.CostEstimate(
            flops=n * 4 * MAXB * CSIZE * CSIZE * HD, bytes_accessed=5 << 20, transcendentals=n * MAXB * CSIZE * CSIZE
        ),
        name="attend",
    )(site, blk, cnt, recv, *kvs)


def backward_kernel(site_ref, blk_ref, g_ref, prob_ref, keep_ref, swap_ref, acc_ref):
    step = pl.program_id(0)

    @pl.when(step == 0)
    def _():
        acc_ref[...] = jnp.zeros_like(acc_ref)

    count = g_ref.shape[0]
    for u in range(count):
        cluster = SITE * (count * step + u) + site_ref[0]
        terms = [
            lax.dot_general(g_ref[u], prob_ref[u, j], (((1,), (1,)), ((), ())), preferred_element_type=F32)
            for j in range(MAXB)
        ]
        for j in range(MAXB):
            acc_ref[blk_ref[MAXB * cluster + j]] += terms[j]

    @pl.when(step == pl.num_programs(0) - 1)
    def _():
        for t in range(SITE):
            first = pl.multiple_of(16 * (site_ref[0] ^ t), 16)
            (swap_ref if t % 2 else keep_ref)[t // 2] = acc_ref[:, pl.ds(first, 16), :].astype(BF)


def backward(site, blk, recv, probs):
    n = recv.shape[0]
    clusters = SITE * n
    return pl.pallas_call(
        backward_kernel,
        grid_spec=pltpu.PrefetchScalarGridSpec(
            num_scalar_prefetch=2,
            grid=(n // BROWS,),
            in_specs=[
                pl.BlockSpec((BROWS, 64, CSIZE), lambda i, *_: (i, 3, 0)),
                pl.BlockSpec((BROWS, MAXB, CSIZE, CSIZE), lambda i, *_: (i, 0, 0, 0)),
            ],
            out_specs=[pl.BlockSpec((2, clusters, 16, CSIZE), lambda i, *_: (0, 0, 0, 0))] * 2,
            scratch_shapes=[pltpu.VMEM((clusters, HD, CSIZE), F32)],
        ),
        out_shape=[jax.ShapeDtypeStruct((2, clusters, 16, CSIZE), BF)] * 2,
        compiler_params=params(60),
        cost_estimate=pl.CostEstimate(
            flops=n * 2 * MAXB * CSIZE * CSIZE * HD, bytes_accessed=3 << 20, transcendentals=0
        ),
        name="value_contrib",
    )(site, blk, recv, probs)


def merge_kernel(own_ref, other_ref, part_ref, out_ref):
    total = own_ref[...].astype(F32) + other_ref[...].astype(F32)
    out_ref[...] = jnp.concatenate([total, part_ref[...]], axis=1).astype(BF)


def merge(own, other, part):
    n, rows, nodes = own.shape
    return pl.pallas_call(
        merge_kernel,
        out_shape=jax.ShapeDtypeStruct((n, rows + part.shape[1], nodes), BF),
        compiler_params=params(),
        cost_estimate=pl.CostEstimate(flops=own.size, bytes_accessed=6 * own.size + 6 * part.size, transcendentals=0),
        name="merge",
    )(own, other, part)


def weight_kernel(att_ref, cot_ref, out_ref, acc_ref):
    step = pl.program_id(0)

    @pl.when(step == 0)
    def _():
        acc_ref[...] = jnp.zeros_like(acc_ref)

    att = jnp.concatenate([att_ref[i] for i in range(att_ref.shape[0])], axis=1)
    acc_ref[...] += jnp.dot(att, cot_ref[...], preferred_element_type=F32)

    @pl.when(step == pl.num_programs(0) - 1)
    def _():
        for i in range(out_ref.shape[1]):
            out_ref[:, i, :] = acc_ref[:, CSIZE * i : CSIZE * (i + 1)]


def weight_part(att, cots):
    n, rows, nodes = att.shape
    width = cots.shape[1]
    batches = min(BATCHES, n)
    return pl.pallas_call(
        weight_kernel,
        grid=(n // batches,),
        in_specs=[
            pl.BlockSpec((batches, rows, nodes), lambda i: (i, 0, 0)),
            pl.BlockSpec((batches * nodes, width), lambda i: (i, 0)),
        ],
        out_specs=pl.BlockSpec((rows, width // CSIZE, CSIZE), lambda i: (0, 0, 0)),
        out_shape=jax.ShapeDtypeStruct((rows, width // CSIZE, CSIZE), F32),
        scratch_shapes=[pltpu.VMEM((rows, width), F32)],
        compiler_params=params(60),
        cost_estimate=pl.CostEstimate(
            flops=2 * n * rows * nodes * width, bytes_accessed=2 * n * nodes * width, transcendentals=0
        ),
        name="weight_part",
    )(att, cots)


def gather_kernel(back_ref, att_ref, out_ref):
    n, rows, _ = att_ref.shape
    total = jnp.sum(back_ref[...].astype(F32), axis=0)[16:]
    high = total.astype(BF).astype(F32)
    both = jnp.concatenate([high, total - high], axis=0).astype(BF)
    for p in range(n):
        out_ref[p, :rows, :] = att_ref[p]
        out_ref[p, rows:, :] = both


def gather_send(back, att):
    n, rows, nodes = att.shape
    more = 2 * (back.shape[1] - 16)
    return pl.pallas_call(
        gather_kernel,
        out_shape=jax.ShapeDtypeStruct((n, rows + more, nodes), BF),
        compiler_params=params(),
        cost_estimate=pl.CostEstimate(flops=back.size, bytes_accessed=2 * back.size + 4 * att.size, transcendentals=0),
        name="gather_send",
    )(back, att)


def finish_kernel(got_ref, w_ref, layer_ref, weight_ref, wide_ref, rows_ref):
    n, total, nodes = got_ref.shape
    rows = w_ref.shape[0] // n
    more = (total - rows) // 2
    for p in range(n):
        wide_ref[pl.ds(p, rows, stride=n), :] = got_ref[p, :rows, :].astype(F32)
        both = got_ref[p, rows:, :].astype(F32)
        rows_ref[p * more : (p + 1) * more, :] = both[:more] + both[more:]
    layer_ref[...] = jnp.dot(
        wide_ref[...].T.astype(BF), w_ref[...], preferred_element_type=F32
    ).astype(BF)
    pieces = weight_ref.shape[1] // nodes
    for i in range(pieces):
        weight_ref[:, i * nodes : (i + 1) * nodes] = rows_ref[pl.ds(i, weight_ref.shape[0], stride=pieces), :]


def finish(got, w_out, own):
    nodes = got.shape[2]
    width = w_out.shape[0]
    more = (got.shape[1] - width // got.shape[0]) // 2
    return pl.pallas_call(
        finish_kernel,
        out_shape=[
            jax.ShapeDtypeStruct((nodes, width), BF),
            jax.ShapeDtypeStruct((own, width), F32),
        ],
        scratch_shapes=[pltpu.VMEM((width, nodes), F32), pltpu.VMEM((got.shape[0] * more, nodes), F32)],
        compiler_params=params(),
        cost_estimate=pl.CostEstimate(flops=2 * nodes * width * width, bytes_accessed=2 * width * width, transcendentals=0),
        name="finish",
    )(got, w_out)


def flip_kernel(x_ref, out_ref):
    out_ref[...] = x_ref[...].T


def flip(x):
    rows, cols = x.shape
    return pl.pallas_call(
        flip_kernel,
        out_shape=jax.ShapeDtypeStruct((cols, rows), x.dtype),
        compiler_params=params(),
        cost_estimate=pl.CostEstimate(flops=0, bytes_accessed=4 * rows * cols, transcendentals=0),
        name="flip",
    )(x)


def body(queries, keys, values, cotangent, w_out, blocks, counts):
    nseq = lax.axis_size("seq")
    ndp = lax.axis_size("dp")
    width = w_out.shape[0]
    site = (lax.axis_index("seq") % SITE).astype(jnp.int32)[None]
    same_site = [[SITE * h + s for h in range(H)] for s in range(SITE)]
    same_site_dp = [[p * nseq + i for p in range(ndp) for i in group] for group in same_site]

    def swap(x, bit):
        return lax.ppermute(x, "seq", [(i, i ^ bit) for i in range(nseq)])

    blk = blocks[0].reshape(-1)
    cnt = counts[0]
    cot = cotangent[0]

    sent = pack(queries[0], keys[0], values[0], cot, w_out)
    recv = lax.all_to_all(sent, "seq", split_axis=0, concat_axis=0, tiled=True, axis_index_groups=same_site)

    cots = lax.all_gather(cot, "dp", axis=0, tiled=True)

    kv, cots = lax.optimization_barrier((recv[:, :128], cots))
    kv_z = swap(kv, 2)
    kvs = [kv, swap(kv, 1), kv_z, swap(kv_z, 1)]
    att, probs = forward(site, blk, cnt, recv, kvs, ndp)
    sent_att = att.reshape(ndp * H, HD // ndp, CSIZE)
    pieces = lax.all_to_all(
        sent_att, ("dp", "seq"), split_axis=0, concat_axis=0, tiled=True, axis_index_groups=same_site_dp
    ).reshape(ndp, width // ndp, CSIZE)
    keep, give = backward(site, blk, recv, probs)
    chip = (keep.astype(F32) + swap(give, 1).astype(F32)).astype(BF)
    part = weight_part(pieces, cots).reshape(nseq, -1, CSIZE)
    back = lax.all_to_all(
        merge(chip[0], swap(chip[1], 2), part), "seq", split_axis=0, concat_axis=0, tiled=True
    )
    got = lax.all_to_all(gather_send(back, pieces), "dp", split_axis=0, concat_axis=0, tiled=True)
    value_grad = flip(back[:, :16].reshape(width, CSIZE))
    layer_out, weight_grad = finish(got, w_out, width // nseq)
    return (layer_out[None], value_grad[None], weight_grad)


def solution(mesh):
    return jax.shard_map(
        body,
        mesh=mesh,
        in_specs=(
            P("dp", "seq", None),
            P("dp", "seq", None),
            P("dp", "seq", None),
            P("dp", "seq", None),
            P(),
            P("dp", None, None),
            P("dp", None),
        ),
        out_specs=(P("dp", "seq", None), P("dp", "seq", None), P("seq", None)),
        check_vma=False,
    )
```

```python
import jax
import jax.numpy as jnp
from jax import lax
from jax.experimental import pallas as pl
from jax.experimental.pallas import tpu as pltpu
from jax.sharding import PartitionSpec as P

H = 16
HD = 64
CSIZE = 128
HALF = CSIZE // 2
MAXB = 4
SITE = 4
ROWS = 8
PAIR = 8
BROWS = 8
BF = jnp.bfloat16
F32 = jnp.float32


def params(mib=40):
    return pltpu.CompilerParams(vmem_limit_bytes=mib * 1024 * 1024)


def pack_kernel(q_ref, k_ref, v_ref, c_ref, w_ref, out_ref, ct_ref):
    @pl.when(pl.program_id(0) == 0)
    def _():
        ct_ref[...] = c_ref[...].T

    keys = k_ref[...]
    vals = v_ref[...].T
    qrys = q_ref[...].T
    grad = jnp.dot(w_ref[...], ct_ref[...], preferred_element_type=F32).astype(BF)
    for i in range(PAIR):
        part = keys[:, i * HD : (i + 1) * HD]
        out_ref[i, 0:HALF, :] = jnp.concatenate([part[:HALF], part[HALF:]], axis=1)
        out_ref[i, 64:128, :] = vals[i * HD : (i + 1) * HD]
        out_ref[i, 128:192, :] = qrys[i * HD : (i + 1) * HD]
        out_ref[i, 192:256, :] = grad[i * HD : (i + 1) * HD]


def pack(q, k, v, cot, w_out):
    rows, width = q.shape
    pair = pl.BlockSpec((rows, PAIR * HD), lambda i: (0, i))
    return pl.pallas_call(
        pack_kernel,
        grid=(H // PAIR,),
        in_specs=[
            pair,
            pair,
            pair,
            pl.BlockSpec((rows, width), lambda i: (0, 0)),
            pl.BlockSpec((PAIR * HD, width), lambda i: (i, 0)),
        ],
        out_specs=pl.BlockSpec((PAIR, 256, CSIZE), lambda i: (i, 0, 0)),
        scratch_shapes=[pltpu.VMEM((width, rows), BF)],
        out_shape=jax.ShapeDtypeStruct((H, 256, CSIZE), BF),
        compiler_params=params(60),
        cost_estimate=pl.CostEstimate(
            flops=2 * rows * width * width, bytes_accessed=2 * width * width + 10 * rows * width, transcendentals=0
        ),
        name="pack",
    )(q, k, v, cot, w_out)


def forward_kernel(site_ref, blk_ref, cnt_ref, q_ref, kv0, kv1, kv2, kv3, att_ref, prob_ref, kv_ref, wide_ref, sems):
    @pl.when(pl.program_id(0) == 0)
    def _():
        copies = [
            pltpu.make_async_copy(part, kv_ref.at[t], sems.at[t])
            for t, part in enumerate((kv0, kv1, kv2, kv3))
        ]
        for copy in copies:
            copy.start()
        for copy in copies:
            copy.wait()

    count = q_ref.shape[0]
    ids, slots, scores = [], [], []
    for u in range(count):
        cluster = SITE * (count * pl.program_id(0) + u) + site_ref[0]
        number = cnt_ref[cluster]
        q = q_ref[u]
        zero = jnp.zeros_like(q)
        both = jnp.concatenate(
            [jnp.concatenate([q, zero], axis=1), jnp.concatenate([zero, q], axis=1)], axis=0
        )
        at = [blk_ref[MAXB * cluster + j] for j in range(MAXB)]
        ids.append([i // SITE for i in at])
        slots.append([(i % SITE) ^ site_ref[0] for i in at])
        mine = []
        for j in range(MAXB):
            keys = kv_ref[slots[u][j], ids[u][j], 0:64, :]
            s = jnp.dot(keys, both, preferred_element_type=F32)
            mine.append(s if j == 0 else jnp.where(j < number, s, -1e30))
        scores.append(jnp.concatenate(mine, axis=0))
    for u in range(count):
        s = scores[u]
        top = jnp.max(s, axis=0, keepdims=True)
        top = jnp.maximum(top[:, :CSIZE], top[:, CSIZE:])
        e = jnp.exp((s - jnp.concatenate([top, top], axis=1)) * (HD**-0.5))
        total = jnp.sum(e, axis=0, keepdims=True)
        inv = 1.0 / (total[:, :CSIZE] + total[:, CSIZE:])
        p = (e * jnp.concatenate([inv, inv], axis=1)).astype(BF)
        halves = [p[i * HALF : (i + 1) * HALF, h : h + CSIZE] for i in range(MAXB) for h in (0, CSIZE)]
        for j in range(MAXB):
            prob_ref[u, j] = jnp.concatenate(halves[2 * j : 2 * j + 2], axis=0)
        vals = jnp.concatenate([kv_ref[slots[u][j], ids[u][j], 64:128, :] for j in range(MAXB)], axis=1)
        att = jnp.dot(vals, jnp.concatenate(halves, axis=0), preferred_element_type=F32)
        wide_ref[u * HD : (u + 1) * HD, :] = att
    split = att_ref.shape[0]
    for p in range(split):
        att_ref[p] = wide_ref[pl.ds(p, att_ref.shape[1], stride=split), :].astype(BF)


def forward(site, blk, cnt, recv, kvs, split):
    n = recv.shape[0]
    return pl.pallas_call(
        forward_kernel,
        grid_spec=pltpu.PrefetchScalarGridSpec(
            num_scalar_prefetch=3,
            grid=(n // ROWS,),
            in_specs=[
                pl.BlockSpec((ROWS, 64, CSIZE), lambda i, *_: (i, 2, 0)),
            ]
            + [pl.BlockSpec(memory_space=pl.ANY)] * SITE,
            out_specs=[
                pl.BlockSpec((split, ROWS * HD // split, CSIZE), lambda i, *_: (0, i, 0)),
                pl.BlockSpec((ROWS, MAXB, CSIZE, CSIZE), lambda i, *_: (i, 0, 0, 0)),
            ],
            scratch_shapes=[
                pltpu.VMEM((SITE,) + kvs[0].shape, BF),
                pltpu.VMEM((ROWS * HD, CSIZE), F32),
                pltpu.SemaphoreType.DMA((SITE,)),
            ],
        ),
        out_shape=[
            jax.ShapeDtypeStruct((split, n * HD // split, CSIZE), BF),
            jax.ShapeDtypeStruct((n, MAXB, CSIZE, CSIZE), BF),
        ],
        compiler_params=params(60),
        cost_estimate=pl.CostEstimate(
            flops=n * 4 * MAXB * CSIZE * CSIZE * HD, bytes_accessed=5 << 20, transcendentals=n * MAXB * CSIZE * CSIZE
        ),
        name="attend",
    )(site, blk, cnt, recv, *kvs)


def backward_kernel(site_ref, blk_ref, g_ref, prob_ref, keep_ref, swap_ref, acc_ref):
    step = pl.program_id(0)

    @pl.when(step == 0)
    def _():
        acc_ref[...] = jnp.zeros_like(acc_ref)

    count = g_ref.shape[0]
    for u in range(count):
        cluster = SITE * (count * step + u) + site_ref[0]
        terms = [
            lax.dot_general(g_ref[u], prob_ref[u, j], (((1,), (1,)), ((), ())), preferred_element_type=F32)
            for j in range(MAXB)
        ]
        for j in range(MAXB):
            acc_ref[blk_ref[MAXB * cluster + j]] += terms[j]

    @pl.when(step == pl.num_programs(0) - 1)
    def _():
        for t in range(SITE):
            first = pl.multiple_of(16 * (site_ref[0] ^ t), 16)
            (swap_ref if t % 2 else keep_ref)[t // 2] = acc_ref[:, pl.ds(first, 16), :].astype(BF)


def backward(site, blk, recv, probs):
    n = recv.shape[0]
    clusters = SITE * n
    return pl.pallas_call(
        backward_kernel,
        grid_spec=pltpu.PrefetchScalarGridSpec(
            num_scalar_prefetch=2,
            grid=(n // BROWS,),
            in_specs=[
                pl.BlockSpec((BROWS, 64, CSIZE), lambda i, *_: (i, 3, 0)),
                pl.BlockSpec((BROWS, MAXB, CSIZE, CSIZE), lambda i, *_: (i, 0, 0, 0)),
            ],
            out_specs=[pl.BlockSpec((2, clusters, 16, CSIZE), lambda i, *_: (0, 0, 0, 0))] * 2,
            scratch_shapes=[pltpu.VMEM((clusters, HD, CSIZE), F32)],
        ),
        out_shape=[jax.ShapeDtypeStruct((2, clusters, 16, CSIZE), BF)] * 2,
        compiler_params=params(60),
        cost_estimate=pl.CostEstimate(
            flops=n * 2 * MAXB * CSIZE * CSIZE * HD, bytes_accessed=3 << 20, transcendentals=0
        ),
        name="value_contrib",
    )(site, blk, recv, probs)


def merge_kernel(own_ref, other_ref, part_ref, out_ref):
    total = own_ref[...].astype(F32) + other_ref[...].astype(F32)
    out_ref[...] = jnp.concatenate([total, part_ref[...]], axis=1).astype(BF)


def merge(own, other, part):
    n, rows, nodes = own.shape
    return pl.pallas_call(
        merge_kernel,
        out_shape=jax.ShapeDtypeStruct((n, rows + part.shape[1], nodes), BF),
        compiler_params=params(),
        cost_estimate=pl.CostEstimate(flops=own.size, bytes_accessed=6 * own.size + 6 * part.size, transcendentals=0),
        name="merge",
    )(own, other, part)


def weight_kernel(me_ref, att_ref, *refs):
    n = att_ref.shape[0]
    cots, (out_ref, cot_ref, acc_ref, sems) = refs[:n], refs[n:]
    copies = [pltpu.make_async_copy(cots[t], cot_ref.at[t], sems.at[t]) for t in range(n)]
    for copy in copies:
        copy.start()
    step = min(2, n)
    for t in range(0, n, step):
        for i in range(step):
            copies[t + i].wait()
        att = jnp.concatenate([att_ref[me_ref[0] ^ (t + i)] for i in range(step)], axis=1)
        cot = jnp.concatenate([cot_ref[t + i] for i in range(step)], axis=0)
        term = jnp.dot(att, cot, preferred_element_type=F32)
        acc_ref[...] = term if t == 0 else acc_ref[...] + term
    for i in range(out_ref.shape[1]):
        out_ref[:, i, :] = acc_ref[:, CSIZE * i : CSIZE * (i + 1)]


def weight_part(me, att, cots):
    n, rows, nodes = att.shape
    width = cots[0].shape[1]
    return pl.pallas_call(
        weight_kernel,
        grid_spec=pltpu.PrefetchScalarGridSpec(
            num_scalar_prefetch=1,
            grid=(1,),
            in_specs=[pl.BlockSpec(att.shape, lambda i, *_: (0, 0, 0))]
            + [pl.BlockSpec(memory_space=pl.ANY)] * n,
            out_specs=pl.BlockSpec((rows, width // CSIZE, CSIZE), lambda i, *_: (0, 0, 0)),
            scratch_shapes=[
                pltpu.VMEM((n, nodes, width), BF),
                pltpu.VMEM((rows, width), F32),
                pltpu.SemaphoreType.DMA((n,)),
            ],
        ),
        out_shape=jax.ShapeDtypeStruct((rows, width // CSIZE, CSIZE), F32),
        compiler_params=params(60),
        cost_estimate=pl.CostEstimate(
            flops=2 * n * rows * nodes * width, bytes_accessed=2 * n * nodes * width, transcendentals=0
        ),
        name="weight_part",
    )(me, att, *cots)


def gather_kernel(back_ref, att_ref, out_ref):
    n, rows, _ = att_ref.shape
    total = jnp.sum(back_ref[...].astype(F32), axis=0)[16:]
    high = total.astype(BF).astype(F32)
    both = jnp.concatenate([high, total - high], axis=0).astype(BF)
    for p in range(n):
        out_ref[p, :rows, :] = att_ref[p]
        out_ref[p, rows:, :] = both


def gather_send(back, att):
    n, rows, nodes = att.shape
    more = 2 * (back.shape[1] - 16)
    return pl.pallas_call(
        gather_kernel,
        out_shape=jax.ShapeDtypeStruct((n, rows + more, nodes), BF),
        compiler_params=params(),
        cost_estimate=pl.CostEstimate(flops=back.size, bytes_accessed=2 * back.size + 4 * att.size, transcendentals=0),
        name="gather_send",
    )(back, att)


def finish_kernel(got_ref, w_ref, layer_ref, weight_ref, wide_ref, rows_ref):
    n, total, nodes = got_ref.shape
    rows = w_ref.shape[0] // n
    more = (total - rows) // 2
    for p in range(n):
        wide_ref[pl.ds(p, rows, stride=n), :] = got_ref[p, :rows, :].astype(F32)
        both = got_ref[p, rows:, :].astype(F32)
        rows_ref[p * more : (p + 1) * more, :] = both[:more] + both[more:]
    layer_ref[...] = jnp.dot(
        wide_ref[...].T.astype(BF), w_ref[...], preferred_element_type=F32
    ).astype(BF)
    pieces = weight_ref.shape[1] // nodes
    for i in range(pieces):
        weight_ref[:, i * nodes : (i + 1) * nodes] = rows_ref[pl.ds(i, weight_ref.shape[0], stride=pieces), :]


def finish(got, w_out, own):
    nodes = got.shape[2]
    width = w_out.shape[0]
    more = (got.shape[1] - width // got.shape[0]) // 2
    return pl.pallas_call(
        finish_kernel,
        out_shape=[
            jax.ShapeDtypeStruct((nodes, width), BF),
            jax.ShapeDtypeStruct((own, width), F32),
        ],
        scratch_shapes=[pltpu.VMEM((width, nodes), F32), pltpu.VMEM((got.shape[0] * more, nodes), F32)],
        compiler_params=params(),
        cost_estimate=pl.CostEstimate(flops=2 * nodes * width * width, bytes_accessed=2 * width * width, transcendentals=0),
        name="finish",
    )(got, w_out)


def flip_kernel(x_ref, out_ref):
    out_ref[...] = x_ref[...].T


def flip(x):
    rows, cols = x.shape
    return pl.pallas_call(
        flip_kernel,
        out_shape=jax.ShapeDtypeStruct((cols, rows), x.dtype),
        compiler_params=params(),
        cost_estimate=pl.CostEstimate(flops=0, bytes_accessed=4 * rows * cols, transcendentals=0),
        name="flip",
    )(x)


def body(queries, keys, values, cotangent, w_out, blocks, counts):
    nseq = lax.axis_size("seq")
    ndp = lax.axis_size("dp")
    width = w_out.shape[0]
    me = lax.axis_index("dp").astype(jnp.int32)[None]
    site = (lax.axis_index("seq") % SITE).astype(jnp.int32)[None]
    same_site = [[SITE * h + s for h in range(H)] for s in range(SITE)]
    same_site_dp = [[p * nseq + i for p in range(ndp) for i in group] for group in same_site]

    def swap(x, bit):
        return lax.ppermute(x, "seq", [(i, i ^ bit) for i in range(nseq)])

    blk = blocks[0].reshape(-1)
    cnt = counts[0]
    cot = cotangent[0]

    sent = pack(queries[0], keys[0], values[0], cot, w_out)
    sent, cot = lax.optimization_barrier((sent, cot))
    cots = [cot] + [lax.ppermute(cot, "dp", [(i, i ^ t) for i in range(ndp)]) for t in range(1, ndp)]
    recv = lax.all_to_all(sent, "seq", split_axis=0, concat_axis=0, tiled=True, axis_index_groups=same_site)
    kv, cots = lax.optimization_barrier((recv[:, :128], cots))
    kv_z = swap(kv, 2)
    kvs = [kv, swap(kv, 1), kv_z, swap(kv_z, 1)]
    att, probs = forward(site, blk, cnt, recv, kvs, ndp)
    sent_att = att.reshape(ndp * H, HD // ndp, CSIZE)
    pieces = lax.all_to_all(
        sent_att, ("dp", "seq"), split_axis=0, concat_axis=0, tiled=True, axis_index_groups=same_site_dp
    ).reshape(ndp, width // ndp, CSIZE)
    keep, give = backward(site, blk, recv, probs)
    chip = (keep.astype(F32) + swap(give, 1).astype(F32)).astype(BF)
    part = weight_part(me, pieces, cots).reshape(nseq, -1, CSIZE)
    back = lax.all_to_all(
        merge(chip[0], swap(chip[1], 2), part), "seq", split_axis=0, concat_axis=0, tiled=True
    )
    got = lax.all_to_all(gather_send(back, pieces), "dp", split_axis=0, concat_axis=0, tiled=True)
    value_grad = flip(back[:, :16].reshape(width, CSIZE))
    layer_out, weight_grad = finish(got, w_out, width // nseq)
    return (layer_out[None], value_grad[None], weight_grad)


def solution(mesh):
    return jax.shard_map(
        body,
        mesh=mesh,
        in_specs=(
            P("dp", "seq", None),
            P("dp", "seq", None),
            P("dp", "seq", None),
            P("dp", "seq", None),
            P(),
            P("dp", None, None),
            P("dp", None),
        ),
        out_specs=(P("dp", "seq", None), P("dp", "seq", None), P("seq", None)),
        check_vma=False,
    )
```

```python
import math

import jax
import jax.numpy as jnp
from jax import lax
from jax.experimental import pallas as pl
from jax.experimental.pallas import tpu as pltpu
from jax.sharding import PartitionSpec as P

H = 16
HD = 64
CSIZE = 128
HALF = HD // 2
MAXB = 4
SITE = 4
ROWS = 8
PAIR = 8
BROWS = 8
BF = jnp.bfloat16
F32 = jnp.float32


def params(mib=40):
    return pltpu.CompilerParams(vmem_limit_bytes=mib * 1024 * 1024)


def pack_kernel(q_ref, k_ref, v_ref, c_ref, w_ref, out_ref, ct_ref):
    @pl.when(pl.program_id(0) == 0)
    def _():
        ct_ref[...] = c_ref[...].T

    keys = k_ref[...]
    vals = v_ref[...].T
    qrys = q_ref[...].T
    grad = jnp.dot(w_ref[...], ct_ref[...], preferred_element_type=F32).astype(BF)
    for i in range(PAIR):
        part = keys[:, i * HD : (i + 1) * HD]
        out_ref[i, 0:64, :] = jnp.concatenate([part[:64], part[64:]], axis=1)
        out_ref[i, 64:128, :] = vals[i * HD : (i + 1) * HD]
        out_ref[i, 128:192, :] = qrys[i * HD : (i + 1) * HD]
        out_ref[i, 192:256, :] = grad[i * HD : (i + 1) * HD]


def pack(q, k, v, cot, w_out):
    rows, width = q.shape
    pair = pl.BlockSpec((rows, PAIR * HD), lambda i: (0, i))
    return pl.pallas_call(
        pack_kernel,
        grid=(H // PAIR,),
        in_specs=[
            pair,
            pair,
            pair,
            pl.BlockSpec((rows, width), lambda i: (0, 0)),
            pl.BlockSpec((PAIR * HD, width), lambda i: (i, 0)),
        ],
        out_specs=pl.BlockSpec((PAIR, 256, CSIZE), lambda i: (i, 0, 0)),
        scratch_shapes=[pltpu.VMEM((width, rows), BF)],
        out_shape=jax.ShapeDtypeStruct((H, 256, CSIZE), BF),
        compiler_params=params(60),
        cost_estimate=pl.CostEstimate(
            flops=2 * rows * width * width, bytes_accessed=2 * width * width + 10 * rows * width, transcendentals=0
        ),
        name="pack",
    )(q, k, v, cot, w_out)


def forward_kernel(site_ref, blk_ref, cnt_ref, q_ref, kv0, kv1, kv2, kv3, att_ref, prob_ref, kv_ref, wide_ref, sems):
    @pl.when(pl.program_id(0) == 0)
    def _():
        copies = [
            pltpu.make_async_copy(part, kv_ref.at[t], sems.at[t])
            for t, part in enumerate((kv0, kv1, kv2, kv3))
        ]
        for copy in copies:
            copy.start()
        for copy in copies:
            copy.wait()

    count = q_ref.shape[0]
    ids, slots, scores = [], [], []
    for u in range(count):
        cluster = SITE * (count * pl.program_id(0) + u) + site_ref[0]
        number = cnt_ref[cluster]
        q = q_ref[u]
        zero = jnp.zeros_like(q)
        both = jnp.concatenate(
            [jnp.concatenate([q, zero], axis=1), jnp.concatenate([zero, q], axis=1)], axis=0
        )
        at = [blk_ref[MAXB * cluster + j] for j in range(MAXB)]
        ids.append([i // SITE for i in at])
        slots.append([(i % SITE) ^ site_ref[0] for i in at])
        mine = []
        for j in range(MAXB):
            keys = kv_ref[slots[u][j], ids[u][j], 0:64, :]
            s = jnp.dot(keys, both, preferred_element_type=F32)
            mine.append(s if j == 0 else jnp.where(j < number, s, -1e30))
        scores.append(jnp.concatenate(mine, axis=0))
    for u in range(count):
        s = scores[u]
        top = jnp.max(s, axis=0, keepdims=True)
        top = jnp.maximum(top[:, :CSIZE], top[:, CSIZE:])
        e = jnp.exp2((s - jnp.concatenate([top, top], axis=1)) * (HD**-0.5 * math.log2(math.e)))
        total = jnp.sum(e, axis=0, keepdims=True)
        inv = 1.0 / (total[:, :CSIZE] + total[:, CSIZE:])
        p = (e * jnp.concatenate([inv, inv], axis=1)).astype(BF)
        halves = [p[i * 64 : (i + 1) * 64, h : h + CSIZE] for i in range(MAXB) for h in (0, CSIZE)]
        for j in range(MAXB):
            prob_ref[u, j] = jnp.concatenate(halves[2 * j : 2 * j + 2], axis=0)
        vals = jnp.concatenate([kv_ref[slots[u][j], ids[u][j], 64:128, :] for j in range(MAXB)], axis=1)
        att = jnp.dot(vals, jnp.concatenate(halves, axis=0), preferred_element_type=F32)
        wide_ref[u * HD : (u + 1) * HD, :] = att
    split = att_ref.shape[0]
    for p in range(split):
        att_ref[p] = wide_ref[pl.ds(p, att_ref.shape[1], stride=split), :].astype(BF)


def forward(site, blk, cnt, recv, kvs, split):
    n = recv.shape[0]
    return pl.pallas_call(
        forward_kernel,
        grid_spec=pltpu.PrefetchScalarGridSpec(
            num_scalar_prefetch=3,
            grid=(n // ROWS,),
            in_specs=[
                pl.BlockSpec((ROWS, 64, CSIZE), lambda i, *_: (i, 2, 0)),
            ]
            + [pl.BlockSpec(memory_space=pl.ANY)] * SITE,
            out_specs=[
                pl.BlockSpec((split, ROWS * HD // split, CSIZE), lambda i, *_: (0, i, 0)),
                pl.BlockSpec((ROWS, MAXB, CSIZE, CSIZE), lambda i, *_: (i, 0, 0, 0)),
            ],
            scratch_shapes=[
                pltpu.VMEM((SITE,) + kvs[0].shape, BF),
                pltpu.VMEM((ROWS * HD, CSIZE), F32),
                pltpu.SemaphoreType.DMA((SITE,)),
            ],
        ),
        out_shape=[
            jax.ShapeDtypeStruct((split, n * HD // split, CSIZE), BF),
            jax.ShapeDtypeStruct((n, MAXB, CSIZE, CSIZE), BF),
        ],
        compiler_params=params(60),
        cost_estimate=pl.CostEstimate(
            flops=n * 4 * MAXB * CSIZE * CSIZE * HD, bytes_accessed=5 << 20, transcendentals=n * MAXB * CSIZE * CSIZE
        ),
        name="attend",
    )(site, blk, cnt, recv, *kvs)


def backward_kernel(site_ref, blk_ref, g_ref, prob_ref, keep_ref, swap_ref, acc_ref):
    step = pl.program_id(0)

    @pl.when(step == 0)
    def _():
        acc_ref[...] = jnp.zeros_like(acc_ref)

    count = g_ref.shape[0]
    for u in range(count):
        cluster = SITE * (count * step + u) + site_ref[0]
        terms = [
            lax.dot_general(g_ref[u], prob_ref[u, j], (((1,), (1,)), ((), ())), preferred_element_type=F32)
            for j in range(MAXB)
        ]
        for j in range(MAXB):
            acc_ref[blk_ref[MAXB * cluster + j]] += terms[j]

    @pl.when(step == pl.num_programs(0) - 1)
    def _():
        core = site_ref[0] % 2
        for t in range(2):
            rows = pl.ds(pl.multiple_of(HALF * ((site_ref[0] // 2) ^ t), HALF), HALF)
            for k in range(keep_ref.shape[1]):
                keep_ref[t, k] = acc_ref[2 * k + core, rows, :].astype(BF)
                swap_ref[t, k] = acc_ref[2 * k + 1 - core, rows, :].astype(BF)


def backward(site, blk, recv, probs):
    n = recv.shape[0]
    clusters = SITE * n
    return pl.pallas_call(
        backward_kernel,
        grid_spec=pltpu.PrefetchScalarGridSpec(
            num_scalar_prefetch=2,
            grid=(n // BROWS,),
            in_specs=[
                pl.BlockSpec((BROWS, 64, CSIZE), lambda i, *_: (i, 3, 0)),
                pl.BlockSpec((BROWS, MAXB, CSIZE, CSIZE), lambda i, *_: (i, 0, 0, 0)),
            ],
            out_specs=[pl.BlockSpec((2, clusters // 2, HALF, CSIZE), lambda i, *_: (0, 0, 0, 0))] * 2,
            scratch_shapes=[pltpu.VMEM((clusters, HD, CSIZE), F32)],
        ),
        out_shape=[jax.ShapeDtypeStruct((2, clusters // 2, HALF, CSIZE), BF)] * 2,
        compiler_params=params(60),
        cost_estimate=pl.CostEstimate(
            flops=n * 2 * MAXB * CSIZE * CSIZE * HD, bytes_accessed=3 << 20, transcendentals=0
        ),
        name="value_contrib",
    )(site, blk, recv, probs)


def merge_kernel(own_ref, other_ref, part_ref, more_ref, out_ref):
    value = own_ref[...].astype(F32) + other_ref[...].astype(F32)
    out_ref[...] = jnp.concatenate([value, part_ref[...] + more_ref[...]], axis=1).astype(BF)


def merge(own, other, part, more):
    n, rows, nodes = own.shape
    return pl.pallas_call(
        merge_kernel,
        out_shape=jax.ShapeDtypeStruct((n, rows + part.shape[1], nodes), BF),
        compiler_params=params(),
        cost_estimate=pl.CostEstimate(flops=own.size, bytes_accessed=6 * own.size + 10 * part.size, transcendentals=0),
        name="merge",
    )(own, other, part, more)


def weight_kernel(me_ref, site_ref, att_ref, *refs):
    n = att_ref.shape[0]
    cots, (keep_ref, swap_ref, cot_ref, acc_ref, wide_ref, sems) = refs[:n], refs[n:]
    copies = [pltpu.make_async_copy(cots[t], cot_ref.at[t], sems.at[t]) for t in range(n)]
    for copy in copies:
        copy.start()
    step = min(2, n)
    for t in range(0, n, step):
        for i in range(step):
            copies[t + i].wait()
        att = jnp.concatenate([att_ref[me_ref[0] ^ (t + i)] for i in range(step)], axis=1)
        cot = jnp.concatenate([cot_ref[t + i] for i in range(step)], axis=0)
        term = jnp.dot(att, cot, preferred_element_type=F32)
        acc_ref[...] = term if t == 0 else acc_ref[...] + term
    for i in range(wide_ref.shape[1]):
        wide_ref[:, i, :] = acc_ref[:, CSIZE * i : CSIZE * (i + 1)]
    core = site_ref[0] % 2
    half, piece, _ = keep_ref.shape
    rows = wide_ref.shape[0] // half // 2
    for k in range(half):
        for to_ref, parity in ((keep_ref, core), (swap_ref, 1 - core)):
            to_ref[k] = wide_ref[pl.ds((2 * k + parity) * rows, rows)].reshape(piece, CSIZE)


def weight_part(me, site, att, cots, targets):
    n, rows, nodes = att.shape
    width = cots[0].shape[1]
    piece = (targets // 2, rows * width // CSIZE // targets, CSIZE)
    return pl.pallas_call(
        weight_kernel,
        grid_spec=pltpu.PrefetchScalarGridSpec(
            num_scalar_prefetch=2,
            grid=(1,),
            in_specs=[pl.BlockSpec(att.shape, lambda i, *_: (0, 0, 0))]
            + [pl.BlockSpec(memory_space=pl.ANY)] * n,
            out_specs=[pl.BlockSpec(piece, lambda i, *_: (0, 0, 0))] * 2,
            scratch_shapes=[
                pltpu.VMEM((n, nodes, width), BF),
                pltpu.VMEM((rows, width), F32),
                pltpu.VMEM((rows, width // CSIZE, CSIZE), F32),
                pltpu.SemaphoreType.DMA((n,)),
            ],
        ),
        out_shape=[jax.ShapeDtypeStruct(piece, F32)] * 2,
        compiler_params=params(60),
        cost_estimate=pl.CostEstimate(
            flops=2 * n * rows * nodes * width, bytes_accessed=2 * n * nodes * width, transcendentals=0
        ),
        name="weight_part",
    )(me, site, att, *cots)


def gather_kernel(back_ref, att_ref, out_ref):
    n, rows, _ = att_ref.shape
    total = jnp.sum(back_ref[...].astype(F32), axis=0)[HALF:]
    high = total.astype(BF).astype(F32)
    both = jnp.concatenate([high, total - high], axis=0).astype(BF)
    for p in range(n):
        out_ref[p, :rows, :] = att_ref[p]
        out_ref[p, rows:, :] = both


def gather_send(back, att):
    n, rows, nodes = att.shape
    more = 2 * (back.shape[1] - HALF)
    return pl.pallas_call(
        gather_kernel,
        out_shape=jax.ShapeDtypeStruct((n, rows + more, nodes), BF),
        compiler_params=params(),
        cost_estimate=pl.CostEstimate(flops=back.size, bytes_accessed=2 * back.size + 4 * att.size, transcendentals=0),
        name="gather_send",
    )(back, att)


def finish_kernel(got_ref, w_ref, layer_ref, weight_ref, wide_ref, rows_ref):
    n, total, nodes = got_ref.shape
    rows = w_ref.shape[0] // n
    more = (total - rows) // 2
    for p in range(n):
        wide_ref[pl.ds(p, rows, stride=n), :] = got_ref[p, :rows, :].astype(F32)
        both = got_ref[p, rows:, :].astype(F32)
        rows_ref[p * more : (p + 1) * more, :] = both[:more] + both[more:]
    layer_ref[...] = jnp.dot(
        wide_ref[...].T.astype(BF), w_ref[...], preferred_element_type=F32
    ).astype(BF)
    pieces = weight_ref.shape[1] // nodes
    for i in range(pieces):
        weight_ref[:, i * nodes : (i + 1) * nodes] = rows_ref[pl.ds(i, weight_ref.shape[0], stride=pieces), :]


def finish(got, w_out, own):
    nodes = got.shape[2]
    width = w_out.shape[0]
    more = (got.shape[1] - width // got.shape[0]) // 2
    return pl.pallas_call(
        finish_kernel,
        out_shape=[
            jax.ShapeDtypeStruct((nodes, width), BF),
            jax.ShapeDtypeStruct((own, width), F32),
        ],
        scratch_shapes=[pltpu.VMEM((width, nodes), F32), pltpu.VMEM((got.shape[0] * more, nodes), F32)],
        compiler_params=params(),
        cost_estimate=pl.CostEstimate(flops=2 * nodes * width * width, bytes_accessed=2 * width * width, transcendentals=0),
        name="finish",
    )(got, w_out)


def flip_kernel(x_ref, out_ref):
    out_ref[...] = x_ref[...].T


def flip(x):
    rows, cols = x.shape
    return pl.pallas_call(
        flip_kernel,
        out_shape=jax.ShapeDtypeStruct((cols, rows), x.dtype),
        compiler_params=params(),
        cost_estimate=pl.CostEstimate(flops=0, bytes_accessed=4 * rows * cols, transcendentals=0),
        name="flip",
    )(x)


def body(queries, keys, values, cotangent, w_out, blocks, counts):
    nseq = lax.axis_size("seq")
    ndp = lax.axis_size("dp")
    width = w_out.shape[0]
    me = lax.axis_index("dp").astype(jnp.int32)[None]
    site = (lax.axis_index("seq") % SITE).astype(jnp.int32)[None]
    same_site = [[SITE * h + s for h in range(H)] for s in range(SITE)]
    same_core = [list(range(c, nseq, 2)) for c in range(2)]
    same_site_dp = [[p * nseq + i for p in range(ndp) for i in group] for group in same_site]

    def swap(x, bit):
        return lax.ppermute(x, "seq", [(i, i ^ bit) for i in range(nseq)])

    blk = blocks[0].reshape(-1)
    cnt = counts[0]
    cot = cotangent[0]

    sent = pack(queries[0], keys[0], values[0], cot, w_out)
    sent, cot = lax.optimization_barrier((sent, cot))
    cots = [cot] + [lax.ppermute(cot, "dp", [(i, i ^ t) for i in range(ndp)]) for t in range(1, ndp)]
    recv = lax.all_to_all(sent, "seq", split_axis=0, concat_axis=0, tiled=True, axis_index_groups=same_site)
    kv, cots = lax.optimization_barrier((recv[:, :128], cots))
    kv_z = swap(kv, 2)
    kvs = [kv, swap(kv, 1), kv_z, swap(kv_z, 1)]
    att, probs = forward(site, blk, cnt, recv, kvs, ndp)
    sent_att = att.reshape(ndp * H, HD // ndp, CSIZE)
    pieces = lax.all_to_all(
        sent_att, ("dp", "seq"), split_axis=0, concat_axis=0, tiled=True, axis_index_groups=same_site_dp
    ).reshape(ndp, width // ndp, CSIZE)
    keep, give = backward(site, blk, recv, probs)
    chip = (keep.astype(F32) + swap(give, 1).astype(F32)).astype(BF)
    pieces, _ = lax.optimization_barrier((pieces, chip))
    part, more = weight_part(me, site, pieces, cots, nseq)
    last = merge(chip[0], swap(chip[1], 2), part, swap(more, 1))
    back = lax.all_to_all(last, "seq", split_axis=0, concat_axis=0, tiled=True, axis_index_groups=same_core)
    got = lax.all_to_all(gather_send(back, pieces), "dp", split_axis=0, concat_axis=0, tiled=True)
    value_grad = flip(back[:, :HALF].reshape(width, CSIZE))
    layer_out, weight_grad = finish(got, w_out, width // nseq)
    return (layer_out[None], value_grad[None], weight_grad)


def solution(mesh):
    return jax.shard_map(
        body,
        mesh=mesh,
        in_specs=(
            P("dp", "seq", None),
            P("dp", "seq", None),
            P("dp", "seq", None),
            P("dp", "seq", None),
            P(),
            P("dp", None, None),
            P("dp", None),
        ),
        out_specs=(P("dp", "seq", None), P("dp", "seq", None), P("seq", None)),
        check_vma=False,
    )
```

```python
import math

import jax
import jax.numpy as jnp
from jax import lax
from jax.experimental import pallas as pl
from jax.experimental.pallas import tpu as pltpu
from jax.sharding import PartitionSpec as P

H = 16
HD = 64
CSIZE = 128
HALF = HD // 2
MAXB = 4
SITE = 4
ROWS = 8
PAIR = 8
BROWS = 8
BF = jnp.bfloat16
F32 = jnp.float32


def params(mib=40):
    return pltpu.CompilerParams(vmem_limit_bytes=mib * 1024 * 1024)


def pack_kernel(q_ref, k_ref, v_ref, c_ref, w_ref, out_ref, ct_ref):
    @pl.when(pl.program_id(0) == 0)
    def _():
        ct_ref[...] = c_ref[...].T

    keys = k_ref[...]
    vals = v_ref[...].T
    qrys = q_ref[...].T
    grad = jnp.dot(w_ref[...], ct_ref[...], preferred_element_type=F32).astype(BF)
    for i in range(PAIR):
        part = keys[:, i * HD : (i + 1) * HD]
        out_ref[i, 0:64, :] = jnp.concatenate([part[:64], part[64:]], axis=1)
        out_ref[i, 64:128, :] = vals[i * HD : (i + 1) * HD]
        out_ref[i, 128:192, :] = qrys[i * HD : (i + 1) * HD]
        out_ref[i, 192:256, :] = grad[i * HD : (i + 1) * HD]


def pack(q, k, v, cot, w_out):
    rows, width = q.shape
    pair = pl.BlockSpec((rows, PAIR * HD), lambda i: (0, i))
    return pl.pallas_call(
        pack_kernel,
        grid=(H // PAIR,),
        in_specs=[
            pair,
            pair,
            pair,
            pl.BlockSpec((rows, width), lambda i: (0, 0)),
            pl.BlockSpec((PAIR * HD, width), lambda i: (i, 0)),
        ],
        out_specs=pl.BlockSpec((PAIR, 256, CSIZE), lambda i: (i, 0, 0)),
        scratch_shapes=[pltpu.VMEM((width, rows), BF)],
        out_shape=jax.ShapeDtypeStruct((H, 256, CSIZE), BF),
        compiler_params=params(60),
        cost_estimate=pl.CostEstimate(
            flops=2 * rows * width * width, bytes_accessed=2 * width * width + 10 * rows * width, transcendentals=0
        ),
        name="pack",
    )(q, k, v, cot, w_out)


def forward_kernel(site_ref, blk_ref, cnt_ref, q_ref, kv0, kv1, kv2, kv3, att_ref, prob_ref, kv_ref, wide_ref, sems):
    @pl.when(pl.program_id(0) == 0)
    def _():
        copies = [
            pltpu.make_async_copy(part, kv_ref.at[t], sems.at[t])
            for t, part in enumerate((kv0, kv1, kv2, kv3))
        ]
        for copy in copies:
            copy.start()
        for copy in copies:
            copy.wait()

    count = q_ref.shape[0]
    ids, slots, scores = [], [], []
    for u in range(count):
        cluster = SITE * (count * pl.program_id(0) + u) + site_ref[0]
        number = cnt_ref[cluster]
        q = q_ref[u]
        zero = jnp.zeros_like(q)
        both = jnp.concatenate(
            [jnp.concatenate([q, zero], axis=1), jnp.concatenate([zero, q], axis=1)], axis=0
        )
        at = [blk_ref[MAXB * cluster + j] for j in range(MAXB)]
        ids.append([i // SITE for i in at])
        slots.append([(i % SITE) ^ site_ref[0] for i in at])
        mine = []
        for j in range(MAXB):
            keys = kv_ref[slots[u][j], ids[u][j], 0:64, :]
            s = jnp.dot(keys, both, preferred_element_type=F32)
            mine.append(s if j == 0 else jnp.where(j < number, s, -1e30))
        scores.append(jnp.concatenate(mine, axis=0))
    for u in range(count):
        s = scores[u]
        top = jnp.max(s, axis=0, keepdims=True)
        top = jnp.maximum(top[:, :CSIZE], top[:, CSIZE:])
        e = jnp.exp2((s - jnp.concatenate([top, top], axis=1)) * (HD**-0.5 * math.log2(math.e)))
        total = jnp.sum(e, axis=0, keepdims=True)
        inv = 1.0 / (total[:, :CSIZE] + total[:, CSIZE:])
        p = (e * jnp.concatenate([inv, inv], axis=1)).astype(BF)
        halves = [p[i * 64 : (i + 1) * 64, h : h + CSIZE] for i in range(MAXB) for h in (0, CSIZE)]
        for j in range(MAXB):
            prob_ref[u, j] = jnp.concatenate(halves[2 * j : 2 * j + 2], axis=0)
        vals = jnp.concatenate([kv_ref[slots[u][j], ids[u][j], 64:128, :] for j in range(MAXB)], axis=1)
        att = jnp.dot(vals, jnp.concatenate(halves, axis=0), preferred_element_type=F32)
        wide_ref[u * HD : (u + 1) * HD, :] = att
    split = att_ref.shape[0]
    for p in range(split):
        att_ref[p] = wide_ref[pl.ds(p, att_ref.shape[1], stride=split), :].astype(BF)


def forward(site, blk, cnt, recv, kvs, split):
    n = recv.shape[0]
    return pl.pallas_call(
        forward_kernel,
        grid_spec=pltpu.PrefetchScalarGridSpec(
            num_scalar_prefetch=3,
            grid=(n // ROWS,),
            in_specs=[
                pl.BlockSpec((ROWS, 64, CSIZE), lambda i, *_: (i, 2, 0)),
            ]
            + [pl.BlockSpec(memory_space=pl.ANY)] * SITE,
            out_specs=[
                pl.BlockSpec((split, ROWS * HD // split, CSIZE), lambda i, *_: (0, i, 0)),
                pl.BlockSpec((ROWS, MAXB, CSIZE, CSIZE), lambda i, *_: (i, 0, 0, 0)),
            ],
            scratch_shapes=[
                pltpu.VMEM((SITE,) + kvs[0].shape, BF),
                pltpu.VMEM((ROWS * HD, CSIZE), F32),
                pltpu.SemaphoreType.DMA((SITE,)),
            ],
        ),
        out_shape=[
            jax.ShapeDtypeStruct((split, n * HD // split, CSIZE), BF),
            jax.ShapeDtypeStruct((n, MAXB, CSIZE, CSIZE), BF),
        ],
        compiler_params=params(60),
        cost_estimate=pl.CostEstimate(
            flops=n * 4 * MAXB * CSIZE * CSIZE * HD, bytes_accessed=5 << 20, transcendentals=n * MAXB * CSIZE * CSIZE
        ),
        name="attend",
    )(site, blk, cnt, recv, *kvs)


def backward_kernel(site_ref, blk_ref, g_ref, prob_ref, keep_ref, swap_ref, acc_ref):
    step = pl.program_id(0)

    @pl.when(step == 0)
    def _():
        acc_ref[...] = jnp.zeros_like(acc_ref)

    count = g_ref.shape[0]
    for u in range(count):
        cluster = SITE * (count * step + u) + site_ref[0]
        terms = [
            lax.dot_general(g_ref[u], prob_ref[u, j], (((1,), (1,)), ((), ())), preferred_element_type=F32)
            for j in range(MAXB)
        ]
        for j in range(MAXB):
            acc_ref[blk_ref[MAXB * cluster + j]] += terms[j]

    @pl.when(step == pl.num_programs(0) - 1)
    def _():
        core = site_ref[0] % 2
        for t in range(2):
            rows = pl.ds(pl.multiple_of(HALF * ((site_ref[0] // 2) ^ t), HALF), HALF)
            for k in range(keep_ref.shape[1]):
                keep_ref[t, k] = acc_ref[2 * k + core, rows, :].astype(BF)
                swap_ref[t, k] = acc_ref[2 * k + 1 - core, rows, :].astype(BF)


def backward(site, blk, recv, probs):
    n = recv.shape[0]
    clusters = SITE * n
    return pl.pallas_call(
        backward_kernel,
        grid_spec=pltpu.PrefetchScalarGridSpec(
            num_scalar_prefetch=2,
            grid=(n // BROWS,),
            in_specs=[
                pl.BlockSpec((BROWS, 64, CSIZE), lambda i, *_: (i, 3, 0)),
                pl.BlockSpec((BROWS, MAXB, CSIZE, CSIZE), lambda i, *_: (i, 0, 0, 0)),
            ],
            out_specs=[pl.BlockSpec((2, clusters // 2, HALF, CSIZE), lambda i, *_: (0, 0, 0, 0))] * 2,
            scratch_shapes=[pltpu.VMEM((clusters, HD, CSIZE), F32)],
        ),
        out_shape=[jax.ShapeDtypeStruct((2, clusters // 2, HALF, CSIZE), BF)] * 2,
        compiler_params=params(60),
        cost_estimate=pl.CostEstimate(
            flops=n * 2 * MAXB * CSIZE * CSIZE * HD, bytes_accessed=3 << 20, transcendentals=0
        ),
        name="value_contrib",
    )(site, blk, recv, probs)


def merge_kernel(own_ref, other_ref, part_ref, more_ref, out_ref):
    value = own_ref[...].astype(F32) + other_ref[...].astype(F32)
    out_ref[...] = jnp.concatenate([value, part_ref[...] + more_ref[...]], axis=1).astype(BF)


def merge(own, other, part, more):
    n, rows, nodes = own.shape
    return pl.pallas_call(
        merge_kernel,
        out_shape=jax.ShapeDtypeStruct((n, rows + part.shape[1], nodes), BF),
        compiler_params=params(),
        cost_estimate=pl.CostEstimate(flops=own.size, bytes_accessed=6 * own.size + 10 * part.size, transcendentals=0),
        name="merge",
    )(own, other, part, more)


def weight_kernel(me_ref, site_ref, att_ref, *refs):
    cots, (keep_ref, swap_ref, acc_ref, wide_ref) = refs[:-4], refs[-4:]
    each = att_ref.shape[0] // len(cots)
    for t, cot_ref in enumerate(cots):
        att = jnp.concatenate([att_ref[me_ref[0] ^ (each * t + i)] for i in range(each)], axis=1)
        term = jnp.dot(att, cot_ref[...], preferred_element_type=F32)
        acc_ref[...] = term if t == 0 else acc_ref[...] + term
    for i in range(wide_ref.shape[1]):
        wide_ref[:, i, :] = acc_ref[:, CSIZE * i : CSIZE * (i + 1)]
    core = site_ref[0] % 2
    half, piece, _ = keep_ref.shape
    rows = wide_ref.shape[0] // half // 2
    for k in range(half):
        for to_ref, parity in ((keep_ref, core), (swap_ref, 1 - core)):
            to_ref[k] = wide_ref[pl.ds((2 * k + parity) * rows, rows)].reshape(piece, CSIZE)


def weight_part(me, site, att, cots, targets):
    n, rows, nodes = att.shape
    width = cots[0].shape[1]
    piece = (targets // 2, rows * width // CSIZE // targets, CSIZE)
    return pl.pallas_call(
        weight_kernel,
        in_specs=[pl.BlockSpec(memory_space=pltpu.SMEM)] * 2 + [pl.BlockSpec(memory_space=pltpu.VMEM)] * (1 + len(cots)),
        out_shape=[jax.ShapeDtypeStruct(piece, F32)] * 2,
        scratch_shapes=[pltpu.VMEM((rows, width), F32), pltpu.VMEM((rows, width // CSIZE, CSIZE), F32)],
        compiler_params=params(16),
        cost_estimate=pl.CostEstimate(
            flops=2 * n * rows * nodes * width, bytes_accessed=2 * n * nodes * width, transcendentals=0
        ),
        name="weight_part",
    )(me, site, att, *cots)


def gather_kernel(back_ref, att_ref, out_ref):
    n, rows, _ = att_ref.shape
    total = jnp.sum(back_ref[...].astype(F32), axis=0)[HALF:]
    high = total.astype(BF).astype(F32)
    both = jnp.concatenate([high, total - high], axis=0).astype(BF)
    for p in range(n):
        out_ref[p, :rows, :] = att_ref[p]
        out_ref[p, rows:, :] = both


def gather_send(back, att):
    n, rows, nodes = att.shape
    more = 2 * (back.shape[1] - HALF)
    return pl.pallas_call(
        gather_kernel,
        out_shape=jax.ShapeDtypeStruct((n, rows + more, nodes), BF),
        compiler_params=params(),
        cost_estimate=pl.CostEstimate(flops=back.size, bytes_accessed=2 * back.size + 4 * att.size, transcendentals=0),
        name="gather_send",
    )(back, att)


def finish_kernel(got_ref, w_ref, layer_ref, weight_ref, wide_ref, rows_ref):
    n, total, nodes = got_ref.shape
    rows = w_ref.shape[0] // n
    more = (total - rows) // 2
    for p in range(n):
        wide_ref[pl.ds(p, rows, stride=n), :] = got_ref[p, :rows, :].astype(F32)
        both = got_ref[p, rows:, :].astype(F32)
        rows_ref[p * more : (p + 1) * more, :] = both[:more] + both[more:]
    layer_ref[...] = jnp.dot(
        wide_ref[...].T.astype(BF), w_ref[...], preferred_element_type=F32
    ).astype(BF)
    pieces = weight_ref.shape[1] // nodes
    for i in range(pieces):
        weight_ref[:, i * nodes : (i + 1) * nodes] = rows_ref[pl.ds(i, weight_ref.shape[0], stride=pieces), :]


def finish(got, w_out, own):
    nodes = got.shape[2]
    width = w_out.shape[0]
    more = (got.shape[1] - width // got.shape[0]) // 2
    return pl.pallas_call(
        finish_kernel,
        out_shape=[
            jax.ShapeDtypeStruct((nodes, width), BF),
            jax.ShapeDtypeStruct((own, width), F32),
        ],
        scratch_shapes=[pltpu.VMEM((width, nodes), F32), pltpu.VMEM((got.shape[0] * more, nodes), F32)],
        compiler_params=params(),
        cost_estimate=pl.CostEstimate(flops=2 * nodes * width * width, bytes_accessed=2 * width * width, transcendentals=0),
        name="finish",
    )(got, w_out)


def flip_kernel(x_ref, out_ref):
    out_ref[...] = x_ref[...].T


def flip(x):
    rows, cols = x.shape
    return pl.pallas_call(
        flip_kernel,
        out_shape=jax.ShapeDtypeStruct((cols, rows), x.dtype),
        compiler_params=params(),
        cost_estimate=pl.CostEstimate(flops=0, bytes_accessed=4 * rows * cols, transcendentals=0),
        name="flip",
    )(x)


def body(queries, keys, values, cotangent, w_out, blocks, counts):
    nseq = lax.axis_size("seq")
    ndp = lax.axis_size("dp")
    width = w_out.shape[0]
    me = lax.axis_index("dp").astype(jnp.int32)[None]
    site = (lax.axis_index("seq") % SITE).astype(jnp.int32)[None]
    same_site = [[SITE * h + s for h in range(H)] for s in range(SITE)]
    same_core = [list(range(c, nseq, 2)) for c in range(2)]
    same_site_dp = [[p * nseq + i for p in range(ndp) for i in group] for group in same_site]

    def swap(x, bit):
        return lax.ppermute(x, "seq", [(i, i ^ bit) for i in range(nseq)])

    blk = blocks[0].reshape(-1)
    cnt = counts[0]
    cot = cotangent[0]

    sent = pack(queries[0], keys[0], values[0], cot, w_out)
    sent, cot = lax.optimization_barrier((sent, cot))
    cots = [cot]
    if ndp > 1:
        cot = jnp.concatenate([cot, lax.ppermute(cot, "dp", [(i, i ^ 1) for i in range(ndp)])], axis=0)
        cots = [cot] + [lax.ppermute(cot, "dp", [(i, i ^ t) for i in range(ndp)]) for t in range(2, ndp, 2)]
    recv = lax.all_to_all(sent, "seq", split_axis=0, concat_axis=0, tiled=True, axis_index_groups=same_site)
    kv, cots = lax.optimization_barrier((recv[:, :128], cots))
    kv_z = swap(kv, 2)
    kvs = [kv, swap(kv, 1), kv_z, swap(kv_z, 1)]
    att, probs = forward(site, blk, cnt, recv, kvs, ndp)
    sent_att = att.reshape(ndp * H, HD // ndp, CSIZE)
    pieces = lax.all_to_all(
        sent_att, ("dp", "seq"), split_axis=0, concat_axis=0, tiled=True, axis_index_groups=same_site_dp
    ).reshape(ndp, width // ndp, CSIZE)
    keep, give = backward(site, blk, recv, probs)
    chip = (keep.astype(F32) + swap(give, 1).astype(F32)).astype(BF)
    pieces, _ = lax.optimization_barrier((pieces, chip))
    part, more = weight_part(me, site, pieces, cots, nseq)
    last = merge(chip[0], swap(chip[1], 2), part, swap(more, 1))
    back = lax.all_to_all(last, "seq", split_axis=0, concat_axis=0, tiled=True, axis_index_groups=same_core)
    got = lax.all_to_all(gather_send(back, pieces), "dp", split_axis=0, concat_axis=0, tiled=True)
    value_grad = flip(back[:, :HALF].reshape(width, CSIZE))
    layer_out, weight_grad = finish(got, w_out, width // nseq)
    return (layer_out[None], value_grad[None], weight_grad)


def solution(mesh):
    return jax.shard_map(
        body,
        mesh=mesh,
        in_specs=(
            P("dp", "seq", None),
            P("dp", "seq", None),
            P("dp", "seq", None),
            P("dp", "seq", None),
            P(),
            P("dp", None, None),
            P("dp", None),
        ),
        out_specs=(P("dp", "seq", None), P("dp", "seq", None), P("seq", None)),
        check_vma=False,
    )
```

```python
import math

import jax
import jax.numpy as jnp
from jax import lax
from jax.experimental import pallas as pl
from jax.experimental.pallas import tpu as pltpu
from jax.sharding import PartitionSpec as P

H = 16
HD = 64
CSIZE = 128
HALF = HD // 2
MAXB = 4
SITE = 4
ROWS = 8
PAIR = 8
BROWS = 8
BF = jnp.bfloat16
F32 = jnp.float32


def params(mib=40):
    return pltpu.CompilerParams(vmem_limit_bytes=mib * 1024 * 1024)


def pack_kernel(q_ref, k_ref, v_ref, c_ref, w_ref, out_ref, ct_ref):
    @pl.when(pl.program_id(0) == 0)
    def _():
        ct_ref[...] = c_ref[...].T

    keys = k_ref[...]
    vals = v_ref[...].T
    qrys = q_ref[...].T
    grad = jnp.dot(w_ref[...], ct_ref[...], preferred_element_type=F32).astype(BF)
    for i in range(PAIR):
        part = keys[:, i * HD : (i + 1) * HD]
        out_ref[i, 0:64, :] = jnp.concatenate([part[:64], part[64:]], axis=1)
        out_ref[i, 64:128, :] = vals[i * HD : (i + 1) * HD]
        out_ref[i, 128:192, :] = qrys[i * HD : (i + 1) * HD]
        out_ref[i, 192:256, :] = grad[i * HD : (i + 1) * HD]


def pack(q, k, v, cot, w_out):
    rows, width = q.shape
    pair = pl.BlockSpec((rows, PAIR * HD), lambda i: (0, i))
    return pl.pallas_call(
        pack_kernel,
        grid=(H // PAIR,),
        in_specs=[
            pair,
            pair,
            pair,
            pl.BlockSpec((rows, width), lambda i: (0, 0)),
            pl.BlockSpec((PAIR * HD, width), lambda i: (i, 0)),
        ],
        out_specs=pl.BlockSpec((PAIR, 256, CSIZE), lambda i: (i, 0, 0)),
        scratch_shapes=[pltpu.VMEM((width, rows), BF)],
        out_shape=jax.ShapeDtypeStruct((H, 256, CSIZE), BF),
        compiler_params=params(60),
        cost_estimate=pl.CostEstimate(
            flops=2 * rows * width * width, bytes_accessed=2 * width * width + 10 * rows * width, transcendentals=0
        ),
        name="pack",
    )(q, k, v, cot, w_out)


def forward_kernel(site_ref, blk_ref, cnt_ref, q_ref, kv0, kv1, kv2, kv3, att_ref, prob_ref, kv_ref, wide_ref, sems):
    @pl.when(pl.program_id(0) == 0)
    def _():
        copies = [
            pltpu.make_async_copy(part, kv_ref.at[t], sems.at[t])
            for t, part in enumerate((kv0, kv1, kv2, kv3))
        ]
        for copy in copies:
            copy.start()
        for copy in copies:
            copy.wait()

    count = q_ref.shape[0]
    ids, slots, scores = [], [], []
    for u in range(count):
        cluster = SITE * (count * pl.program_id(0) + u) + site_ref[0]
        number = cnt_ref[cluster]
        q = q_ref[u]
        zero = jnp.zeros_like(q)
        both = jnp.concatenate(
            [jnp.concatenate([q, zero], axis=1), jnp.concatenate([zero, q], axis=1)], axis=0
        )
        at = [blk_ref[MAXB * cluster + j] for j in range(MAXB)]
        ids.append([i // SITE for i in at])
        slots.append([(i % SITE) ^ site_ref[0] for i in at])
        mine = []
        for j in range(MAXB):
            keys = kv_ref[slots[u][j], ids[u][j], 0:64, :]
            s = jnp.dot(keys, both, preferred_element_type=F32)
            mine.append(s if j == 0 else jnp.where(j < number, s, -1e30))
        scores.append(jnp.concatenate(mine, axis=0))
    for u in range(count):
        s = scores[u]
        top = jnp.max(s, axis=0, keepdims=True)
        top = jnp.maximum(top[:, :CSIZE], top[:, CSIZE:])
        e = jnp.exp2((s - jnp.concatenate([top, top], axis=1)) * (HD**-0.5 * math.log2(math.e)))
        total = jnp.sum(e, axis=0, keepdims=True)
        inv = 1.0 / (total[:, :CSIZE] + total[:, CSIZE:])
        p = (e * jnp.concatenate([inv, inv], axis=1)).astype(BF)
        halves = [p[i * 64 : (i + 1) * 64, h : h + CSIZE] for i in range(MAXB) for h in (0, CSIZE)]
        for j in range(MAXB):
            prob_ref[u, j] = jnp.concatenate(halves[2 * j : 2 * j + 2], axis=0)
        vals = jnp.concatenate([kv_ref[slots[u][j], ids[u][j], 64:128, :] for j in range(MAXB)], axis=1)
        att = jnp.dot(vals, jnp.concatenate(halves, axis=0), preferred_element_type=F32)
        wide_ref[u * HD : (u + 1) * HD, :] = att
    split = att_ref.shape[0]
    for p in range(split):
        att_ref[p] = wide_ref[pl.ds(p, att_ref.shape[1], stride=split), :].astype(BF)


def forward(site, blk, cnt, recv, kvs, split):
    n = recv.shape[0]
    return pl.pallas_call(
        forward_kernel,
        grid_spec=pltpu.PrefetchScalarGridSpec(
            num_scalar_prefetch=3,
            grid=(n // ROWS,),
            in_specs=[
                pl.BlockSpec((ROWS, 64, CSIZE), lambda i, *_: (i, 2, 0)),
            ]
            + [pl.BlockSpec(memory_space=pl.ANY)] * SITE,
            out_specs=[
                pl.BlockSpec((split, ROWS * HD // split, CSIZE), lambda i, *_: (0, i, 0)),
                pl.BlockSpec((ROWS, MAXB, CSIZE, CSIZE), lambda i, *_: (i, 0, 0, 0)),
            ],
            scratch_shapes=[
                pltpu.VMEM((SITE,) + kvs[0].shape, BF),
                pltpu.VMEM((ROWS * HD, CSIZE), F32),
                pltpu.SemaphoreType.DMA((SITE,)),
            ],
        ),
        out_shape=[
            pltpu.HBM((split, n * HD // split, CSIZE), BF),
            pltpu.HBM((n, MAXB, CSIZE, CSIZE), BF),
        ],
        compiler_params=params(24),
        cost_estimate=pl.CostEstimate(
            flops=n * 4 * MAXB * CSIZE * CSIZE * HD, bytes_accessed=5 << 20, transcendentals=n * MAXB * CSIZE * CSIZE
        ),
        name="attend",
    )(site, blk, cnt, recv, *kvs)


def backward_kernel(site_ref, blk_ref, g_ref, prob_ref, keep_ref, swap_ref, acc_ref):
    step = pl.program_id(0)

    @pl.when(step == 0)
    def _():
        acc_ref[...] = jnp.zeros_like(acc_ref)

    count = g_ref.shape[0]
    for u in range(count):
        cluster = SITE * (count * step + u) + site_ref[0]
        terms = [
            lax.dot_general(g_ref[u], prob_ref[u, j], (((1,), (1,)), ((), ())), preferred_element_type=F32)
            for j in range(MAXB)
        ]
        for j in range(MAXB):
            acc_ref[blk_ref[MAXB * cluster + j]] += terms[j]

    @pl.when(step == pl.num_programs(0) - 1)
    def _():
        core = site_ref[0] % 2
        for t in range(2):
            rows = pl.ds(pl.multiple_of(HALF * ((site_ref[0] // 2) ^ t), HALF), HALF)
            for k in range(keep_ref.shape[1]):
                keep_ref[t, k] = acc_ref[2 * k + core, rows, :].astype(BF)
                swap_ref[t, k] = acc_ref[2 * k + 1 - core, rows, :].astype(BF)


def backward(site, blk, recv, probs):
    n = recv.shape[0]
    clusters = SITE * n
    return pl.pallas_call(
        backward_kernel,
        grid_spec=pltpu.PrefetchScalarGridSpec(
            num_scalar_prefetch=2,
            grid=(n // BROWS,),
            in_specs=[
                pl.BlockSpec((BROWS, 64, CSIZE), lambda i, *_: (i, 3, 0)),
                pl.BlockSpec((BROWS, MAXB, CSIZE, CSIZE), lambda i, *_: (i, 0, 0, 0)),
            ],
            out_specs=[pl.BlockSpec((2, clusters // 2, HALF, CSIZE), lambda i, *_: (0, 0, 0, 0))] * 2,
            scratch_shapes=[pltpu.VMEM((clusters, HD, CSIZE), F32)],
        ),
        out_shape=[jax.ShapeDtypeStruct((2, clusters // 2, HALF, CSIZE), BF)] * 2,
        compiler_params=params(24),
        cost_estimate=pl.CostEstimate(
            flops=n * 2 * MAXB * CSIZE * CSIZE * HD, bytes_accessed=3 << 20, transcendentals=0
        ),
        name="value_contrib",
    )(site, blk, recv, probs)


def merge_kernel(own_ref, other_ref, part_ref, more_ref, out_ref):
    value = own_ref[...].astype(F32) + other_ref[...].astype(F32)
    out_ref[...] = jnp.concatenate([value, part_ref[...] + more_ref[...]], axis=1).astype(BF)


def merge(own, other, part, more):
    n, rows, nodes = own.shape
    return pl.pallas_call(
        merge_kernel,
        out_shape=jax.ShapeDtypeStruct((n, rows + part.shape[1], nodes), BF),
        compiler_params=params(),
        cost_estimate=pl.CostEstimate(flops=own.size, bytes_accessed=6 * own.size + 10 * part.size, transcendentals=0),
        name="merge",
    )(own, other, part, more)


def weight_kernel(me_ref, site_ref, att_ref, *refs):
    cots, (keep_ref, swap_ref, acc_ref, wide_ref) = refs[:-4], refs[-4:]
    each = att_ref.shape[0] // len(cots)
    for t, cot_ref in enumerate(cots):
        att = jnp.concatenate([att_ref[me_ref[0] ^ (each * t + i)] for i in range(each)], axis=1)
        term = jnp.dot(att, cot_ref[...], preferred_element_type=F32)
        acc_ref[...] = term if t == 0 else acc_ref[...] + term
    for i in range(wide_ref.shape[1]):
        wide_ref[:, i, :] = acc_ref[:, CSIZE * i : CSIZE * (i + 1)]
    core = site_ref[0] % 2
    half, piece, _ = keep_ref.shape
    rows = wide_ref.shape[0] // half // 2
    for k in range(half):
        for to_ref, parity in ((keep_ref, core), (swap_ref, 1 - core)):
            to_ref[k] = wide_ref[pl.ds((2 * k + parity) * rows, rows)].reshape(piece, CSIZE)


def weight_part(me, site, att, cots, targets):
    n, rows, nodes = att.shape
    width = cots[0].shape[1]
    piece = (targets // 2, rows * width // CSIZE // targets, CSIZE)
    return pl.pallas_call(
        weight_kernel,
        in_specs=[pl.BlockSpec(memory_space=pltpu.SMEM)] * 2 + [pl.BlockSpec(memory_space=pltpu.VMEM)] * (1 + len(cots)),
        out_shape=[jax.ShapeDtypeStruct(piece, F32)] * 2,
        scratch_shapes=[pltpu.VMEM((rows, width), F32), pltpu.VMEM((rows, width // CSIZE, CSIZE), F32)],
        compiler_params=params(16),
        cost_estimate=pl.CostEstimate(
            flops=2 * n * rows * nodes * width, bytes_accessed=2 * n * nodes * width, transcendentals=0
        ),
        name="weight_part",
    )(me, site, att, *cots)


def gather_kernel(back_ref, att_ref, out_ref):
    n, rows, _ = att_ref.shape
    total = jnp.sum(back_ref[...].astype(F32), axis=0)[HALF:]
    high = total.astype(BF).astype(F32)
    both = jnp.concatenate([high, total - high], axis=0).astype(BF)
    for p in range(n):
        out_ref[p, :rows, :] = att_ref[p]
        out_ref[p, rows:, :] = both


def gather_send(back, att):
    n, rows, nodes = att.shape
    more = 2 * (back.shape[1] - HALF)
    return pl.pallas_call(
        gather_kernel,
        out_shape=jax.ShapeDtypeStruct((n, rows + more, nodes), BF),
        compiler_params=params(),
        cost_estimate=pl.CostEstimate(flops=back.size, bytes_accessed=2 * back.size + 4 * att.size, transcendentals=0),
        name="gather_send",
    )(back, att)


def finish_kernel(got_ref, w_ref, layer_ref, weight_ref, wide_ref, rows_ref):
    n, total, nodes = got_ref.shape
    rows = w_ref.shape[0] // n
    more = (total - rows) // 2
    for p in range(n):
        wide_ref[pl.ds(p, rows, stride=n), :] = got_ref[p, :rows, :].astype(F32)
        both = got_ref[p, rows:, :].astype(F32)
        rows_ref[p * more : (p + 1) * more, :] = both[:more] + both[more:]
    layer_ref[...] = jnp.dot(
        wide_ref[...].T.astype(BF), w_ref[...], preferred_element_type=F32
    ).astype(BF)
    pieces = weight_ref.shape[1] // nodes
    for i in range(pieces):
        weight_ref[:, i * nodes : (i + 1) * nodes] = rows_ref[pl.ds(i, weight_ref.shape[0], stride=pieces), :]


def finish(got, w_out, own):
    nodes = got.shape[2]
    width = w_out.shape[0]
    more = (got.shape[1] - width // got.shape[0]) // 2
    return pl.pallas_call(
        finish_kernel,
        out_shape=[
            jax.ShapeDtypeStruct((nodes, width), BF),
            jax.ShapeDtypeStruct((own, width), F32),
        ],
        scratch_shapes=[pltpu.VMEM((width, nodes), F32), pltpu.VMEM((got.shape[0] * more, nodes), F32)],
        compiler_params=params(),
        cost_estimate=pl.CostEstimate(flops=2 * nodes * width * width, bytes_accessed=2 * width * width, transcendentals=0),
        name="finish",
    )(got, w_out)


def flip_kernel(x_ref, out_ref):
    out_ref[...] = x_ref[...].T


def flip(x):
    rows, cols = x.shape
    return pl.pallas_call(
        flip_kernel,
        out_shape=jax.ShapeDtypeStruct((cols, rows), x.dtype),
        compiler_params=params(),
        cost_estimate=pl.CostEstimate(flops=0, bytes_accessed=4 * rows * cols, transcendentals=0),
        name="flip",
    )(x)


def body(queries, keys, values, cotangent, w_out, blocks, counts):
    nseq = lax.axis_size("seq")
    ndp = lax.axis_size("dp")
    width = w_out.shape[0]
    me = lax.axis_index("dp").astype(jnp.int32)[None]
    site = (lax.axis_index("seq") % SITE).astype(jnp.int32)[None]
    same_site = [[SITE * h + s for h in range(H)] for s in range(SITE)]
    same_core = [list(range(c, nseq, 2)) for c in range(2)]
    same_site_dp = [[p * nseq + i for p in range(ndp) for i in group] for group in same_site]

    def swap(x, bit):
        return lax.ppermute(x, "seq", [(i, i ^ bit) for i in range(nseq)])

    blk = blocks[0].reshape(-1)
    cnt = counts[0]
    cot = cotangent[0]

    sent = pack(queries[0], keys[0], values[0], cot, w_out)
    sent, cot = lax.optimization_barrier((sent, cot))
    cots = [cot]
    if ndp > 1:
        cot = jnp.concatenate([cot, lax.ppermute(cot, "dp", [(i, i ^ 1) for i in range(ndp)])], axis=0)
        cots = [cot] + [lax.ppermute(cot, "dp", [(i, i ^ t) for i in range(ndp)]) for t in range(2, ndp, 2)]
    recv = lax.all_to_all(sent, "seq", split_axis=0, concat_axis=0, tiled=True, axis_index_groups=same_site)
    kv, cots = lax.optimization_barrier((recv[:, :128], cots))
    kv_z = swap(kv, 2)
    kvs = [kv, swap(kv, 1), kv_z, swap(kv_z, 1)]
    att, probs = forward(site, blk, cnt, recv, kvs, ndp)
    sent_att = att.reshape(ndp * H, HD // ndp, CSIZE)
    pieces = lax.all_to_all(
        sent_att, ("dp", "seq"), split_axis=0, concat_axis=0, tiled=True, axis_index_groups=same_site_dp
    ).reshape(ndp, width // ndp, CSIZE)
    keep, give = backward(site, blk, recv, probs)
    chip = (keep.astype(F32) + swap(give, 1).astype(F32)).astype(BF)
    pieces, _ = lax.optimization_barrier((pieces, chip))
    part, more = weight_part(me, site, pieces, cots, nseq)
    last = merge(chip[0], swap(chip[1], 2), part, swap(more, 1))
    back = lax.all_to_all(last, "seq", split_axis=0, concat_axis=0, tiled=True, axis_index_groups=same_core)
    got = lax.all_to_all(gather_send(back, pieces), "dp", split_axis=0, concat_axis=0, tiled=True)
    value_grad = flip(back[:, :HALF].reshape(width, CSIZE))
    layer_out, weight_grad = finish(got, w_out, width // nseq)
    return (layer_out[None], value_grad[None], weight_grad)


def solution(mesh):
    return jax.shard_map(
        body,
        mesh=mesh,
        in_specs=(
            P("dp", "seq", None),
            P("dp", "seq", None),
            P("dp", "seq", None),
            P("dp", "seq", None),
            P(),
            P("dp", None, None),
            P("dp", None),
        ),
        out_specs=(P("dp", "seq", None), P("dp", "seq", None), P("seq", None)),
        check_vma=False,
    )
```

```python
import math

import jax
import jax.numpy as jnp
from jax import lax
from jax.experimental import pallas as pl
from jax.experimental.pallas import tpu as pltpu
from jax.sharding import PartitionSpec as P

H = 16
HD = 64
CSIZE = 128
HALF = HD // 2
MAXB = 4
SITE = 4
ROWS = 8
PAIR = 8
BROWS = 8
BF = jnp.bfloat16
F32 = jnp.float32


def params(mib=40):
    return pltpu.CompilerParams(vmem_limit_bytes=mib * 1024 * 1024)


def pack_kernel(q_ref, k_ref, v_ref, c_ref, w_ref, out_ref, ct_ref):
    @pl.when(pl.program_id(0) == 0)
    def _():
        ct_ref[...] = c_ref[...].T

    keys = k_ref[...]
    vals = v_ref[...].T
    qrys = q_ref[...].T
    grad = jnp.dot(w_ref[...], ct_ref[...], preferred_element_type=F32).astype(BF)
    for i in range(PAIR):
        part = keys[:, i * HD : (i + 1) * HD]
        out_ref[i, 0:64, :] = jnp.concatenate([part[:64], part[64:]], axis=1)
        out_ref[i, 64:128, :] = vals[i * HD : (i + 1) * HD]
        out_ref[i, 128:192, :] = qrys[i * HD : (i + 1) * HD]
        out_ref[i, 192:256, :] = grad[i * HD : (i + 1) * HD]


def pack(q, k, v, cot, w_out):
    rows, width = q.shape
    pair = pl.BlockSpec((rows, PAIR * HD), lambda i: (0, i))
    return pl.pallas_call(
        pack_kernel,
        grid=(H // PAIR,),
        in_specs=[
            pair,
            pair,
            pair,
            pl.BlockSpec((rows, width), lambda i: (0, 0)),
            pl.BlockSpec((PAIR * HD, width), lambda i: (i, 0)),
        ],
        out_specs=pl.BlockSpec((PAIR, 256, CSIZE), lambda i: (i, 0, 0)),
        scratch_shapes=[pltpu.VMEM((width, rows), BF)],
        out_shape=jax.ShapeDtypeStruct((H, 256, CSIZE), BF),
        compiler_params=params(60),
        cost_estimate=pl.CostEstimate(
            flops=2 * rows * width * width, bytes_accessed=2 * width * width + 10 * rows * width, transcendentals=0
        ),
        name="pack",
    )(q, k, v, cot, w_out)


def forward_kernel(site_ref, blk_ref, cnt_ref, q_ref, *refs):
    parts, (att_ref, prob_ref, kv_ref, wide_ref, sems) = refs[:-5], refs[-5:]
    each = parts[0].shape[0]
    pieces = len(parts) // SITE

    @pl.when(pl.program_id(0) == 0)
    def _():
        copies = [
            pltpu.make_async_copy(part, kv_ref.at[t // pieces, pl.ds(t % pieces * each, each)], sems.at[t])
            for t, part in enumerate(parts)
        ]
        for copy in copies:
            copy.start()
        for copy in copies:
            copy.wait()

    count = q_ref.shape[0]
    ids, slots, scores = [], [], []
    for u in range(count):
        cluster = SITE * (count * pl.program_id(0) + u) + site_ref[0]
        number = cnt_ref[cluster]
        q = q_ref[u]
        zero = jnp.zeros_like(q)
        both = jnp.concatenate(
            [jnp.concatenate([q, zero], axis=1), jnp.concatenate([zero, q], axis=1)], axis=0
        )
        at = [blk_ref[MAXB * cluster + j] for j in range(MAXB)]
        ids.append([i // SITE for i in at])
        slots.append([(i % SITE) ^ site_ref[0] for i in at])
        mine = []
        for j in range(MAXB):
            keys = kv_ref[slots[u][j], ids[u][j], 0:64, :]
            s = jnp.dot(keys, both, preferred_element_type=F32)
            mine.append(s if j == 0 else jnp.where(j < number, s, -1e30))
        scores.append(jnp.concatenate(mine, axis=0))
    for u in range(count):
        s = scores[u]
        top = jnp.max(s, axis=0, keepdims=True)
        top = jnp.maximum(top[:, :CSIZE], top[:, CSIZE:])
        e = jnp.exp2((s - jnp.concatenate([top, top], axis=1)) * (HD**-0.5 * math.log2(math.e)))
        total = jnp.sum(e, axis=0, keepdims=True)
        inv = 1.0 / (total[:, :CSIZE] + total[:, CSIZE:])
        p = (e * jnp.concatenate([inv, inv], axis=1)).astype(BF)
        halves = [p[i * 64 : (i + 1) * 64, h : h + CSIZE] for i in range(MAXB) for h in (0, CSIZE)]
        for j in range(MAXB):
            prob_ref[u, j] = jnp.concatenate(halves[2 * j : 2 * j + 2], axis=0)
        vals = jnp.concatenate([kv_ref[slots[u][j], ids[u][j], 64:128, :] for j in range(MAXB)], axis=1)
        att = jnp.dot(vals, jnp.concatenate(halves, axis=0), preferred_element_type=F32)
        wide_ref[u * HD : (u + 1) * HD, :] = att
    split = att_ref.shape[0]
    for p in range(split):
        att_ref[p] = wide_ref[pl.ds(p, att_ref.shape[1], stride=split), :].astype(BF)


def forward(site, blk, cnt, recv, kvs, split):
    parts = [part for member in kvs for part in member]
    n = recv.shape[0]
    return pl.pallas_call(
        forward_kernel,
        grid_spec=pltpu.PrefetchScalarGridSpec(
            num_scalar_prefetch=3,
            grid=(n // ROWS,),
            in_specs=[
                pl.BlockSpec((ROWS, 64, CSIZE), lambda i, *_: (i, 2, 0)),
            ]
            + [pl.BlockSpec(memory_space=pl.ANY)] * len(parts),
            out_specs=[
                pl.BlockSpec((split, ROWS * HD // split, CSIZE), lambda i, *_: (0, i, 0)),
                pl.BlockSpec((ROWS, MAXB, CSIZE, CSIZE), lambda i, *_: (i, 0, 0, 0)),
            ],
            scratch_shapes=[
                pltpu.VMEM((SITE, n) + parts[0].shape[1:], BF),
                pltpu.VMEM((ROWS * HD, CSIZE), F32),
                pltpu.SemaphoreType.DMA((len(parts),)),
            ],
        ),
        out_shape=[
            pltpu.HBM((split, n * HD // split, CSIZE), BF),
            pltpu.HBM((n, MAXB, CSIZE, CSIZE), BF),
        ],
        compiler_params=params(24),
        cost_estimate=pl.CostEstimate(
            flops=n * 4 * MAXB * CSIZE * CSIZE * HD, bytes_accessed=5 << 20, transcendentals=n * MAXB * CSIZE * CSIZE
        ),
        name="attend",
    )(site, blk, cnt, recv, *parts)


def backward_kernel(site_ref, blk_ref, g_ref, prob_ref, keep_ref, swap_ref, acc_ref):
    step = pl.program_id(0)

    @pl.when(step == 0)
    def _():
        acc_ref[...] = jnp.zeros_like(acc_ref)

    count = g_ref.shape[0]
    for u in range(count):
        cluster = SITE * (count * step + u) + site_ref[0]
        terms = [
            lax.dot_general(g_ref[u], prob_ref[u, j], (((1,), (1,)), ((), ())), preferred_element_type=F32)
            for j in range(MAXB)
        ]
        for j in range(MAXB):
            acc_ref[blk_ref[MAXB * cluster + j]] += terms[j]

    @pl.when(step == pl.num_programs(0) - 1)
    def _():
        core = site_ref[0] % 2
        for t in range(2):
            rows = pl.ds(pl.multiple_of(HALF * ((site_ref[0] // 2) ^ t), HALF), HALF)
            for k in range(keep_ref.shape[1]):
                keep_ref[t, k] = acc_ref[2 * k + core, rows, :].astype(BF)
                swap_ref[t, k] = acc_ref[2 * k + 1 - core, rows, :].astype(BF)


def backward(site, blk, recv, probs):
    n = recv.shape[0]
    clusters = SITE * n
    return pl.pallas_call(
        backward_kernel,
        grid_spec=pltpu.PrefetchScalarGridSpec(
            num_scalar_prefetch=2,
            grid=(n // BROWS,),
            in_specs=[
                pl.BlockSpec((BROWS, 64, CSIZE), lambda i, *_: (i, 3, 0)),
                pl.BlockSpec((BROWS, MAXB, CSIZE, CSIZE), lambda i, *_: (i, 0, 0, 0)),
            ],
            out_specs=[pl.BlockSpec((2, clusters // 2, HALF, CSIZE), lambda i, *_: (0, 0, 0, 0))] * 2,
            scratch_shapes=[pltpu.VMEM((clusters, HD, CSIZE), F32)],
        ),
        out_shape=[jax.ShapeDtypeStruct((2, clusters // 2, HALF, CSIZE), BF)] * 2,
        compiler_params=params(24),
        cost_estimate=pl.CostEstimate(
            flops=n * 2 * MAXB * CSIZE * CSIZE * HD, bytes_accessed=3 << 20, transcendentals=0
        ),
        name="value_contrib",
    )(site, blk, recv, probs)


def merge_kernel(own_ref, other_ref, part_ref, more_ref, out_ref):
    value = own_ref[...].astype(F32) + other_ref[...].astype(F32)
    out_ref[...] = jnp.concatenate([value, part_ref[...] + more_ref[...]], axis=1).astype(BF)


def merge(own, other, part, more):
    n, rows, nodes = own.shape
    return pl.pallas_call(
        merge_kernel,
        out_shape=jax.ShapeDtypeStruct((n, rows + part.shape[1], nodes), BF),
        compiler_params=params(),
        cost_estimate=pl.CostEstimate(flops=own.size, bytes_accessed=6 * own.size + 10 * part.size, transcendentals=0),
        name="merge",
    )(own, other, part, more)


def weight_kernel(me_ref, site_ref, att_ref, *refs):
    cots, (keep_ref, swap_ref, acc_ref, wide_ref) = refs[:-4], refs[-4:]
    each = att_ref.shape[0] // len(cots)
    for t, cot_ref in enumerate(cots):
        att = jnp.concatenate([att_ref[me_ref[0] ^ (each * t + i)] for i in range(each)], axis=1)
        term = jnp.dot(att, cot_ref[...], preferred_element_type=F32)
        acc_ref[...] = term if t == 0 else acc_ref[...] + term
    for i in range(wide_ref.shape[1]):
        wide_ref[:, i, :] = acc_ref[:, CSIZE * i : CSIZE * (i + 1)]
    core = site_ref[0] % 2
    half, piece, _ = keep_ref.shape
    rows = wide_ref.shape[0] // half // 2
    for k in range(half):
        for to_ref, parity in ((keep_ref, core), (swap_ref, 1 - core)):
            to_ref[k] = wide_ref[pl.ds((2 * k + parity) * rows, rows)].reshape(piece, CSIZE)


def weight_part(me, site, att, cots, targets):
    n, rows, nodes = att.shape
    width = cots[0].shape[1]
    piece = (targets // 2, rows * width // CSIZE // targets, CSIZE)
    return pl.pallas_call(
        weight_kernel,
        in_specs=[pl.BlockSpec(memory_space=pltpu.SMEM)] * 2 + [pl.BlockSpec(memory_space=pltpu.VMEM)] * (1 + len(cots)),
        out_shape=[jax.ShapeDtypeStruct(piece, F32)] * 2,
        scratch_shapes=[pltpu.VMEM((rows, width), F32), pltpu.VMEM((rows, width // CSIZE, CSIZE), F32)],
        compiler_params=params(16),
        cost_estimate=pl.CostEstimate(
            flops=2 * n * rows * nodes * width, bytes_accessed=2 * n * nodes * width, transcendentals=0
        ),
        name="weight_part",
    )(me, site, att, *cots)


def gather_kernel(back_ref, att_ref, out_ref):
    n, rows, _ = att_ref.shape
    total = jnp.sum(back_ref[...].astype(F32), axis=0)[HALF:]
    high = total.astype(BF).astype(F32)
    both = jnp.concatenate([high, total - high], axis=0).astype(BF)
    for p in range(n):
        out_ref[p, :rows, :] = att_ref[p]
        out_ref[p, rows:, :] = both


def gather_send(back, att):
    n, rows, nodes = att.shape
    more = 2 * (back.shape[1] - HALF)
    return pl.pallas_call(
        gather_kernel,
        out_shape=jax.ShapeDtypeStruct((n, rows + more, nodes), BF),
        compiler_params=params(),
        cost_estimate=pl.CostEstimate(flops=back.size, bytes_accessed=2 * back.size + 4 * att.size, transcendentals=0),
        name="gather_send",
    )(back, att)


def finish_kernel(got_ref, w_ref, layer_ref, weight_ref, wide_ref, rows_ref):
    n, total, nodes = got_ref.shape
    rows = w_ref.shape[0] // n
    more = (total - rows) // 2
    for p in range(n):
        wide_ref[pl.ds(p, rows, stride=n), :] = got_ref[p, :rows, :].astype(F32)
        both = got_ref[p, rows:, :].astype(F32)
        rows_ref[p * more : (p + 1) * more, :] = both[:more] + both[more:]
    layer_ref[...] = jnp.dot(
        wide_ref[...].T.astype(BF), w_ref[...], preferred_element_type=F32
    ).astype(BF)
    pieces = weight_ref.shape[1] // nodes
    for i in range(pieces):
        weight_ref[:, i * nodes : (i + 1) * nodes] = rows_ref[pl.ds(i, weight_ref.shape[0], stride=pieces), :]


def finish(got, w_out, own):
    nodes = got.shape[2]
    width = w_out.shape[0]
    more = (got.shape[1] - width // got.shape[0]) // 2
    return pl.pallas_call(
        finish_kernel,
        out_shape=[
            jax.ShapeDtypeStruct((nodes, width), BF),
            jax.ShapeDtypeStruct((own, width), F32),
        ],
        scratch_shapes=[pltpu.VMEM((width, nodes), F32), pltpu.VMEM((got.shape[0] * more, nodes), F32)],
        compiler_params=params(),
        cost_estimate=pl.CostEstimate(flops=2 * nodes * width * width, bytes_accessed=2 * width * width, transcendentals=0),
        name="finish",
    )(got, w_out)


def flip_kernel(x_ref, out_ref):
    out_ref[...] = x_ref[...].T


def flip(x):
    rows, cols = x.shape
    return pl.pallas_call(
        flip_kernel,
        out_shape=jax.ShapeDtypeStruct((cols, rows), x.dtype),
        compiler_params=params(),
        cost_estimate=pl.CostEstimate(flops=0, bytes_accessed=4 * rows * cols, transcendentals=0),
        name="flip",
    )(x)


def body(queries, keys, values, cotangent, w_out, blocks, counts):
    nseq = lax.axis_size("seq")
    ndp = lax.axis_size("dp")
    width = w_out.shape[0]
    me = lax.axis_index("dp").astype(jnp.int32)[None]
    site = (lax.axis_index("seq") % SITE).astype(jnp.int32)[None]
    same_site = [[SITE * h + s for h in range(H)] for s in range(SITE)]
    same_core = [list(range(c, nseq, 2)) for c in range(2)]
    same_site_dp = [[p * nseq + i for p in range(ndp) for i in group] for group in same_site]

    def swap(x, bit):
        return lax.ppermute(x, "seq", [(i, i ^ bit) for i in range(nseq)])

    blk = blocks[0].reshape(-1)
    cnt = counts[0]
    cot = cotangent[0]

    sent = pack(queries[0], keys[0], values[0], cot, w_out)
    sent, cot = lax.optimization_barrier((sent, cot))
    cots = [cot]
    if ndp > 1:
        cot = jnp.concatenate([cot, lax.ppermute(cot, "dp", [(i, i ^ 1) for i in range(ndp)])], axis=0)
        cots = [cot] + [lax.ppermute(cot, "dp", [(i, i ^ t) for i in range(ndp)]) for t in range(2, ndp, 2)]
    recv = lax.all_to_all(sent, "seq", split_axis=0, concat_axis=0, tiled=True, axis_index_groups=same_site)
    half = H // 2
    kv, cots = lax.optimization_barrier(([recv[:half, :128], recv[half:, :128]], cots))
    kv_z = [swap(x, 2) for x in kv]
    kvs = [kv, [swap(x, 1) for x in kv], kv_z, [swap(x, 1) for x in kv_z]]
    att, probs = forward(site, blk, cnt, recv, kvs, ndp)
    sent_att = att.reshape(ndp * H, HD // ndp, CSIZE)
    pieces = lax.all_to_all(
        sent_att, ("dp", "seq"), split_axis=0, concat_axis=0, tiled=True, axis_index_groups=same_site_dp
    ).reshape(ndp, width // ndp, CSIZE)
    keep, give = backward(site, blk, recv, probs)
    chip = (keep.astype(F32) + swap(give, 1).astype(F32)).astype(BF)
    pieces, _ = lax.optimization_barrier((pieces, chip))
    part, more = weight_part(me, site, pieces, cots, nseq)
    last = merge(chip[0], swap(chip[1], 2), part, swap(more, 1))
    back = lax.all_to_all(last, "seq", split_axis=0, concat_axis=0, tiled=True, axis_index_groups=same_core)
    got = lax.all_to_all(gather_send(back, pieces), "dp", split_axis=0, concat_axis=0, tiled=True)
    value_grad = flip(back[:, :HALF].reshape(width, CSIZE))
    layer_out, weight_grad = finish(got, w_out, width // nseq)
    return (layer_out[None], value_grad[None], weight_grad)


def solution(mesh):
    return jax.shard_map(
        body,
        mesh=mesh,
        in_specs=(
            P("dp", "seq", None),
            P("dp", "seq", None),
            P("dp", "seq", None),
            P("dp", "seq", None),
            P(),
            P("dp", None, None),
            P("dp", None),
        ),
        out_specs=(P("dp", "seq", None), P("dp", "seq", None), P("seq", None)),
        check_vma=False,
    )
```

```python
import math

import jax
import jax.numpy as jnp
from jax import lax
from jax.experimental import pallas as pl
from jax.experimental.pallas import tpu as pltpu
from jax.sharding import PartitionSpec as P

H = 16
HD = 64
CSIZE = 128
HALF = HD // 2
MAXB = 4
SITE = 4
ROWS = 8
PAIR = 8
BROWS = 8
BF = jnp.bfloat16
F32 = jnp.float32


def params(mib=40):
    return pltpu.CompilerParams(vmem_limit_bytes=mib * 1024 * 1024)


def pack_kernel(q_ref, k_ref, v_ref, c_ref, w_ref, out_ref, ct_ref):
    @pl.when(pl.program_id(0) == 0)
    def _():
        ct_ref[...] = c_ref[...].T

    keys = k_ref[...]
    vals = v_ref[...].T
    qrys = q_ref[...].T
    grad = jnp.dot(w_ref[...], ct_ref[...], preferred_element_type=F32).astype(BF)
    for i in range(PAIR):
        part = keys[:, i * HD : (i + 1) * HD]
        out_ref[i, 0:64, :] = jnp.concatenate([part[:64], part[64:]], axis=1)
        out_ref[i, 64:128, :] = vals[i * HD : (i + 1) * HD]
        out_ref[i, 128:192, :] = qrys[i * HD : (i + 1) * HD]
        out_ref[i, 192:256, :] = grad[i * HD : (i + 1) * HD]


def pack(q, k, v, cot, w_out):
    rows, width = q.shape
    pair = pl.BlockSpec((rows, PAIR * HD), lambda i: (0, i))
    return pl.pallas_call(
        pack_kernel,
        grid=(H // PAIR,),
        in_specs=[
            pair,
            pair,
            pair,
            pl.BlockSpec((rows, width), lambda i: (0, 0)),
            pl.BlockSpec((PAIR * HD, width), lambda i: (i, 0)),
        ],
        out_specs=pl.BlockSpec((PAIR, 256, CSIZE), lambda i: (i, 0, 0)),
        scratch_shapes=[pltpu.VMEM((width, rows), BF)],
        out_shape=jax.ShapeDtypeStruct((H, 256, CSIZE), BF),
        compiler_params=params(60),
        cost_estimate=pl.CostEstimate(
            flops=2 * rows * width * width, bytes_accessed=2 * width * width + 10 * rows * width, transcendentals=0
        ),
        name="pack",
    )(q, k, v, cot, w_out)


def forward_kernel(site_ref, blk_ref, cnt_ref, q_ref, *refs):
    parts, (att_ref, prob_ref, kv_ref, wide_ref, sems) = refs[:-5], refs[-5:]

    @pl.when(pl.program_id(0) == 0)
    def _():
        copies = []
        row = 0
        for t, part in enumerate(parts):
            member, first = divmod(row, kv_ref.shape[1])
            to = kv_ref.at[member, pl.ds(first, part.shape[0])]
            copies.append(pltpu.make_async_copy(part, to, sems.at[t]))
            row += part.shape[0]
        for copy in copies:
            copy.start()
        for copy in copies:
            copy.wait()

    count = q_ref.shape[0]
    ids, slots, scores = [], [], []
    for u in range(count):
        cluster = SITE * (count * pl.program_id(0) + u) + site_ref[0]
        number = cnt_ref[cluster]
        q = q_ref[u]
        zero = jnp.zeros_like(q)
        both = jnp.concatenate(
            [jnp.concatenate([q, zero], axis=1), jnp.concatenate([zero, q], axis=1)], axis=0
        )
        at = [blk_ref[MAXB * cluster + j] for j in range(MAXB)]
        ids.append([i // SITE for i in at])
        slots.append([(i % SITE) ^ site_ref[0] for i in at])
        mine = []
        for j in range(MAXB):
            keys = kv_ref[slots[u][j], ids[u][j], 0:64, :]
            s = jnp.dot(keys, both, preferred_element_type=F32)
            mine.append(s if j == 0 else jnp.where(j < number, s, -1e30))
        scores.append(jnp.concatenate(mine, axis=0))
    for u in range(count):
        s = scores[u]
        top = jnp.max(s, axis=0, keepdims=True)
        top = jnp.maximum(top[:, :CSIZE], top[:, CSIZE:])
        e = jnp.exp2((s - jnp.concatenate([top, top], axis=1)) * (HD**-0.5 * math.log2(math.e)))
        total = jnp.sum(e, axis=0, keepdims=True)
        inv = 1.0 / (total[:, :CSIZE] + total[:, CSIZE:])
        p = (e * jnp.concatenate([inv, inv], axis=1)).astype(BF)
        halves = [p[i * 64 : (i + 1) * 64, h : h + CSIZE] for i in range(MAXB) for h in (0, CSIZE)]
        for j in range(MAXB):
            prob_ref[u, j] = jnp.concatenate(halves[2 * j : 2 * j + 2], axis=0)
        vals = jnp.concatenate([kv_ref[slots[u][j], ids[u][j], 64:128, :] for j in range(MAXB)], axis=1)
        att = jnp.dot(vals, jnp.concatenate(halves, axis=0), preferred_element_type=F32)
        wide_ref[u * HD : (u + 1) * HD, :] = att
    split = att_ref.shape[0]
    for p in range(split):
        att_ref[p] = wide_ref[pl.ds(p, att_ref.shape[1], stride=split), :].astype(BF)


def forward(site, blk, cnt, recv, kvs, split):
    parts = [part for member in kvs for part in member]
    n = recv.shape[0]
    return pl.pallas_call(
        forward_kernel,
        grid_spec=pltpu.PrefetchScalarGridSpec(
            num_scalar_prefetch=3,
            grid=(n // ROWS,),
            in_specs=[
                pl.BlockSpec((ROWS, 64, CSIZE), lambda i, *_: (i, 2, 0)),
            ]
            + [pl.BlockSpec(memory_space=pl.ANY)] * len(parts),
            out_specs=[
                pl.BlockSpec((split, ROWS * HD // split, CSIZE), lambda i, *_: (0, i, 0)),
                pl.BlockSpec((ROWS, MAXB, CSIZE, CSIZE), lambda i, *_: (i, 0, 0, 0)),
            ],
            scratch_shapes=[
                pltpu.VMEM((SITE, n) + parts[0].shape[1:], BF),
                pltpu.VMEM((ROWS * HD, CSIZE), F32),
                pltpu.SemaphoreType.DMA((len(parts),)),
            ],
        ),
        out_shape=[
            pltpu.HBM((split, n * HD // split, CSIZE), BF),
            pltpu.HBM((n, MAXB, CSIZE, CSIZE), BF),
        ],
        compiler_params=params(24),
        cost_estimate=pl.CostEstimate(
            flops=n * 4 * MAXB * CSIZE * CSIZE * HD, bytes_accessed=5 << 20, transcendentals=n * MAXB * CSIZE * CSIZE
        ),
        name="attend",
    )(site, blk, cnt, recv, *parts)


def backward_kernel(site_ref, blk_ref, g_ref, prob_ref, keep_ref, swap_ref, acc_ref):
    step = pl.program_id(0)

    @pl.when(step == 0)
    def _():
        acc_ref[...] = jnp.zeros_like(acc_ref)

    count = g_ref.shape[0]
    for u in range(count):
        cluster = SITE * (count * step + u) + site_ref[0]
        terms = [
            lax.dot_general(g_ref[u], prob_ref[u, j], (((1,), (1,)), ((), ())), preferred_element_type=F32)
            for j in range(MAXB)
        ]
        for j in range(MAXB):
            acc_ref[blk_ref[MAXB * cluster + j]] += terms[j]

    @pl.when(step == pl.num_programs(0) - 1)
    def _():
        core = site_ref[0] % 2
        for t in range(2):
            rows = pl.ds(pl.multiple_of(HALF * ((site_ref[0] // 2) ^ t), HALF), HALF)
            for k in range(keep_ref.shape[1]):
                keep_ref[t, k] = acc_ref[2 * k + core, rows, :].astype(BF)
                swap_ref[t, k] = acc_ref[2 * k + 1 - core, rows, :].astype(BF)


def backward(site, blk, recv, probs):
    n = recv.shape[0]
    clusters = SITE * n
    return pl.pallas_call(
        backward_kernel,
        grid_spec=pltpu.PrefetchScalarGridSpec(
            num_scalar_prefetch=2,
            grid=(n // BROWS,),
            in_specs=[
                pl.BlockSpec((BROWS, 64, CSIZE), lambda i, *_: (i, 3, 0)),
                pl.BlockSpec((BROWS, MAXB, CSIZE, CSIZE), lambda i, *_: (i, 0, 0, 0)),
            ],
            out_specs=[pl.BlockSpec((2, clusters // 2, HALF, CSIZE), lambda i, *_: (0, 0, 0, 0))] * 2,
            scratch_shapes=[pltpu.VMEM((clusters, HD, CSIZE), F32)],
        ),
        out_shape=[jax.ShapeDtypeStruct((2, clusters // 2, HALF, CSIZE), BF)] * 2,
        compiler_params=params(24),
        cost_estimate=pl.CostEstimate(
            flops=n * 2 * MAXB * CSIZE * CSIZE * HD, bytes_accessed=3 << 20, transcendentals=0
        ),
        name="value_contrib",
    )(site, blk, recv, probs)


def merge_kernel(own_ref, other_ref, part_ref, more_ref, out_ref):
    value = own_ref[...].astype(F32) + other_ref[...].astype(F32)
    out_ref[...] = jnp.concatenate([value, part_ref[...] + more_ref[...]], axis=1).astype(BF)


def merge(own, other, part, more):
    n, rows, nodes = own.shape
    return pl.pallas_call(
        merge_kernel,
        out_shape=jax.ShapeDtypeStruct((n, rows + part.shape[1], nodes), BF),
        compiler_params=params(),
        cost_estimate=pl.CostEstimate(flops=own.size, bytes_accessed=6 * own.size + 10 * part.size, transcendentals=0),
        name="merge",
    )(own, other, part, more)


def weight_kernel(me_ref, site_ref, att_ref, *refs):
    cots, (keep_ref, swap_ref, acc_ref, wide_ref) = refs[:-4], refs[-4:]
    each = att_ref.shape[0] // len(cots)
    for t, cot_ref in enumerate(cots):
        att = jnp.concatenate([att_ref[me_ref[0] ^ (each * t + i)] for i in range(each)], axis=1)
        term = jnp.dot(att, cot_ref[...], preferred_element_type=F32)
        acc_ref[...] = term if t == 0 else acc_ref[...] + term
    for i in range(wide_ref.shape[1]):
        wide_ref[:, i, :] = acc_ref[:, CSIZE * i : CSIZE * (i + 1)]
    core = site_ref[0] % 2
    half, piece, _ = keep_ref.shape
    rows = wide_ref.shape[0] // half // 2
    for k in range(half):
        for to_ref, parity in ((keep_ref, core), (swap_ref, 1 - core)):
            to_ref[k] = wide_ref[pl.ds((2 * k + parity) * rows, rows)].reshape(piece, CSIZE)


def weight_part(me, site, att, cots, targets):
    n, rows, nodes = att.shape
    width = cots[0].shape[1]
    piece = (targets // 2, rows * width // CSIZE // targets, CSIZE)
    return pl.pallas_call(
        weight_kernel,
        in_specs=[pl.BlockSpec(memory_space=pltpu.SMEM)] * 2 + [pl.BlockSpec(memory_space=pltpu.VMEM)] * (1 + len(cots)),
        out_shape=[jax.ShapeDtypeStruct(piece, F32)] * 2,
        scratch_shapes=[pltpu.VMEM((rows, width), F32), pltpu.VMEM((rows, width // CSIZE, CSIZE), F32)],
        compiler_params=params(16),
        cost_estimate=pl.CostEstimate(
            flops=2 * n * rows * nodes * width, bytes_accessed=2 * n * nodes * width, transcendentals=0
        ),
        name="weight_part",
    )(me, site, att, *cots)


def gather_kernel(back_ref, att_ref, out_ref):
    n, rows, _ = att_ref.shape
    total = jnp.sum(back_ref[...].astype(F32), axis=0)[HALF:]
    high = total.astype(BF).astype(F32)
    both = jnp.concatenate([high, total - high], axis=0).astype(BF)
    for p in range(n):
        out_ref[p, :rows, :] = att_ref[p]
        out_ref[p, rows:, :] = both


def gather_send(back, att):
    n, rows, nodes = att.shape
    more = 2 * (back.shape[1] - HALF)
    return pl.pallas_call(
        gather_kernel,
        out_shape=jax.ShapeDtypeStruct((n, rows + more, nodes), BF),
        compiler_params=params(),
        cost_estimate=pl.CostEstimate(flops=back.size, bytes_accessed=2 * back.size + 4 * att.size, transcendentals=0),
        name="gather_send",
    )(back, att)


def finish_kernel(got_ref, w_ref, layer_ref, weight_ref, wide_ref, rows_ref):
    n, total, nodes = got_ref.shape
    rows = w_ref.shape[0] // n
    more = (total - rows) // 2
    for p in range(n):
        wide_ref[pl.ds(p, rows, stride=n), :] = got_ref[p, :rows, :].astype(F32)
        both = got_ref[p, rows:, :].astype(F32)
        rows_ref[p * more : (p + 1) * more, :] = both[:more] + both[more:]
    layer_ref[...] = jnp.dot(
        wide_ref[...].T.astype(BF), w_ref[...], preferred_element_type=F32
    ).astype(BF)
    pieces = weight_ref.shape[1] // nodes
    for i in range(pieces):
        weight_ref[:, i * nodes : (i + 1) * nodes] = rows_ref[pl.ds(i, weight_ref.shape[0], stride=pieces), :]


def finish(got, w_out, own):
    nodes = got.shape[2]
    width = w_out.shape[0]
    more = (got.shape[1] - width // got.shape[0]) // 2
    return pl.pallas_call(
        finish_kernel,
        out_shape=[
            jax.ShapeDtypeStruct((nodes, width), BF),
            jax.ShapeDtypeStruct((own, width), F32),
        ],
        scratch_shapes=[pltpu.VMEM((width, nodes), F32), pltpu.VMEM((got.shape[0] * more, nodes), F32)],
        compiler_params=params(),
        cost_estimate=pl.CostEstimate(flops=2 * nodes * width * width, bytes_accessed=2 * width * width, transcendentals=0),
        name="finish",
    )(got, w_out)


def flip_kernel(x_ref, out_ref):
    out_ref[...] = x_ref[...].T


def flip(x):
    rows, cols = x.shape
    return pl.pallas_call(
        flip_kernel,
        out_shape=jax.ShapeDtypeStruct((cols, rows), x.dtype),
        compiler_params=params(),
        cost_estimate=pl.CostEstimate(flops=0, bytes_accessed=4 * rows * cols, transcendentals=0),
        name="flip",
    )(x)


def body(queries, keys, values, cotangent, w_out, blocks, counts):
    nseq = lax.axis_size("seq")
    ndp = lax.axis_size("dp")
    width = w_out.shape[0]
    me = lax.axis_index("dp").astype(jnp.int32)[None]
    site = (lax.axis_index("seq") % SITE).astype(jnp.int32)[None]
    same_site = [[SITE * h + s for h in range(H)] for s in range(SITE)]
    same_core = [list(range(c, nseq, 2)) for c in range(2)]
    same_site_dp = [[p * nseq + i for p in range(ndp) for i in group] for group in same_site]

    def swap(x, bit):
        return lax.ppermute(x, "seq", [(i, i ^ bit) for i in range(nseq)])

    blk = blocks[0].reshape(-1)
    cnt = counts[0]
    cot = cotangent[0]

    sent = pack(queries[0], keys[0], values[0], cot, w_out)
    sent, cot = lax.optimization_barrier((sent, cot))
    cots = [cot]
    if ndp > 1:
        cot = jnp.concatenate([cot, lax.ppermute(cot, "dp", [(i, i ^ 1) for i in range(ndp)])], axis=0)
        cots = [cot] + [lax.ppermute(cot, "dp", [(i, i ^ t) for i in range(ndp)]) for t in range(2, ndp, 2)]
    recv = lax.all_to_all(sent, "seq", split_axis=0, concat_axis=0, tiled=True, axis_index_groups=same_site)
    half = H // 2
    kv, cots = lax.optimization_barrier((recv[:, :128], cots))
    kv_z = [swap(x, 2) for x in (kv[:half], kv[half:])]
    kvs = [[kv], [swap(kv, 1)], kv_z, [swap(x, 1) for x in kv_z]]
    att, probs = forward(site, blk, cnt, recv, kvs, ndp)
    sent_att = att.reshape(ndp * H, HD // ndp, CSIZE)
    pieces = lax.all_to_all(
        sent_att, ("dp", "seq"), split_axis=0, concat_axis=0, tiled=True, axis_index_groups=same_site_dp
    ).reshape(ndp, width // ndp, CSIZE)
    keep, give = backward(site, blk, recv, probs)
    chip = (keep.astype(F32) + swap(give, 1).astype(F32)).astype(BF)
    pieces, _ = lax.optimization_barrier((pieces, chip))
    part, more = weight_part(me, site, pieces, cots, nseq)
    last = merge(chip[0], swap(chip[1], 2), part, swap(more, 1))
    back = lax.all_to_all(last, "seq", split_axis=0, concat_axis=0, tiled=True, axis_index_groups=same_core)
    got = lax.all_to_all(gather_send(back, pieces), "dp", split_axis=0, concat_axis=0, tiled=True)
    value_grad = flip(back[:, :HALF].reshape(width, CSIZE))
    layer_out, weight_grad = finish(got, w_out, width // nseq)
    return (layer_out[None], value_grad[None], weight_grad)


def solution(mesh):
    return jax.shard_map(
        body,
        mesh=mesh,
        in_specs=(
            P("dp", "seq", None),
            P("dp", "seq", None),
            P("dp", "seq", None),
            P("dp", "seq", None),
            P(),
            P("dp", None, None),
            P("dp", None),
        ),
        out_specs=(P("dp", "seq", None), P("dp", "seq", None), P("seq", None)),
        check_vma=False,
    )
```

```python
import math

import jax
import jax.numpy as jnp
from jax import lax
from jax.experimental import pallas as pl
from jax.experimental.pallas import tpu as pltpu
from jax.sharding import PartitionSpec as P

H = 16
HD = 64
CSIZE = 128
HALF = HD // 2
MAXB = 4
SITE = 4
ROWS = 8
PAIR = 8
BROWS = 8
BF = jnp.bfloat16
F32 = jnp.float32


def params(mib=40):
    return pltpu.CompilerParams(vmem_limit_bytes=mib * 1024 * 1024)


def pack_kernel(q_ref, k_ref, v_ref, c_ref, w_ref, out_ref, ct_ref):
    @pl.when(pl.program_id(0) == 0)
    def _():
        ct_ref[...] = c_ref[...].T

    keys = k_ref[...]
    vals = v_ref[...].T
    qrys = q_ref[...].T
    grad = jnp.dot(w_ref[...], ct_ref[...], preferred_element_type=F32).astype(BF)
    for i in range(PAIR):
        part = keys[:, i * HD : (i + 1) * HD]
        out_ref[i, 0:64, :] = jnp.concatenate([part[:64], part[64:]], axis=1)
        out_ref[i, 64:128, :] = vals[i * HD : (i + 1) * HD]
        out_ref[i, 128:192, :] = qrys[i * HD : (i + 1) * HD]
        out_ref[i, 192:256, :] = grad[i * HD : (i + 1) * HD]


def pack(q, k, v, cot, w_out):
    rows, width = q.shape
    pair = pl.BlockSpec((rows, PAIR * HD), lambda i: (0, i))
    return pl.pallas_call(
        pack_kernel,
        grid=(H // PAIR,),
        in_specs=[
            pair,
            pair,
            pair,
            pl.BlockSpec((rows, width), lambda i: (0, 0)),
            pl.BlockSpec((PAIR * HD, width), lambda i: (i, 0)),
        ],
        out_specs=pl.BlockSpec((PAIR, 256, CSIZE), lambda i: (i, 0, 0)),
        scratch_shapes=[pltpu.VMEM((width, rows), BF)],
        out_shape=jax.ShapeDtypeStruct((H, 256, CSIZE), BF),
        compiler_params=params(60),
        cost_estimate=pl.CostEstimate(
            flops=2 * rows * width * width, bytes_accessed=2 * width * width + 10 * rows * width, transcendentals=0
        ),
        name="pack",
    )(q, k, v, cot, w_out)


def forward_kernel(site_ref, blk_ref, cnt_ref, q_ref, *refs):
    parts, (att_ref, prob_ref, kv_ref, wide_ref, sems) = refs[:-5], refs[-5:]

    def copies(kind):
        row, made = 0, []
        for t, part in enumerate(parts):
            member, first = divmod(row, kv_ref.shape[1])
            lines = pl.ds(kind * 64, 64)
            to = kv_ref.at[member, pl.ds(first, part.shape[0]), lines]
            made.append(pltpu.make_async_copy(part.at[:, lines], to, sems.at[kind, t]))
            row += part.shape[0]
        return made

    @pl.when(pl.program_id(0) == 0)
    def _():
        for copy in copies(0) + copies(1):
            copy.start()
        for copy in copies(0):
            copy.wait()

    count = q_ref.shape[0]
    ids, slots, scores = [], [], []
    for u in range(count):
        cluster = SITE * (count * pl.program_id(0) + u) + site_ref[0]
        number = cnt_ref[cluster]
        q = q_ref[u]
        zero = jnp.zeros_like(q)
        both = jnp.concatenate(
            [jnp.concatenate([q, zero], axis=1), jnp.concatenate([zero, q], axis=1)], axis=0
        )
        at = [blk_ref[MAXB * cluster + j] for j in range(MAXB)]
        ids.append([i // SITE for i in at])
        slots.append([(i % SITE) ^ site_ref[0] for i in at])
        mine = []
        for j in range(MAXB):
            keys = kv_ref[slots[u][j], ids[u][j], 0:64, :]
            s = jnp.dot(keys, both, preferred_element_type=F32)
            mine.append(s if j == 0 else jnp.where(j < number, s, -1e30))
        scores.append(jnp.concatenate(mine, axis=0))

    @pl.when(pl.program_id(0) == 0)
    def _():
        for copy in copies(1):
            copy.wait()

    for u in range(count):
        s = scores[u]
        top = jnp.max(s, axis=0, keepdims=True)
        top = jnp.maximum(top[:, :CSIZE], top[:, CSIZE:])
        e = jnp.exp2((s - jnp.concatenate([top, top], axis=1)) * (HD**-0.5 * math.log2(math.e)))
        total = jnp.sum(e, axis=0, keepdims=True)
        inv = 1.0 / (total[:, :CSIZE] + total[:, CSIZE:])
        p = (e * jnp.concatenate([inv, inv], axis=1)).astype(BF)
        halves = [p[i * 64 : (i + 1) * 64, h : h + CSIZE] for i in range(MAXB) for h in (0, CSIZE)]
        for j in range(MAXB):
            prob_ref[u, j] = jnp.concatenate(halves[2 * j : 2 * j + 2], axis=0)
        vals = jnp.concatenate([kv_ref[slots[u][j], ids[u][j], 64:128, :] for j in range(MAXB)], axis=1)
        att = jnp.dot(vals, jnp.concatenate(halves, axis=0), preferred_element_type=F32)
        wide_ref[u * HD : (u + 1) * HD, :] = att
    split = att_ref.shape[0]
    for p in range(split):
        att_ref[p] = wide_ref[pl.ds(p, att_ref.shape[1], stride=split), :].astype(BF)


def forward(site, blk, cnt, recv, kvs, split):
    parts = [part for member in kvs for part in member]
    n = recv.shape[0]
    return pl.pallas_call(
        forward_kernel,
        grid_spec=pltpu.PrefetchScalarGridSpec(
            num_scalar_prefetch=3,
            grid=(n // ROWS,),
            in_specs=[
                pl.BlockSpec((ROWS, 64, CSIZE), lambda i, *_: (i, 2, 0)),
            ]
            + [pl.BlockSpec(memory_space=pl.ANY)] * len(parts),
            out_specs=[
                pl.BlockSpec((split, ROWS * HD // split, CSIZE), lambda i, *_: (0, i, 0)),
                pl.BlockSpec((ROWS, MAXB, CSIZE, CSIZE), lambda i, *_: (i, 0, 0, 0)),
            ],
            scratch_shapes=[
                pltpu.VMEM((SITE, n) + parts[0].shape[1:], BF),
                pltpu.VMEM((ROWS * HD, CSIZE), F32),
                pltpu.SemaphoreType.DMA((2, len(parts))),
            ],
        ),
        out_shape=[
            pltpu.HBM((split, n * HD // split, CSIZE), BF),
            pltpu.HBM((n, MAXB, CSIZE, CSIZE), BF),
        ],
        compiler_params=params(24),
        cost_estimate=pl.CostEstimate(
            flops=n * 4 * MAXB * CSIZE * CSIZE * HD, bytes_accessed=5 << 20, transcendentals=n * MAXB * CSIZE * CSIZE
        ),
        name="attend",
    )(site, blk, cnt, recv, *parts)


def backward_kernel(site_ref, blk_ref, g_ref, prob_ref, keep_ref, swap_ref, acc_ref):
    step = pl.program_id(0)

    @pl.when(step == 0)
    def _():
        acc_ref[...] = jnp.zeros_like(acc_ref)

    count = g_ref.shape[0]
    for u in range(count):
        cluster = SITE * (count * step + u) + site_ref[0]
        terms = [
            lax.dot_general(g_ref[u], prob_ref[u, j], (((1,), (1,)), ((), ())), preferred_element_type=F32)
            for j in range(MAXB)
        ]
        for j in range(MAXB):
            acc_ref[blk_ref[MAXB * cluster + j]] += terms[j]

    @pl.when(step == pl.num_programs(0) - 1)
    def _():
        core = site_ref[0] % 2
        for t in range(2):
            rows = pl.ds(pl.multiple_of(HALF * ((site_ref[0] // 2) ^ t), HALF), HALF)
            for k in range(keep_ref.shape[1]):
                keep_ref[t, k] = acc_ref[2 * k + core, rows, :].astype(BF)
                swap_ref[t, k] = acc_ref[2 * k + 1 - core, rows, :].astype(BF)


def backward(site, blk, recv, probs):
    n = recv.shape[0]
    clusters = SITE * n
    return pl.pallas_call(
        backward_kernel,
        grid_spec=pltpu.PrefetchScalarGridSpec(
            num_scalar_prefetch=2,
            grid=(n // BROWS,),
            in_specs=[
                pl.BlockSpec((BROWS, 64, CSIZE), lambda i, *_: (i, 3, 0)),
                pl.BlockSpec((BROWS, MAXB, CSIZE, CSIZE), lambda i, *_: (i, 0, 0, 0)),
            ],
            out_specs=[pl.BlockSpec((2, clusters // 2, HALF, CSIZE), lambda i, *_: (0, 0, 0, 0))] * 2,
            scratch_shapes=[pltpu.VMEM((clusters, HD, CSIZE), F32)],
        ),
        out_shape=[jax.ShapeDtypeStruct((2, clusters // 2, HALF, CSIZE), BF)] * 2,
        compiler_params=params(24),
        cost_estimate=pl.CostEstimate(
            flops=n * 2 * MAXB * CSIZE * CSIZE * HD, bytes_accessed=3 << 20, transcendentals=0
        ),
        name="value_contrib",
    )(site, blk, recv, probs)


def merge_kernel(own_ref, other_ref, part_ref, more_ref, out_ref):
    value = own_ref[...].astype(F32) + other_ref[...].astype(F32)
    out_ref[...] = jnp.concatenate([value, part_ref[...] + more_ref[...]], axis=1).astype(BF)


def merge(own, other, part, more):
    n, rows, nodes = own.shape
    return pl.pallas_call(
        merge_kernel,
        out_shape=jax.ShapeDtypeStruct((n, rows + part.shape[1], nodes), BF),
        compiler_params=params(),
        cost_estimate=pl.CostEstimate(flops=own.size, bytes_accessed=6 * own.size + 10 * part.size, transcendentals=0),
        name="merge",
    )(own, other, part, more)


def weight_kernel(me_ref, site_ref, att_ref, *refs):
    cots, (keep_ref, swap_ref, acc_ref, wide_ref) = refs[:-4], refs[-4:]
    each = att_ref.shape[0] // len(cots)
    for t, cot_ref in enumerate(cots):
        att = jnp.concatenate([att_ref[me_ref[0] ^ (each * t + i)] for i in range(each)], axis=1)
        term = jnp.dot(att, cot_ref[...], preferred_element_type=F32)
        acc_ref[...] = term if t == 0 else acc_ref[...] + term
    for i in range(wide_ref.shape[1]):
        wide_ref[:, i, :] = acc_ref[:, CSIZE * i : CSIZE * (i + 1)]
    core = site_ref[0] % 2
    half, piece, _ = keep_ref.shape
    rows = wide_ref.shape[0] // half // 2
    for k in range(half):
        for to_ref, parity in ((keep_ref, core), (swap_ref, 1 - core)):
            to_ref[k] = wide_ref[pl.ds((2 * k + parity) * rows, rows)].reshape(piece, CSIZE)


def weight_part(me, site, att, cots, targets):
    n, rows, nodes = att.shape
    width = cots[0].shape[1]
    piece = (targets // 2, rows * width // CSIZE // targets, CSIZE)
    return pl.pallas_call(
        weight_kernel,
        in_specs=[pl.BlockSpec(memory_space=pltpu.SMEM)] * 2 + [pl.BlockSpec(memory_space=pltpu.VMEM)] * (1 + len(cots)),
        out_shape=[jax.ShapeDtypeStruct(piece, F32)] * 2,
        scratch_shapes=[pltpu.VMEM((rows, width), F32), pltpu.VMEM((rows, width // CSIZE, CSIZE), F32)],
        compiler_params=params(16),
        cost_estimate=pl.CostEstimate(
            flops=2 * n * rows * nodes * width, bytes_accessed=2 * n * nodes * width, transcendentals=0
        ),
        name="weight_part",
    )(me, site, att, *cots)


def gather_kernel(back_ref, att_ref, out_ref):
    n, rows, _ = att_ref.shape
    total = jnp.sum(back_ref[...].astype(F32), axis=0)[HALF:]
    high = total.astype(BF).astype(F32)
    both = jnp.concatenate([high, total - high], axis=0).astype(BF)
    for p in range(n):
        out_ref[p, :rows, :] = att_ref[p]
        out_ref[p, rows:, :] = both


def gather_send(back, att):
    n, rows, nodes = att.shape
    more = 2 * (back.shape[1] - HALF)
    return pl.pallas_call(
        gather_kernel,
        out_shape=jax.ShapeDtypeStruct((n, rows + more, nodes), BF),
        compiler_params=params(),
        cost_estimate=pl.CostEstimate(flops=back.size, bytes_accessed=2 * back.size + 4 * att.size, transcendentals=0),
        name="gather_send",
    )(back, att)


def finish_kernel(got_ref, w_ref, layer_ref, weight_ref, wide_ref, rows_ref):
    n, total, nodes = got_ref.shape
    rows = w_ref.shape[0] // n
    more = (total - rows) // 2
    for p in range(n):
        wide_ref[pl.ds(p, rows, stride=n), :] = got_ref[p, :rows, :].astype(F32)
        both = got_ref[p, rows:, :].astype(F32)
        rows_ref[p * more : (p + 1) * more, :] = both[:more] + both[more:]
    layer_ref[...] = jnp.dot(
        wide_ref[...].T.astype(BF), w_ref[...], preferred_element_type=F32
    ).astype(BF)
    pieces = weight_ref.shape[1] // nodes
    for i in range(pieces):
        weight_ref[:, i * nodes : (i + 1) * nodes] = rows_ref[pl.ds(i, weight_ref.shape[0], stride=pieces), :]


def finish(got, w_out, own):
    nodes = got.shape[2]
    width = w_out.shape[0]
    more = (got.shape[1] - width // got.shape[0]) // 2
    return pl.pallas_call(
        finish_kernel,
        out_shape=[
            jax.ShapeDtypeStruct((nodes, width), BF),
            jax.ShapeDtypeStruct((own, width), F32),
        ],
        scratch_shapes=[pltpu.VMEM((width, nodes), F32), pltpu.VMEM((got.shape[0] * more, nodes), F32)],
        compiler_params=params(),
        cost_estimate=pl.CostEstimate(flops=2 * nodes * width * width, bytes_accessed=2 * width * width, transcendentals=0),
        name="finish",
    )(got, w_out)


def flip_kernel(x_ref, out_ref):
    out_ref[...] = x_ref[...].T


def flip(x):
    rows, cols = x.shape
    return pl.pallas_call(
        flip_kernel,
        out_shape=jax.ShapeDtypeStruct((cols, rows), x.dtype),
        compiler_params=params(),
        cost_estimate=pl.CostEstimate(flops=0, bytes_accessed=4 * rows * cols, transcendentals=0),
        name="flip",
    )(x)


def body(queries, keys, values, cotangent, w_out, blocks, counts):
    nseq = lax.axis_size("seq")
    ndp = lax.axis_size("dp")
    width = w_out.shape[0]
    me = lax.axis_index("dp").astype(jnp.int32)[None]
    site = (lax.axis_index("seq") % SITE).astype(jnp.int32)[None]
    same_site = [[SITE * h + s for h in range(H)] for s in range(SITE)]
    same_core = [list(range(c, nseq, 2)) for c in range(2)]
    same_site_dp = [[p * nseq + i for p in range(ndp) for i in group] for group in same_site]

    def swap(x, bit):
        return lax.ppermute(x, "seq", [(i, i ^ bit) for i in range(nseq)])

    blk = blocks[0].reshape(-1)
    cnt = counts[0]
    cot = cotangent[0]

    sent = pack(queries[0], keys[0], values[0], cot, w_out)
    sent, cot = lax.optimization_barrier((sent, cot))
    cots = [cot]
    if ndp > 1:
        cot = jnp.concatenate([cot, lax.ppermute(cot, "dp", [(i, i ^ 1) for i in range(ndp)])], axis=0)
        cots = [cot] + [lax.ppermute(cot, "dp", [(i, i ^ t) for i in range(ndp)]) for t in range(2, ndp, 2)]
    recv = lax.all_to_all(sent, "seq", split_axis=0, concat_axis=0, tiled=True, axis_index_groups=same_site)
    most = 3 * H // 4
    kv, cots = lax.optimization_barrier((recv[:, :128], cots))
    kv_z = [swap(x, 2) for x in (kv[:most], kv[most:])]
    kvs = [[kv], [swap(kv, 1)], kv_z, [swap(x, 1) for x in kv_z]]
    att, probs = forward(site, blk, cnt, recv, kvs, ndp)
    sent_att = att.reshape(ndp * H, HD // ndp, CSIZE)
    pieces = lax.all_to_all(
        sent_att, ("dp", "seq"), split_axis=0, concat_axis=0, tiled=True, axis_index_groups=same_site_dp
    ).reshape(ndp, width // ndp, CSIZE)
    keep, give = backward(site, blk, recv, probs)
    chip = (keep.astype(F32) + swap(give, 1).astype(F32)).astype(BF)
    pieces, _ = lax.optimization_barrier((pieces, chip))
    part, more = weight_part(me, site, pieces, cots, nseq)
    last = merge(chip[0], swap(chip[1], 2), part, swap(more, 1))
    back = lax.all_to_all(last, "seq", split_axis=0, concat_axis=0, tiled=True, axis_index_groups=same_core)
    got = lax.all_to_all(gather_send(back, pieces), "dp", split_axis=0, concat_axis=0, tiled=True)
    value_grad = flip(back[:, :HALF].reshape(width, CSIZE))
    layer_out, weight_grad = finish(got, w_out, width // nseq)
    return (layer_out[None], value_grad[None], weight_grad)


def solution(mesh):
    return jax.shard_map(
        body,
        mesh=mesh,
        in_specs=(
            P("dp", "seq", None),
            P("dp", "seq", None),
            P("dp", "seq", None),
            P("dp", "seq", None),
            P(),
            P("dp", None, None),
            P("dp", None),
        ),
        out_specs=(P("dp", "seq", None), P("dp", "seq", None), P("seq", None)),
        check_vma=False,
    )
```

```python
import math

import jax
import jax.numpy as jnp
from jax import lax
from jax.experimental import pallas as pl
from jax.experimental.pallas import tpu as pltpu
from jax.sharding import PartitionSpec as P

H = 16
HD = 64
CSIZE = 128
HALF = HD // 2
MAXB = 4
SITE = 4
ROWS = 8
PAIR = 8
BROWS = 8
BF = jnp.bfloat16
F32 = jnp.float32


def params(mib=40):
    return pltpu.CompilerParams(vmem_limit_bytes=mib * 1024 * 1024)


def pack_kernel(q_ref, k_ref, v_ref, c_ref, w_ref, out_ref, ct_ref):
    @pl.when(pl.program_id(0) == 0)
    def _():
        ct_ref[...] = c_ref[...].T

    keys = k_ref[...]
    vals = v_ref[...].T
    qrys = q_ref[...].T
    grad = jnp.dot(w_ref[...], ct_ref[...], preferred_element_type=F32).astype(BF)
    for i in range(PAIR):
        part = keys[:, i * HD : (i + 1) * HD]
        out_ref[i, 0:64, :] = jnp.concatenate([part[:64], part[64:]], axis=1)
        out_ref[i, 64:128, :] = vals[i * HD : (i + 1) * HD]
        out_ref[i, 128:192, :] = qrys[i * HD : (i + 1) * HD]
        out_ref[i, 192:256, :] = grad[i * HD : (i + 1) * HD]


def pack(q, k, v, cot, w_out):
    rows, width = q.shape
    pair = pl.BlockSpec((rows, PAIR * HD), lambda i: (0, i))
    return pl.pallas_call(
        pack_kernel,
        grid=(H // PAIR,),
        in_specs=[
            pair,
            pair,
            pair,
            pl.BlockSpec((rows, width), lambda i: (0, 0)),
            pl.BlockSpec((PAIR * HD, width), lambda i: (i, 0)),
        ],
        out_specs=pl.BlockSpec((PAIR, 256, CSIZE), lambda i: (i, 0, 0)),
        scratch_shapes=[pltpu.VMEM((width, rows), BF)],
        out_shape=jax.ShapeDtypeStruct((H, 256, CSIZE), BF),
        compiler_params=params(60),
        cost_estimate=pl.CostEstimate(
            flops=2 * rows * width * width, bytes_accessed=2 * width * width + 10 * rows * width, transcendentals=0
        ),
        name="pack",
    )(q, k, v, cot, w_out)


def forward_kernel(site_ref, blk_ref, cnt_ref, q_ref, *refs):
    parts, (att_ref, prob_ref, kv_ref, wide_ref, sems) = refs[:-5], refs[-5:]
    each = parts[0].shape[0]
    pieces = len(parts) // SITE

    @pl.when(pl.program_id(0) == 0)
    def _():
        copies = [
            pltpu.make_async_copy(part, kv_ref.at[t // pieces, pl.ds(t % pieces * each, each)], sems.at[t])
            for t, part in enumerate(parts)
        ]
        for copy in copies:
            copy.start()
        for copy in copies:
            copy.wait()

    count = q_ref.shape[0]
    ids, slots, scores = [], [], []
    for u in range(count):
        cluster = SITE * (count * pl.program_id(0) + u) + site_ref[0]
        number = cnt_ref[cluster]
        q = q_ref[u]
        zero = jnp.zeros_like(q)
        both = jnp.concatenate(
            [jnp.concatenate([q, zero], axis=1), jnp.concatenate([zero, q], axis=1)], axis=0
        )
        at = [blk_ref[MAXB * cluster + j] for j in range(MAXB)]
        ids.append([i // SITE for i in at])
        slots.append([(i % SITE) ^ site_ref[0] for i in at])
        mine = []
        for j in range(MAXB):
            keys = kv_ref[slots[u][j], ids[u][j], 0:64, :]
            s = jnp.dot(keys, both, preferred_element_type=F32)
            mine.append(s if j == 0 else jnp.where(j < number, s, -1e30))
        scores.append(jnp.concatenate(mine, axis=0))
    for u in range(count):
        s = scores[u]
        top = jnp.max(s, axis=0, keepdims=True)
        top = jnp.maximum(top[:, :CSIZE], top[:, CSIZE:])
        e = jnp.exp2((s - jnp.concatenate([top, top], axis=1)) * (HD**-0.5 * math.log2(math.e)))
        total = jnp.sum(e, axis=0, keepdims=True)
        inv = 1.0 / (total[:, :CSIZE] + total[:, CSIZE:])
        p = (e * jnp.concatenate([inv, inv], axis=1)).astype(BF)
        halves = [p[i * 64 : (i + 1) * 64, h : h + CSIZE] for i in range(MAXB) for h in (0, CSIZE)]
        for j in range(MAXB):
            prob_ref[u, j] = jnp.concatenate(halves[2 * j : 2 * j + 2], axis=0)
        vals = jnp.concatenate([kv_ref[slots[u][j], ids[u][j], 64:128, :] for j in range(MAXB)], axis=1)
        att = jnp.dot(vals, jnp.concatenate(halves, axis=0), preferred_element_type=F32)
        wide_ref[u * HD : (u + 1) * HD, :] = att
    split = att_ref.shape[0]
    for p in range(split):
        att_ref[p] = wide_ref[pl.ds(p, att_ref.shape[1], stride=split), :].astype(BF)


def forward(site, blk, cnt, recv, kvs, split):
    parts = [part for member in kvs for part in member]
    n = recv.shape[0]
    return pl.pallas_call(
        forward_kernel,
        grid_spec=pltpu.PrefetchScalarGridSpec(
            num_scalar_prefetch=3,
            grid=(n // ROWS,),
            in_specs=[
                pl.BlockSpec((ROWS, 64, CSIZE), lambda i, *_: (i, 2, 0)),
            ]
            + [pl.BlockSpec(memory_space=pl.ANY)] * len(parts),
            out_specs=[
                pl.BlockSpec((split, ROWS * HD // split, CSIZE), lambda i, *_: (0, i, 0)),
                pl.BlockSpec((ROWS, MAXB, CSIZE, CSIZE), lambda i, *_: (i, 0, 0, 0)),
            ],
            scratch_shapes=[
                pltpu.VMEM((SITE, n) + parts[0].shape[1:], BF),
                pltpu.VMEM((ROWS * HD, CSIZE), F32),
                pltpu.SemaphoreType.DMA((len(parts),)),
            ],
        ),
        out_shape=[
            pltpu.HBM((split, n * HD // split, CSIZE), BF),
            pltpu.HBM((n, MAXB, CSIZE, CSIZE), BF),
        ],
        compiler_params=params(24),
        cost_estimate=pl.CostEstimate(
            flops=n * 4 * MAXB * CSIZE * CSIZE * HD, bytes_accessed=5 << 20, transcendentals=n * MAXB * CSIZE * CSIZE
        ),
        name="attend",
    )(site, blk, cnt, recv, *parts)


def backward_kernel(site_ref, blk_ref, g_ref, prob_ref, keep_ref, swap_ref, acc_ref):
    step = pl.program_id(0)

    @pl.when(step == 0)
    def _():
        acc_ref[...] = jnp.zeros_like(acc_ref)

    count = g_ref.shape[0]
    for u in range(count):
        cluster = SITE * (count * step + u) + site_ref[0]
        terms = [
            lax.dot_general(g_ref[u], prob_ref[u, j], (((1,), (1,)), ((), ())), preferred_element_type=F32)
            for j in range(MAXB)
        ]
        for j in range(MAXB):
            acc_ref[blk_ref[MAXB * cluster + j]] += terms[j]

    @pl.when(step == pl.num_programs(0) - 1)
    def _():
        core = site_ref[0] % 2
        for t in range(2):
            rows = pl.ds(pl.multiple_of(HALF * ((site_ref[0] // 2) ^ t), HALF), HALF)
            for k in range(keep_ref.shape[1]):
                keep_ref[t, k] = acc_ref[2 * k + core, rows, :].astype(BF)
                swap_ref[t, k] = acc_ref[2 * k + 1 - core, rows, :].astype(BF)


def backward(site, blk, recv, probs):
    n = recv.shape[0]
    clusters = SITE * n
    return pl.pallas_call(
        backward_kernel,
        grid_spec=pltpu.PrefetchScalarGridSpec(
            num_scalar_prefetch=2,
            grid=(n // BROWS,),
            in_specs=[
                pl.BlockSpec((BROWS, 64, CSIZE), lambda i, *_: (i, 3, 0)),
                pl.BlockSpec((BROWS, MAXB, CSIZE, CSIZE), lambda i, *_: (i, 0, 0, 0)),
            ],
            out_specs=[pl.BlockSpec((2, clusters // 2, HALF, CSIZE), lambda i, *_: (0, 0, 0, 0))] * 2,
            scratch_shapes=[pltpu.VMEM((clusters, HD, CSIZE), F32)],
        ),
        out_shape=[jax.ShapeDtypeStruct((2, clusters // 2, HALF, CSIZE), BF)] * 2,
        compiler_params=params(24),
        cost_estimate=pl.CostEstimate(
            flops=n * 2 * MAXB * CSIZE * CSIZE * HD, bytes_accessed=3 << 20, transcendentals=0
        ),
        name="value_contrib",
    )(site, blk, recv, probs)


def merge_kernel(own_ref, other_ref, part_ref, more_ref, out_ref):
    value = own_ref[...].astype(F32) + other_ref[...].astype(F32)
    out_ref[...] = jnp.concatenate([value, part_ref[...] + more_ref[...]], axis=1).astype(BF)


def merge(own, other, part, more):
    n, rows, nodes = own.shape
    return pl.pallas_call(
        merge_kernel,
        out_shape=jax.ShapeDtypeStruct((n, rows + part.shape[1], nodes), BF),
        compiler_params=params(),
        cost_estimate=pl.CostEstimate(flops=own.size, bytes_accessed=6 * own.size + 10 * part.size, transcendentals=0),
        name="merge",
    )(own, other, part, more)


def weight_kernel(me_ref, site_ref, att_ref, *refs):
    cots, (keep_ref, swap_ref, wide_ref) = refs[:-3], refs[-3:]
    each = att_ref.shape[0] // len(cots)
    atts = [
        jnp.concatenate([att_ref[me_ref[0] ^ (each * t + i)] for i in range(each)], axis=1)
        for t in range(len(cots))
    ]
    for i in range(0, wide_ref.shape[1], 2):
        block = slice(CSIZE * i, CSIZE * (i + 2))
        total = sum(jnp.dot(att, cot[:, block], preferred_element_type=F32) for att, cot in zip(atts, cots))
        wide_ref[:, i, :] = total[:, :CSIZE]
        wide_ref[:, i + 1, :] = total[:, CSIZE:]
    core = site_ref[0] % 2
    half, piece, _ = keep_ref.shape
    rows = wide_ref.shape[0] // half // 2
    for k in range(half):
        for to_ref, parity in ((keep_ref, core), (swap_ref, 1 - core)):
            to_ref[k] = wide_ref[pl.ds((2 * k + parity) * rows, rows)].reshape(piece, CSIZE)


def weight_part(me, site, att, cots, targets):
    n, rows, nodes = att.shape
    width = cots[0].shape[1]
    piece = (targets // 2, rows * width // CSIZE // targets, CSIZE)
    return pl.pallas_call(
        weight_kernel,
        in_specs=[pl.BlockSpec(memory_space=pltpu.SMEM)] * 2 + [pl.BlockSpec(memory_space=pltpu.VMEM)] * (1 + len(cots)),
        out_shape=[jax.ShapeDtypeStruct(piece, F32)] * 2,
        scratch_shapes=[pltpu.VMEM((rows, width // CSIZE, CSIZE), F32)],
        compiler_params=params(16),
        cost_estimate=pl.CostEstimate(
            flops=2 * n * rows * nodes * width, bytes_accessed=2 * n * nodes * width, transcendentals=0
        ),
        name="weight_part",
    )(me, site, att, *cots)


def gather_kernel(back_ref, att_ref, out_ref):
    n, rows, _ = att_ref.shape
    total = jnp.sum(back_ref[...].astype(F32), axis=0)[HALF:]
    high = total.astype(BF).astype(F32)
    both = jnp.concatenate([high, total - high], axis=0).astype(BF)
    for p in range(n):
        out_ref[p, :rows, :] = att_ref[p]
        out_ref[p, rows:, :] = both


def gather_send(back, att):
    n, rows, nodes = att.shape
    more = 2 * (back.shape[1] - HALF)
    return pl.pallas_call(
        gather_kernel,
        out_shape=jax.ShapeDtypeStruct((n, rows + more, nodes), BF),
        compiler_params=params(),
        cost_estimate=pl.CostEstimate(flops=back.size, bytes_accessed=2 * back.size + 4 * att.size, transcendentals=0),
        name="gather_send",
    )(back, att)


def finish_kernel(got_ref, w_ref, layer_ref, weight_ref, wide_ref, rows_ref):
    n, total, nodes = got_ref.shape
    rows = w_ref.shape[0] // n
    more = (total - rows) // 2
    for p in range(n):
        wide_ref[pl.ds(p, rows, stride=n), :] = got_ref[p, :rows, :].astype(F32)
        both = got_ref[p, rows:, :].astype(F32)
        rows_ref[p * more : (p + 1) * more, :] = both[:more] + both[more:]
    layer_ref[...] = jnp.dot(
        wide_ref[...].T.astype(BF), w_ref[...], preferred_element_type=F32
    ).astype(BF)
    pieces = weight_ref.shape[1] // nodes
    for i in range(pieces):
        weight_ref[:, i * nodes : (i + 1) * nodes] = rows_ref[pl.ds(i, weight_ref.shape[0], stride=pieces), :]


def finish(got, w_out, own):
    nodes = got.shape[2]
    width = w_out.shape[0]
    more = (got.shape[1] - width // got.shape[0]) // 2
    return pl.pallas_call(
        finish_kernel,
        out_shape=[
            jax.ShapeDtypeStruct((nodes, width), BF),
            jax.ShapeDtypeStruct((own, width), F32),
        ],
        scratch_shapes=[pltpu.VMEM((width, nodes), F32), pltpu.VMEM((got.shape[0] * more, nodes), F32)],
        compiler_params=params(),
        cost_estimate=pl.CostEstimate(flops=2 * nodes * width * width, bytes_accessed=2 * width * width, transcendentals=0),
        name="finish",
    )(got, w_out)


def flip_kernel(x_ref, out_ref):
    out_ref[...] = x_ref[...].T


def flip(x):
    rows, cols = x.shape
    return pl.pallas_call(
        flip_kernel,
        out_shape=jax.ShapeDtypeStruct((cols, rows), x.dtype),
        compiler_params=params(),
        cost_estimate=pl.CostEstimate(flops=0, bytes_accessed=4 * rows * cols, transcendentals=0),
        name="flip",
    )(x)


def body(queries, keys, values, cotangent, w_out, blocks, counts):
    nseq = lax.axis_size("seq")
    ndp = lax.axis_size("dp")
    width = w_out.shape[0]
    me = lax.axis_index("dp").astype(jnp.int32)[None]
    site = (lax.axis_index("seq") % SITE).astype(jnp.int32)[None]
    same_site = [[SITE * h + s for h in range(H)] for s in range(SITE)]
    same_core = [list(range(c, nseq, 2)) for c in range(2)]
    same_site_dp = [[p * nseq + i for p in range(ndp) for i in group] for group in same_site]

    def swap(x, bit):
        return lax.ppermute(x, "seq", [(i, i ^ bit) for i in range(nseq)])

    blk = blocks[0].reshape(-1)
    cnt = counts[0]
    cot = cotangent[0]

    sent = pack(queries[0], keys[0], values[0], cot, w_out)
    sent, cot = lax.optimization_barrier((sent, cot))
    cots = [cot]
    if ndp > 1:
        cot = jnp.concatenate([cot, lax.ppermute(cot, "dp", [(i, i ^ 1) for i in range(ndp)])], axis=0)
        cots = [cot] + [lax.ppermute(cot, "dp", [(i, i ^ t) for i in range(ndp)]) for t in range(2, ndp, 2)]
    recv = lax.all_to_all(sent, "seq", split_axis=0, concat_axis=0, tiled=True, axis_index_groups=same_site)
    half = H // 2
    kv, cots = lax.optimization_barrier(([recv[:half, :128], recv[half:, :128]], cots))
    kv_z = [swap(x, 2) for x in kv]
    kvs = [kv, [swap(x, 1) for x in kv], kv_z, [swap(x, 1) for x in kv_z]]
    att, probs = forward(site, blk, cnt, recv, kvs, ndp)
    sent_att = att.reshape(ndp * H, HD // ndp, CSIZE)
    pieces = lax.all_to_all(
        sent_att, ("dp", "seq"), split_axis=0, concat_axis=0, tiled=True, axis_index_groups=same_site_dp
    ).reshape(ndp, width // ndp, CSIZE)
    keep, give = backward(site, blk, recv, probs)
    chip = (keep.astype(F32) + swap(give, 1).astype(F32)).astype(BF)
    pieces, _ = lax.optimization_barrier((pieces, chip))
    part, more = weight_part(me, site, pieces, cots, nseq)
    last = merge(chip[0], swap(chip[1], 2), part, swap(more, 1))
    back = lax.all_to_all(last, "seq", split_axis=0, concat_axis=0, tiled=True, axis_index_groups=same_core)
    got = lax.all_to_all(gather_send(back, pieces), "dp", split_axis=0, concat_axis=0, tiled=True)
    value_grad = flip(back[:, :HALF].reshape(width, CSIZE))
    layer_out, weight_grad = finish(got, w_out, width // nseq)
    return (layer_out[None], value_grad[None], weight_grad)


def solution(mesh):
    return jax.shard_map(
        body,
        mesh=mesh,
        in_specs=(
            P("dp", "seq", None),
            P("dp", "seq", None),
            P("dp", "seq", None),
            P("dp", "seq", None),
            P(),
            P("dp", None, None),
            P("dp", None),
        ),
        out_specs=(P("dp", "seq", None), P("dp", "seq", None), P("seq", None)),
        check_vma=False,
    )
```
